32 devices in a mesh: mol: 8 (over z, x), row: 4 (over y, core).
Axes of the slice: x: 2, y: 2, z: 4, core: 2. Of those that a mesh axis runs over, the one named last changes fastest.
Arguments:
- edge_feats: bfloat16 [128, 384, 16], P('mol'), may hold values from -5 to 5
- edge_source: int32 [128, 384], P('mol'), may hold values from 0 to 31, as said below
- edge_target: int32 [128, 384], P('mol'), may hold values from 0 to 31, as said below
- atom_counts: int32 [128], P('mol'), may hold values from 16 to 32, as said below
- edge_counts: int32 [128], P('mol'), may hold values from 192 to 384, as said below
- atom_states: bfloat16 [128, 32, 128], P('mol'), may hold values from -3 to 3
- targets: float32 [128, 12], P('mol'), may hold values from -5 to 5
- label_mask: int32 [128, 12], P('mol'), may hold values from 0 to 1, as said below
- edge_input: float32 [16, 128], replicated, may hold values from -1.5 to 1.5
- edge_input_first: float32 [16, 128], replicated, may hold values from -0.00061035156 to 0.00061035156
- edge_input_second: float32 [16, 128], replicated, may hold values from 7.8125e-10 to 3.125e-09
- edge_output: float32 [128, 16384], P(None, 'row'), may hold values from -0.015625 to 0.015625
- edge_output_first: float32 [128, 16384], P(None, 'row'), may hold values from -6.1035156e-05 to 6.1035156e-05
- edge_output_second: float32 [128, 16384], P(None, 'row'), may hold values from 7.8125e-12 to 3.125e-11
- gated_weights: float32 [2, 128, 384], replicated, may hold values from -0.5 to 0.5
- gated_first: float32 [2, 128, 384], replicated, may hold values from -0.00030517578 to 0.00030517578
- gated_second: float32 [2, 128, 384], replicated, may hold values from 1.953125e-10 to 7.8125e-10
- memory_weights: float32 [384, 512], replicated, may hold values from -0.3125 to 0.3125
- memory_first: float32 [384, 512], replicated, may hold values from -0.00018310547 to 0.00018310547
- memory_second: float32 [384, 512], replicated, may hold values from 7.03125e-11 to 2.8125e-10
- readout_hidden: float32 [256, 128], replicated, may hold values from -0.375 to 0.375
- readout_hidden_first: float32 [256, 128], replicated, may hold values from -0.00061035156 to 0.00061035156
- readout_hidden_second: float32 [256, 128], replicated, may hold values from 7.8125e-10 to 3.125e-09
- readout_final: float32 [128, 12], replicated, may hold values from -0.5 to 0.5
- readout_final_first: float32 [128, 12], replicated, may hold values from -0.0048828125 to 0.0048828125
- readout_final_second: float32 [128, 12], replicated, may hold values from 5e-08 to 2e-07
- bias_vector: float32 [1548], replicated, may hold values from -1 to 1
- bias_first: float32 [1548], replicated, may hold values from -0.0029296875 to 0.0029296875
- bias_second: float32 [1548], replicated, may hold values from 1.953125e-08 to 7.8125e-08
Outputs:
- loss_sum: float32 [], replicated
- label_count: float32 [], replicated
- edge_input_new: float32 [16, 128], replicated
- edge_input_first_new: float32 [16, 128], replicated
- edge_input_second_new: float32 [16, 128], replicated
- edge_input_copy: bfloat16 [16, 128], replicated
- edge_output_new: float32 [128, 16384], P(None, 'row')
- edge_output_first_new: float32 [128, 16384], P(None, 'row')
- edge_output_second_new: float32 [128, 16384], P(None, 'row')
- edge_output_copy: bfloat16 [128, 16384], P(None, 'row')
- gated_new: float32 [2, 128, 384], replicated
- gated_first_new: float32 [2, 128, 384], replicated
- gated_second_new: float32 [2, 128, 384], replicated
- gated_copy: bfloat16 [2, 128, 384], replicated
- memory_new: float32 [384, 512], replicated
- memory_first_new: float32 [384, 512], replicated
- memory_second_new: float32 [384, 512], replicated
- memory_copy: bfloat16 [384, 512], replicated
- readout_hidden_new: float32 [256, 128], replicated
- readout_hidden_first_new: float32 [256, 128], replicated
- readout_hidden_second_new: float32 [256, 128], replicated
- readout_hidden_copy: bfloat16 [256, 128], replicated
- readout_final_new: float32 [128, 12], replicated
- readout_final_first_new: float32 [128, 12], replicated
- readout_final_second_new: float32 [128, 12], replicated
- readout_final_copy: bfloat16 [128, 12], replicated
- bias_new: float32 [1548], replicated
- bias_first_new: float32 [1548], replicated
- bias_second_new: float32 [1548], replicated
- bias_copy: bfloat16 [1548], replicated
The draws below stay inside these ranges and needn't reach their ends.
Inputs may be any that keep to these rules, and one draw needn't show every extreme that they name: Each molecule's edge_source and edge_target entries lie below its atom count and differ; slots at or past its edge count are not edges. `edge_target`: as for edge_source. `atom_counts`: some molecule has 32 atoms. `edge_counts`: some molecule has 384 edges. `label_mask`: at least one label is present.
All inputs are finite; a program needn't handle non-finite values.
Results may differ from the reference program's by a relative error of at most 0.012.
Values may be sent and summed in bfloat16 or wider, within the bound.
A program may use at most 128 MiB of HBM per device.

```python
import math
import jax
import jax.numpy as jnp
from jax import lax

H = 128
E1 = 128
F = 16
TARGETS = 12
A_PAD = 32
E_PAD = 384
LAYERS = 2
ROUNDS = 6
STEP = 10
MOLS = 128
NBIAS = 1548


def molecule_sizes(key):
    order = jnp.arange(MOLS)
    atoms = jax.random.randint(jax.random.fold_in(key, 11), (MOLS,), A_PAD // 2, A_PAD + 1)
    fullest = jax.random.randint(jax.random.fold_in(key, 12), (), 0, MOLS)
    atoms = jnp.where(order == fullest, A_PAD, atoms)
    edges = jax.random.randint(jax.random.fold_in(key, 13), (MOLS,), E_PAD // 2, E_PAD + 1)
    busiest = jax.random.randint(jax.random.fold_in(key, 14), (), 0, MOLS)
    edges = jnp.where(order == busiest, E_PAD, edges)
    return (atoms.astype(jnp.int32), edges.astype(jnp.int32))


def edge_pairs(key):
    atoms = molecule_sizes(key)[0]
    source = jax.random.randint(jax.random.fold_in(key, 15), (MOLS, E_PAD), 0, atoms[:, None])
    offset = jax.random.randint(jax.random.fold_in(key, 16), (MOLS, E_PAD), 1, atoms[:, None])
    target = (source + offset) % atoms[:, None]
    return (source.astype(jnp.int32), target.astype(jnp.int32))


def draw_edge_source(key, part):
    return edge_pairs(key)[0]


def draw_edge_target(key, part):
    return edge_pairs(key)[1]


def draw_atom_counts(key, part):
    return molecule_sizes(key)[0]


def draw_edge_counts(key, part):
    return molecule_sizes(key)[1]


def draw_label_mask(key, part):
    key = jax.random.fold_in(key, 5)
    rows = jnp.arange(MOLS)[:, None]
    columns = jnp.arange(TARGETS)[None, :]
    limit = 250 + 600 * rows // max(MOLS - 1, 1)
    rolls = jax.random.randint(key, (MOLS, TARGETS), 0, 1000)
    chosen = jax.random.randint(jax.random.fold_in(key, 6), (), 0, MOLS)
    mask = (rolls < limit) | (rows == chosen) & (columns == 0)
    return mask.astype(jnp.int32)


def block_scale(key, shape, shards, least, top_value):
    factor_of, own = 1.0, jax.random.fold_in(key, 6)
    for dim, parts in shards:
        steps = jnp.exp(jax.random.uniform(jax.random.fold_in(own, dim), (parts,), jnp.float32, least / len(shards), top_value / len(shards)))
        factor_of = factor_of * jnp.repeat(steps, shape[dim] // parts).reshape([-1 if axis == dim else 1 for axis in range(len(shape))])
    return factor_of


def centred(key, dims, deviation, bound, split=(), kind=jnp.bfloat16):
    factor_of = block_scale(key, dims, split, -0.22, 0.18) if split else 1.0
    result = jax.random.normal(key, dims, jnp.float32) * deviation * factor_of
    return jnp.minimum(jnp.maximum(result, -bound), bound).astype(kind)


def setup_inputs(seed: int = 0) -> dict:
    splits = jax.random.split(jax.random.key(seed), 30)
    edge_feats = centred(splits[0], (MOLS, E_PAD, F), 1.0, 5.0, ((0, 8),))
    edge_source = draw_edge_source(jax.random.fold_in(splits[29], 71), 0)
    edge_target = draw_edge_target(jax.random.fold_in(splits[29], 71), 0)
    atom_counts = draw_atom_counts(jax.random.fold_in(splits[29], 71), 0)
    edge_counts = draw_edge_counts(jax.random.fold_in(splits[29], 71), 0)
    atom_states = centred(splits[5], (MOLS, A_PAD, H), 0.5, 3.0, ((0, 8),))
    targets = centred(splits[6], (MOLS, TARGETS), 1.0, 5.0, ((0, 8),), jnp.float32)
    label_mask = draw_label_mask(jax.random.fold_in(splits[29], 71), 0)
    edge_input = centred(splits[8], (F, E1), F ** -0.5, 1.5, (), jnp.float32)
    edge_input_first = centred(splits[9], (F, E1), (0.11 * 0.01 / MOLS ** 0.5), 0.00061035156, (), jnp.float32)
    edge_input_second = jnp.clip(jnp.exp(jax.random.uniform(splits[10], (F, E1), jnp.float32, math.log(7.812500091297636e-10), math.log(3.1250000365190544e-09))), 7.812500091297636e-10, 3.1250000365190544e-09)
    edge_output = centred(splits[11], (E1, H * H), (8 * E1 * H) ** -0.5, 0.015625, ((1, 4),), jnp.float32)
    edge_output_first = centred(splits[12], (E1, H * H), (0.11 * 0.001 / MOLS ** 0.5), 6.103515625e-05, ((1, 4),), jnp.float32)
    edge_output_second = jnp.clip(jnp.exp(math.log(3.124999911618964e-11) - 1.3862944 * jax.random.uniform(splits[13], (E1, H * H), jnp.float32) ** block_scale(splits[13], (E1, H * H), ((1, 4),), -0.2, 0.2)), 7.81249977904741e-12, 3.124999911618964e-11)
    gated_weights = centred(splits[14], (2, H, 3 * H), H ** -0.5, 0.5, (), jnp.float32)
    gated_first = centred(splits[15], (2, H, 3 * H), (0.11 * 0.005 / MOLS ** 0.5), 0.00030517578, (), jnp.float32)
    gated_second = jnp.clip(jnp.exp(jax.random.uniform(splits[16], (2, H, 3 * H), jnp.float32, math.log(1.953125022824409e-10), math.log(7.812500091297636e-10))), 1.953125022824409e-10, 7.812500091297636e-10)
    memory_weights = centred(splits[17], (3 * H, 4 * H), (3 * H) ** -0.5, 0.3125, (), jnp.float32)
    memory_first = centred(splits[18], (3 * H, 4 * H), (0.11 * 0.003 / MOLS ** 0.5), 0.00018310547, (), jnp.float32)
    memory_second = jnp.clip(jnp.exp(jax.random.uniform(splits[19], (3 * H, 4 * H), jnp.float32, math.log(7.031249887878843e-11), math.log(2.8124999551515373e-10))), 7.031249887878843e-11, 2.8124999551515373e-10)
    readout_hidden = centred(splits[20], (2 * H, H), (2 * H) ** -0.5, 0.375, (), jnp.float32)
    readout_hidden_first = centred(splits[21], (2 * H, H), (0.11 * 0.01 / MOLS ** 0.5), 0.00061035156, (), jnp.float32)
    readout_hidden_second = jnp.clip(jnp.exp(jax.random.uniform(splits[22], (2 * H, H), jnp.float32, math.log(7.812500091297636e-10), math.log(3.1250000365190544e-09))), 7.812500091297636e-10, 3.1250000365190544e-09)
    readout_final = centred(splits[23], (H, TARGETS), H ** -0.5, 0.5, (), jnp.float32)
    readout_final_first = centred(splits[24], (H, TARGETS), (0.11 * 0.08 / MOLS ** 0.5), 0.0048828125, (), jnp.float32)
    readout_final_second = jnp.clip(jnp.exp(jax.random.uniform(splits[25], (H, TARGETS), jnp.float32, math.log(5.000000058430487e-08), math.log(2.0000000233721948e-07))), 5.000000058430487e-08, 2.0000000233721948e-07)
    bias_vector = centred(splits[26], (NBIAS,), 0.2, 1.0, (), jnp.float32)
    bias_first = centred(splits[27], (NBIAS,), (0.11 * 0.05 / MOLS ** 0.5), 0.0029296875, (), jnp.float32)
    bias_second = jnp.clip(jnp.exp(jax.random.uniform(splits[28], (NBIAS,), jnp.float32, math.log(1.9531249506599124e-08), math.log(7.81249980263965e-08))), 1.9531249506599124e-08, 7.81249980263965e-08)
    return {"edge_feats": edge_feats, "edge_source": edge_source, "edge_target": edge_target, "atom_counts": atom_counts, "edge_counts": edge_counts, "atom_states": atom_states, "targets": targets, "label_mask": label_mask, "edge_input": edge_input, "edge_input_first": edge_input_first, "edge_input_second": edge_input_second, "edge_output": edge_output, "edge_output_first": edge_output_first, "edge_output_second": edge_output_second, "gated_weights": gated_weights, "gated_first": gated_first, "gated_second": gated_second, "memory_weights": memory_weights, "memory_first": memory_first, "memory_second": memory_second, "readout_hidden": readout_hidden, "readout_hidden_first": readout_hidden_first, "readout_hidden_second": readout_hidden_second, "readout_final": readout_final, "readout_final_first": readout_final_first, "readout_final_second": readout_final_second, "bias_vector": bias_vector, "bias_first": bias_first, "bias_second": bias_second}


@jax.custom_vjp
def low(v):
    return lax.optimization_barrier(v.astype(jnp.bfloat16)).astype(jnp.float32)

@jax.custom_vjp
def low_back(v):
    return v

def low_keep(v):
    return (low(v), None)

def low_pass(kept, grad):
    return (grad,)

def back_keep(v):
    return (v, None)

def back_low(kept, grad):
    return (low(grad),)
low.defvjp(low_keep, low_pass)
low_back.defvjp(back_keep, back_low)
FULL_PRECISION = lax.Precision.HIGHEST
BETA_ONE = 0.9
BETA_TWO = 0.999
EPSILON = 1e-08
DECAY = 0.01
RATES = (0.25, 0.004, 0.09, 0.05, 0.06, 0.09, 0.2)

def product(left, right):
    return jnp.dot(left, right, precision=FULL_PRECISION, preferred_element_type=jnp.float32)

def split_bias(bias_vector, width, inner):
    first = bias_vector[:inner]
    gate_in = bias_vector[inner:inner + 3 * width]
    gate_hid = bias_vector[inner + 3 * width:inner + 6 * width]
    memory = bias_vector[inner + 6 * width:inner + 10 * width]
    readout = bias_vector[inner + 10 * width:inner + 11 * width]
    final = bias_vector[inner + 11 * width:]
    return (first, gate_in, gate_hid, memory, readout, final)

def gated_update(gathered, state, state_reduced, gated_low, bias_in, bias_hid):
    width = state.shape[-1]
    gate_in = product(gathered, gated_low[0]) + bias_in
    gate_hid = product(state_reduced, gated_low[1]) + bias_hid
    reset = jax.nn.sigmoid(gate_in[:, :width] + gate_hid[:, :width])
    update = jax.nn.sigmoid(gate_in[:, width:2 * width] + gate_hid[:, width:2 * width])
    candidate = jnp.tanh(gate_in[:, 2 * width:] + reset * gate_hid[:, 2 * width:])
    return (1.0 - update) * candidate + update * state

def readout_loss(state, memory_low, hidden_low, final_low, bias_memory, bias_readout, bias_final, atom_live, targets, label_float, rounding):
    mols, atoms, width = state.shape
    atom_low = rounding(state)
    cell = jnp.zeros((mols, width), jnp.float32)
    memory_low_state = jnp.zeros((mols, width), jnp.float32)
    read_low = jnp.zeros((mols, width), jnp.float32)
    for turn in range(ROUNDS):
        joined = jnp.concatenate([memory_low_state, read_low, memory_low_state], axis=1)
        gates = product(joined, memory_low) + bias_memory
        cell = jax.nn.sigmoid(gates[:, width:2 * width]) * cell + jax.nn.sigmoid(gates[:, :width]) * jnp.tanh(gates[:, 2 * width:3 * width])
        memory_state = jax.nn.sigmoid(gates[:, 3 * width:]) * jnp.tanh(cell)
        memory_low_state = rounding(memory_state)
        scores = jnp.einsum('mac,mc->ma', atom_low, memory_low_state, precision=FULL_PRECISION)
        scores = jnp.where(atom_live, scores, -1000000000.0)
        weights = jnp.exp(scores - lax.optimization_barrier(jnp.max(scores, axis=1, keepdims=True)))
        weights = weights / lax.optimization_barrier(jnp.sum(weights, axis=1, keepdims=True))
        read = jnp.einsum('ma,mac->mc', rounding(weights), atom_low, precision=FULL_PRECISION)
        read_low = rounding(read)
    joined = jnp.concatenate([memory_low_state, read_low], axis=1)
    inner = jax.nn.silu(product(joined, hidden_low) + bias_readout)
    predicted = product(rounding(inner), final_low) + bias_final
    return jnp.sum(label_float * (predicted - targets) ** 2)

def edge_messages(feats, source_onehot, target_onehot, state_reduced, edge_in_low, bias_edge, edge_out_low):
    blocks, edges, _ = feats.shape
    width = state_reduced.shape[-1]
    before = jnp.einsum('mef,fk->mek', feats, edge_in_low, precision=FULL_PRECISION) + bias_edge
    hidden = low(jax.nn.silu(before))
    matrix = low(low_back(jnp.einsum('mek,kj->mej', hidden, edge_out_low, precision=FULL_PRECISION))).reshape(blocks, edges, width, width)
    sent_messages = jnp.einsum('gkn,gny->gky', source_onehot, state_reduced, precision=FULL_PRECISION)
    edge_message = jnp.einsum('merc,mec->mer', matrix, sent_messages, precision=FULL_PRECISION)
    return jnp.einsum('ykh,yks->yhs', target_onehot, edge_message, precision=FULL_PRECISION)

def blocked(value):
    size = 4 if value.shape[0] % 4 == 0 else 2
    return value.reshape((value.shape[0] // size, size) + value.shape[1:])

def loss_parts(params, data):
    edge_input, edge_output, gated_weights, memory_weights, readout_hidden, readout_final, bias_vector = params
    feats, source_onehot, target_onehot, atom_live, state, targets, label_float = data
    mols, atoms, width = state.shape
    bias_parts = split_bias(bias_vector, width, edge_input.shape[1])
    edge_in_low = low(edge_input)
    edge_out_low = low(edge_output)
    gated_low = low(gated_weights)
    block_step = jax.checkpoint(edge_messages)
    for layer in range(LAYERS):
        state_reduced = low(state)

        def one_block(block):
            return block_step(block[0], block[1], block[2], block[3], edge_in_low, bias_parts[0], edge_out_low)
        summed = lax.map(one_block, (blocked(feats), blocked(source_onehot), blocked(target_onehot), blocked(state_reduced)))
        gathered = low(low_back(summed.reshape(mols * atoms, width)))
        state = gated_update(gathered, state.reshape(-1, width), state_reduced.reshape(-1, width), gated_low, bias_parts[1], bias_parts[2]).reshape(mols, atoms, width)
    return readout_loss(state, low(memory_weights), low(readout_hidden), low(readout_final), bias_parts[3], bias_parts[4], bias_parts[5], atom_live, targets, label_float, low)

def adamw(weight, first, second, grad, rate):
    first_new = BETA_ONE * first + (1.0 - BETA_ONE) * grad
    second_new = BETA_TWO * second + (1.0 - BETA_TWO) * grad * grad
    corrected = first_new / (1.0 - BETA_ONE ** STEP)
    scaled = jnp.sqrt(second_new / (1.0 - BETA_TWO ** STEP))
    weight_new = weight - rate * (corrected / (scaled + EPSILON) + DECAY * weight)
    return (weight_new, first_new, second_new, weight_new.astype(jnp.bfloat16))

def reference(edge_feats, edge_source, edge_target, atom_counts, edge_counts, atom_states, targets, label_mask, edge_input, edge_input_first, edge_input_second, edge_output, edge_output_first, edge_output_second, gated_weights, gated_first, gated_second, memory_weights, memory_first, memory_second, readout_hidden, readout_hidden_first, readout_hidden_second, readout_final, readout_final_first, readout_final_second, bias_vector, bias_first, bias_second):
    atom_pad = atom_states.shape[1]
    edge_pad = edge_feats.shape[1]
    slots = jnp.arange(atom_pad, dtype=jnp.int32)
    live = jnp.arange(edge_pad, dtype=jnp.int32)[None, :] < edge_counts[:, None]
    source_onehot = (live[..., None] & (edge_source[..., None] == slots)).astype(jnp.float32)
    target_onehot = (live[..., None] & (edge_target[..., None] == slots)).astype(jnp.float32)
    atom_live = slots[None, :] < atom_counts[:, None]
    label_float = label_mask.astype(jnp.float32)
    count = jnp.sum(label_float)
    data = (edge_feats.astype(jnp.float32), source_onehot, target_onehot, atom_live, atom_states.astype(jnp.float32), targets, label_float)
    params = (edge_input, edge_output, gated_weights, memory_weights, readout_hidden, readout_final, bias_vector)

    def loss_of(weights):
        total = loss_parts(weights, data)
        return (total / count, total)
    loss, pullback, loss_sum = jax.vjp(loss_of, params, has_aux=True)
    grads = pullback(jnp.ones_like(loss))[0]
    firsts = (edge_input_first, edge_output_first, gated_first, memory_first, readout_hidden_first, readout_final_first, bias_first)
    seconds = (edge_input_second, edge_output_second, gated_second, memory_second, readout_hidden_second, readout_final_second, bias_second)
    res = [adamw(params[index], firsts[index], seconds[index], grads[index], RATES[index]) for index in range(7)]
    return (loss_sum, count, res[0][0], res[0][1], res[0][2], res[0][3], res[1][0], res[1][1], res[1][2], res[1][3], res[2][0], res[2][1], res[2][2], res[2][3], res[3][0], res[3][1], res[3][2], res[3][3], res[4][0], res[4][1], res[4][2], res[4][3], res[5][0], res[5][1], res[5][2], res[5][3], res[6][0], res[6][1], res[6][2], res[6][3])
```

```python
import functools

import jax
import jax.numpy as jnp
from jax import lax
from jax.experimental import pallas as pl
from jax.experimental.pallas import tpu as pltpu
from jax.sharding import PartitionSpec as P

LAYERS = 2
ROUNDS = 6
STEP = 10
BETA_ONE = 0.9
BETA_TWO = 0.999
EPSILON = 1e-08
DECAY = 0.01
RATES = (0.25, 0.004, 0.09, 0.05, 0.06, 0.09, 0.2)

MESH = pl.DeviceIdType.MESH
F32 = jnp.float32
BF16 = jnp.bfloat16
GROUP = 8
WIDE = 128


def nn(left, right):
    return lax.dot_general(left, right, (((1,), (0,)), ((), ())), preferred_element_type=F32)


def nt(left, right):
    return lax.dot_general(left, right, (((1,), (1,)), ((), ())), preferred_element_type=F32)


def tn(left, right):
    return lax.dot_general(left, right, (((0,), (0,)), ((), ())), preferred_element_type=F32)


def iota(shape, dim):
    return lax.broadcasted_iota(jnp.int32, shape, dim)


def one_hot(condition):
    return jnp.where(condition, 1.0, 0.0).astype(BF16)


def wide(bias_ref, first, count):
    return jnp.concatenate([bias_ref[first + i : first + i + 1, :] for i in range(count)], axis=1)


def step_kernel(
    ring,
    atom_counts,
    edge_counts,
    feats,
    source,
    target,
    states,
    targets,
    labels,
    edge_in,
    edge_out,
    gated,
    memory,
    hidden_w,
    final_w,
    bias,
    grad_edge,
    grad_in,
    grad_gated,
    grad_memory,
    grad_hidden,
    grad_final,
    grad_bias,
    totals,
    edge_low,
    pairs,
    pair_cols,
    sent,
    turned,
    slope,
    pair_grad,
    lows,
    turned_lows,
    gathered,
    gates,
    state,
    state_grad,
    gate_grad,
    pulled,
    memory_low,
    padded,
    parcels,
    reduce_send,
    reduce_recv,
    send_sem,
    recv_sem,
):
    mols, edges, features = feats.shape
    rows_all, width = states.shape
    atoms = rows_all // mols
    local = width // ring
    groups = mols // GROUP
    span = GROUP * atoms
    half = GROUP * local
    block = rows_all // ring
    n_targets = targets.shape[1]
    me = lax.axis_index("row")

    barrier = pltpu.get_barrier_semaphore()
    for k in range(1, ring):
        pl.semaphore_signal(barrier, inc=1, device_id={"row": lax.rem(me + k, ring)}, device_id_type=MESH)

    for r in range(local):
        edge_low[r * width : (r + 1) * width, :] = edge_out[:, r * width : (r + 1) * width].astype(BF16)
    low_in = edge_in[...].astype(BF16)
    memory_low[...] = memory[...].astype(BF16)

    lane_edge = iota((1, edges), 1)
    row_index = iota((256, edges), 0)
    for m in range(mols):
        pairs[m : m + 1, :] = jnp.where(
            lane_edge < edge_counts[m], source[m : m + 1, :] * atoms + target[m : m + 1, :], -1
        )
    pair_cols[...] = pairs[...].astype(F32).T

    def edge_network(m, carry):
        before = nn(feats[m], low_in) + bias[0:1, :]
        squash = jax.nn.sigmoid(before)
        act = before * squash
        slope[m] = squash + act * (1.0 - squash)
        act = act.astype(BF16)
        pair = pairs[pl.ds(m, 1), :]
        rows = pl.ds(pl.multiple_of(m * atoms, atoms), atoms)
        for part in range(atoms * atoms // 256):
            sums = nn(one_hot(row_index + part * 256 == pair), act).astype(BF16)
            for j in range(256 // atoms):
                a = part * (256 // atoms) + j
                sent[rows, a * width : (a + 1) * width] = sums[j * atoms : (j + 1) * atoms]
        return carry

    lax.fori_loop(0, mols, edge_network, 0)

    order = one_hot(
        (iota((span, span), 1) // atoms == iota((span, span), 0) % GROUP)
        & (iota((span, span), 1) % atoms == iota((span, span), 0) // GROUP)
    )
    order_back = one_hot(
        (iota((span, span), 0) // atoms == iota((span, span), 1) % GROUP)
        & (iota((span, span), 0) % atoms == iota((span, span), 1) // GROUP)
    )
    same_mol = iota((span, half), 0) // atoms == iota((span, half), 1) % GROUP
    same_mol_t = iota((half, span), 0) % GROUP == iota((half, span), 1) // atoms

    def message(layer):
        for g in range(groups):
            lows[layer, g * span : (g + 1) * span, :] = nn(
                order, state_low(layer, g)
            ).astype(BF16)
        low_p = lows[layer]
        turned_lows[:, layer * rows_all : (layer + 1) * rows_all] = low_p.astype(F32).T.astype(BF16)

        def rows_pair(rp, carry):
            t = nt(low_p, edge_low[pl.ds(pl.multiple_of(rp * 2 * width, 2 * width), 2 * width), :])
            for g in range(groups):
                base = (g * LAYERS + layer) * half
                where = pl.ds(pl.multiple_of(base + rp * 16, 16), 16)
                for a in range(atoms):
                    at = g * span + a * GROUP
                    tile = jnp.concatenate([t[at : at + GROUP, :width], t[at : at + GROUP, width:]], axis=0)
                    turned[where, a * width : (a + 1) * width] = tile.astype(BF16)
            return carry

        lax.fori_loop(0, local // 2, rows_pair, 0)
        packed = jnp.zeros((block, WIDE), F32)
        for g in range(groups):
            base = (g * LAYERS + layer) * half
            u = nt(sent[g * span : (g + 1) * span, :], turned[base : base + half, :])
            u = jnp.where(same_mol, u, 0.0).astype(BF16)
            for j in range(span // block):
                slot = g * (span // block) + j
                pick = one_hot(iota((half, WIDE), 1) == slot * local + iota((half, WIDE), 0) // GROUP)
                packed = packed + nn(u[j * block : (j + 1) * block], pick)
        return packed.astype(BF16)

    def state_low(layer, g):
        rows = slice(g * span, (g + 1) * span)
        if layer == 0:
            return states[rows, :]
        return state[layer - 1, rows, :].astype(BF16)

    def exchange(stage):
        copies = []
        for k in range(1, ring):
            copy = pltpu.make_async_remote_copy(
                src_ref=parcels.at[stage, me],
                dst_ref=parcels.at[stage, me],
                send_sem=send_sem.at[stage, k - 1],
                recv_sem=recv_sem.at[stage, k - 1],
                device_id={"row": lax.rem(me + k, ring)},
                device_id_type=MESH,
            )
            copy.start()
            copies.append(copy)
        return copies

    gated_low = [gated[i].astype(BF16) for i in range(2)]
    bias_in = wide(bias, 1, 3)
    bias_hid = wide(bias, 4, 3)
    for layer in range(LAYERS):
        parcels[layer, me] = message(layer)
        if layer == 0:
            pl.semaphore_wait(barrier, ring - 1)
        for copy in exchange(layer):
            copy.wait()
        joined = jnp.concatenate([parcels[layer, q] for q in range(ring)], axis=1)
        for j in range(ring):
            line, column = iota((ring * WIDE, width), 0), iota((ring * WIDE, width), 1)
            pick = one_hot(
                (line % WIDE // local == j) & (line // WIDE == column // local) & (line % local == column % local)
            )
            rows = slice(j * block, (j + 1) * block)
            got = nn(joined, pick).astype(BF16)
            gathered[layer, rows, :] = got
            if layer == 0:
                low = states[rows, :]
                old = low.astype(F32)
            else:
                old = state[layer - 1, rows, :]
                low = old.astype(BF16)
            gate_in = nn(got, gated_low[0]) + bias_in
            gate_hid = nn(low, gated_low[1]) + bias_hid
            reset = jax.nn.sigmoid(gate_in[:, :width] + gate_hid[:, :width])
            update = jax.nn.sigmoid(gate_in[:, width : 2 * width] + gate_hid[:, width : 2 * width])
            third = gate_hid[:, 2 * width :]
            candidate = jnp.tanh(gate_in[:, 2 * width :] + reset * third)
            gates[layer, 0, rows, :] = reset
            gates[layer, 1, rows, :] = update
            gates[layer, 2, rows, :] = candidate
            gates[layer, 3, rows, :] = third
            state[layer, rows, :] = (1.0 - update) * candidate + update * old

    atom_low = state[LAYERS - 1].astype(BF16)
    counts = jnp.zeros((mols, 1), jnp.int32)
    for m in range(mols):
        counts = jnp.where(iota((mols, 1), 0) == m, atom_counts[m], counts)
    lane = iota((mols, rows_all), 1)
    own = (lane // atoms == iota((mols, rows_all), 0)) & (lane % atoms < counts)
    bias_memory = wide(bias, 7, 4)
    zero = jnp.zeros((mols, width), F32)
    cell, mem_low, read_low = zero, zero.astype(BF16), zero.astype(BF16)
    kept = []
    for turn in range(ROUNDS):
        join = jnp.concatenate([mem_low, read_low, mem_low], axis=1)
        z = jnp.broadcast_to(bias_memory, (mols, 4 * width))
        if turn > 0:
            z = nn(join, memory_low[...]) + z
        i = jax.nn.sigmoid(z[:, :width])
        f = jax.nn.sigmoid(z[:, width : 2 * width])
        c = jnp.tanh(z[:, 2 * width : 3 * width])
        o = jax.nn.sigmoid(z[:, 3 * width :])
        before_cell = cell
        cell = f * cell + i * c
        squashed = jnp.tanh(cell)
        mem_low = (o * squashed).astype(BF16)
        scores = jnp.where(own, nt(mem_low, atom_low), -1000000000.0)
        weights = jnp.exp(scores - jnp.max(scores, axis=1, keepdims=True))
        weights = weights / jnp.sum(weights, axis=1, keepdims=True)
        weights_low = weights.astype(BF16)
        read_low = nn(weights_low, atom_low).astype(BF16)
        kept.append((join, i, f, c, o, before_cell, squashed, mem_low, weights, weights_low))
    join = jnp.concatenate([mem_low, read_low], axis=1)
    hidden_low = hidden_w[...].astype(BF16)
    padded[...] = jnp.zeros_like(padded)
    padded[0:width, 0:n_targets] = final_w[...]
    final_low = padded[0:width, :].astype(BF16)
    before = nn(join, hidden_low) + bias[11:12, :]
    squash = jax.nn.sigmoid(before)
    inner = before * squash
    inner_low = inner.astype(BF16)
    padded[width : width + mols, 0:n_targets] = targets[...]
    padded[width + mols : width + 2 * mols, 0:n_targets] = labels[...].astype(F32)
    label = padded[width + mols : width + 2 * mols, :]
    gap = nn(inner_low, final_low) + bias[12:13, :] - padded[width : width + mols, :]
    loss = jnp.sum(label * gap * gap)
    present = jnp.sum(label)
    spot = iota((8, WIDE), 1)
    totals[...] = jnp.where(spot == 0, loss, jnp.where(spot == 1, present, 0.0))
    d_pred = 2.0 * label * gap
    d_pred_low = d_pred.astype(BF16)
    grad_final[...] = tn(d_pred_low, inner_low)
    d_before = nt(d_pred_low, final_low) * (squash + inner * (1.0 - squash))
    d_before_low = d_before.astype(BF16)
    grad_hidden[...] = tn(join, d_before_low)
    grad_bias[...] = jnp.zeros_like(grad_bias)
    grad_bias[11:12, :] = jnp.sum(d_before, axis=0, keepdims=True)
    grad_bias[12:13, :] = jnp.sum(d_pred, axis=0, keepdims=True)
    d_join = nt(d_before_low, hidden_low)
    d_mem, d_read = d_join[:, :width], d_join[:, width:]
    d_cell = zero
    d_bias = jnp.zeros((1, 4 * width), F32)
    lefts, rights, joins, d_gates = [], [], [], []
    for turn in reversed(range(ROUNDS)):
        join, i, f, c, o, before_cell, squashed, mem_low, weights, weights_low = kept[turn]
        d_read_low = d_read.astype(BF16)
        d_weights = nt(d_read_low, atom_low)
        d_scores = weights * (d_weights - jnp.sum(weights * d_weights, axis=1, keepdims=True))
        d_scores_low = d_scores.astype(BF16)
        d_mem = d_mem + nn(d_scores_low, atom_low)
        lefts += [weights_low, d_scores_low]
        rights += [d_read_low, mem_low]
        d_out = d_mem * squashed
        d_cell = d_cell + d_mem * o * (1.0 - squashed * squashed)
        d_z = jnp.concatenate(
            [
                d_cell * c * i * (1.0 - i),
                d_cell * before_cell * f * (1.0 - f),
                d_cell * i * (1.0 - c * c),
                d_out * o * (1.0 - o),
            ],
            axis=1,
        )
        d_cell = d_cell * f
        d_bias = d_bias + jnp.sum(d_z, axis=0, keepdims=True)
        d_z_low = d_z.astype(BF16)
        if turn > 0:
            joins.append(join)
            d_gates.append(d_z_low)
            d_join = nt(d_z_low, memory_low[...])
            d_mem = d_join[:, :width] + d_join[:, 2 * width :]
            d_read = d_join[:, width : 2 * width]
    grad_memory[...] = tn(jnp.concatenate(joins, axis=0), jnp.concatenate(d_gates, axis=0))
    for i in range(4):
        grad_bias[7 + i : 8 + i, :] = d_bias[:, i * width : (i + 1) * width]
    state_grad[...] = tn(jnp.concatenate(lefts, axis=0), jnp.concatenate(rights, axis=0))

    def gated_back(layer):
        bias_parts = [jnp.zeros((1, 3 * width), F32) for _ in range(2)]
        for j in range(ring):
            rows = slice(j * block, (j + 1) * block)
            reset, update = gates[layer, 0, rows, :], gates[layer, 1, rows, :]
            candidate, third = gates[layer, 2, rows, :], gates[layer, 3, rows, :]
            old = states[rows, :].astype(F32) if layer == 0 else state[layer - 1, rows, :]
            grad = state_grad[rows, :]
            d_candidate = grad * (1.0 - update) * (1.0 - candidate * candidate)
            d_update = grad * (old - candidate) * update * (1.0 - update)
            d_reset = d_candidate * third * reset * (1.0 - reset)
            d_in = jnp.concatenate([d_reset, d_update, d_candidate], axis=1)
            d_hid = jnp.concatenate([d_reset, d_update, d_candidate * reset], axis=1)
            bias_parts[0] = bias_parts[0] + jnp.sum(d_in, axis=0, keepdims=True)
            bias_parts[1] = bias_parts[1] + jnp.sum(d_hid, axis=0, keepdims=True)
            d_in_low, d_hid_low = d_in.astype(BF16), d_hid.astype(BF16)
            gate_grad[0, rows, :] = d_in_low
            gate_grad[1, rows, :] = d_hid_low
            pulled[layer, rows, :] = nt(d_in_low, gated_low[0]).astype(BF16)
            if layer > 0:
                state_grad[rows, :] = grad * update + nt(d_hid_low, gated_low[1])
        low = states[...] if layer == 0 else state[layer - 1].astype(BF16)
        d_first = tn(gathered[layer], gate_grad[0])
        d_second = tn(low, gate_grad[1])
        if layer == LAYERS - 1:
            grad_gated[0], grad_gated[1] = d_first, d_second
        else:
            grad_gated[0] += d_first
            grad_gated[1] += d_second
        for s in range(2):
            for i in range(3):
                at = 1 + 3 * s + i
                grad_bias[at : at + 1, :] += bias_parts[s][:, i * width : (i + 1) * width]

    pick_t = one_hot(iota((half, width), 1) == me * local + iota((half, width), 0) // GROUP)
    pick_n = one_hot(iota((width, half), 0) == me * local + iota((width, half), 1) // GROUP)

    def message_back(layer, gt):
        for g in range(groups):
            wide_grad = jnp.where(same_mol_t, nt(pick_t, pulled[layer, g * span : (g + 1) * span, :]), 0.0).astype(BF16)

            def atoms_pair(ap, carry, g=g, wide_grad=wide_grad):
                columns = pl.ds(pl.multiple_of(ap * 2 * width, 2 * width), 2 * width)
                x = nn(wide_grad, sent[g * span : (g + 1) * span, columns])
                where = pl.ds(pl.multiple_of(layer * rows_all + g * span + ap * 16, 16), 16)
                for r in range(local):
                    at = r * GROUP
                    tile = jnp.concatenate([x[at : at + GROUP, :width], x[at : at + GROUP, width:]], axis=0)
                    gt[where, r * width : (r + 1) * width] = tile.astype(BF16)
                return carry

            lax.fori_loop(0, atoms // 2, atoms_pair, 0)

    def run(gt):
        for layer in reversed(range(LAYERS)):
            gated_back(layer)
            message_back(layer, gt)
            if layer > 0:
                back = nn(gt[layer * rows_all : (layer + 1) * rows_all, :], edge_low[...]).astype(BF16)
                for g in range(groups):
                    reduce_send[g * span : (g + 1) * span, :] = nn(order_back, back[g * span : (g + 1) * span]).astype(BF16)
                copies = []
                for k in range(1, ring):
                    peer = lax.rem(me + k, ring)
                    copy = pltpu.make_async_remote_copy(
                        src_ref=reduce_send.at[pl.ds(pl.multiple_of(peer * block, block), block), :],
                        dst_ref=reduce_recv.at[k - 1],
                        send_sem=send_sem.at[LAYERS + 1, k - 1],
                        recv_sem=recv_sem.at[LAYERS + 1, k - 1],
                        device_id={"row": peer},
                        device_id_type=MESH,
                    )
                    copy.start()
                    copies.append(copy)
                for copy in copies:
                    copy.wait()
                total = reduce_send[pl.ds(pl.multiple_of(me * block, block), block), :].astype(F32)
                for k in range(ring - 1):
                    total = total + reduce_recv[k].astype(F32)
                parcels[LAYERS, me] = total.astype(BF16)
                for copy in exchange(LAYERS):
                    copy.wait()
                for j in range(ring):
                    rows = slice(j * block, (j + 1) * block)
                    state_grad[rows, :] += parcels[LAYERS, j].astype(F32)

        def out_weights(rp, carry):
            columns = pl.ds(pl.multiple_of(rp * 2 * width, 2 * width), 2 * width)
            grad_edge[columns, :] = nn(turned_lows[...], gt[:, columns]).T.astype(BF16)
            return carry

        lax.fori_loop(0, local // 2, out_weights, 0)

    pl.run_scoped(run, pltpu.VMEM((LAYERS * rows_all, local * width), BF16))

    for g in range(groups):
        wide_grad = jnp.concatenate(
            [
                jnp.where(same_mol, nn(pulled[layer, g * span : (g + 1) * span, :], pick_n), 0.0).astype(BF16)
                for layer in range(LAYERS)
            ],
            axis=1,
        )

        def pair_back(ap, carry, g=g, wide_grad=wide_grad):
            columns = pl.ds(pl.multiple_of(ap * 2 * width, 2 * width), 2 * width)
            x = nn(wide_grad, turned[g * LAYERS * half : (g + 1) * LAYERS * half, columns]).astype(BF16)
            for s in range(2):
                where = pl.ds(pl.multiple_of((ap * 2 + s) * atoms, atoms), atoms)
                for m in range(GROUP):
                    pair_grad[g * GROUP + m, where, :] = x[m * atoms : (m + 1) * atoms, s * width : (s + 1) * width]
            return carry

        lax.fori_loop(0, atoms // 2, pair_back, 0)

    lane_pair = iota((edges, atoms * atoms), 1).astype(F32)
    lane_mol = iota((edges, mols), 1)

    def edge_back(m, carry):
        total_in, total_bias = carry
        column = jnp.sum(jnp.where(lane_mol == m, pair_cols[...], 0.0), axis=1, keepdims=True)
        d_act = nn(one_hot(lane_pair == column), pair_grad[m])
        d_first = d_act * slope[m]
        total_in = total_in + tn(feats[m], d_first.astype(BF16))
        return (total_in, total_bias + jnp.sum(d_first, axis=0, keepdims=True))

    total_in, total_bias = lax.fori_loop(
        0, mols, edge_back, (jnp.zeros((features, width), F32), jnp.zeros((1, width), F32))
    )
    grad_in[...] = total_in
    grad_bias[0:1, :] = total_bias


def adamw(weight, first, second, grad, rate):
    first_new = BETA_ONE * first + (1.0 - BETA_ONE) * grad
    second_new = BETA_TWO * second + (1.0 - BETA_TWO) * grad * grad
    corrected = first_new / (1.0 - BETA_ONE**STEP)
    scaled = jnp.sqrt(second_new / (1.0 - BETA_TWO**STEP))
    weight_new = weight - rate * (corrected / (scaled + EPSILON) + DECAY * weight)
    return (weight_new, first_new, second_new, weight_new.astype(BF16))


def shards(
    edge_feats,
    edge_source,
    edge_target,
    atom_counts,
    edge_counts,
    atom_states,
    targets,
    label_mask,
    edge_input,
    edge_input_first,
    edge_input_second,
    edge_output,
    edge_output_first,
    edge_output_second,
    gated_weights,
    gated_first,
    gated_second,
    memory_weights,
    memory_first,
    memory_second,
    readout_hidden,
    readout_hidden_first,
    readout_hidden_second,
    readout_final,
    readout_final_first,
    readout_final_second,
    bias_vector,
    bias_first,
    bias_second,
):
    mols, edges, features = edge_feats.shape
    atoms, width = atom_states.shape[1:]
    ring = lax.axis_size("row")
    local = width // ring
    rows_all = mols * atoms
    block = rows_all // ring
    n_bias = bias_vector.shape[0]
    n_targets = targets.shape[1]
    bias_rows = jnp.pad(bias_vector, (0, 16 * WIDE - n_bias)).reshape(16, WIDE)
    vmem = pl.BlockSpec(memory_space=pltpu.VMEM)
    smem = pl.BlockSpec(memory_space=pltpu.SMEM)
    shape = jax.ShapeDtypeStruct
    grad_edge, grad_in, grad_gated, grad_memory, grad_hidden, grad_final, grad_bias, totals = pl.pallas_call(
        functools.partial(step_kernel, ring),
        out_shape=[
            shape((local * width, width), BF16),
            shape((features, width), F32),
            shape((2, width, 3 * width), F32),
            shape((3 * width, 4 * width), F32),
            shape((2 * width, width), F32),
            shape((WIDE, width), F32),
            shape((16, WIDE), F32),
            shape((8, WIDE), F32),
        ],
        in_specs=[smem, smem] + [vmem] * 13,
        out_specs=[vmem] * 8,
        scratch_shapes=[
            pltpu.VMEM((local * width, width), BF16),
            pltpu.VMEM((mols, edges), jnp.int32),
            pltpu.VMEM((edges, mols), F32),
            pltpu.VMEM((rows_all, atoms * width), BF16),
            pltpu.VMEM((mols // GROUP * LAYERS * GROUP * local, atoms * width), BF16),
            pltpu.VMEM((mols, edges, width), F32),
            pltpu.VMEM((mols, atoms * atoms, width), BF16),
            pltpu.VMEM((LAYERS, rows_all, width), BF16),
            pltpu.VMEM((width, LAYERS * rows_all), BF16),
            pltpu.VMEM((LAYERS, rows_all, width), BF16),
            pltpu.VMEM((LAYERS, 4, rows_all, width), F32),
            pltpu.VMEM((LAYERS, rows_all, width), F32),
            pltpu.VMEM((rows_all, width), F32),
            pltpu.VMEM((2, rows_all, 3 * width), BF16),
            pltpu.VMEM((LAYERS, rows_all, width), BF16),
            pltpu.VMEM((3 * width, 4 * width), BF16),
            pltpu.VMEM((width + 2 * mols, WIDE), F32),
            pltpu.VMEM((LAYERS + 1, ring, block, WIDE), BF16),
            pltpu.VMEM((rows_all, width), BF16),
            pltpu.VMEM((ring - 1, block, width), BF16),
            pltpu.SemaphoreType.DMA((LAYERS + 2, ring - 1)),
            pltpu.SemaphoreType.DMA((LAYERS + 2, ring - 1)),
        ],
        compiler_params=pltpu.CompilerParams(
            collective_id=0, has_side_effects=True, vmem_limit_bytes=60 * 1024 * 1024
        ),
    )(
        atom_counts,
        edge_counts,
        edge_feats,
        edge_source,
        edge_target,
        atom_states.reshape(rows_all, width),
        targets,
        label_mask,
        edge_input,
        edge_output,
        gated_weights,
        memory_weights,
        readout_hidden,
        readout_final,
        bias_rows,
    )
    share = 1.0 / ring
    spread = jnp.where(jnp.arange(16)[:, None] == 0, 1.0, share)
    totals = lax.psum(totals, "mol")
    loss_sum, label_count = totals[0, 0], totals[0, 1]
    scale = 1.0 / label_count
    grad_in, grad_gated, grad_memory, grad_hidden, grad_final, grad_bias = lax.psum(
        (
            grad_in,
            grad_gated * share,
            grad_memory * share,
            grad_hidden * share,
            grad_final * share,
            grad_bias * spread,
        ),
        ("mol", "row"),
    )
    grad_edge = lax.psum(grad_edge.astype(F32), "mol").reshape(local, width, width)
    grad_edge = grad_edge.transpose(1, 0, 2).reshape(width, local * width)
    grads = (
        grad_in,
        grad_edge,
        grad_gated,
        grad_memory,
        grad_hidden,
        grad_final.T[:, :n_targets],
        grad_bias.reshape(-1)[:n_bias],
    )
    kept = (
        (edge_input, edge_input_first, edge_input_second),
        (edge_output, edge_output_first, edge_output_second),
        (gated_weights, gated_first, gated_second),
        (memory_weights, memory_first, memory_second),
        (readout_hidden, readout_hidden_first, readout_hidden_second),
        (readout_final, readout_final_first, readout_final_second),
        (bias_vector, bias_first, bias_second),
    )
    outs = (loss_sum, label_count)
    for (weight, first, second), grad, rate in zip(kept, grads, RATES):
        outs += adamw(weight, first, second, grad * scale, rate)
    return outs


def solution(mesh):
    cut = P(None, "row")
    per_mol = (P("mol", None, None), P("mol", None), P("mol", None), P("mol"), P("mol"), P("mol", None, None))
    per_mol += (P("mol", None), P("mol", None))
    return jax.shard_map(
        shards,
        mesh=mesh,
        in_specs=per_mol + (P(),) * 3 + (cut,) * 3 + (P(),) * 15,
        out_specs=(P(),) * 6 + (cut,) * 4 + (P(),) * 20,
        check_vma=False,
    )
```

```python
import functools

import jax
import jax.numpy as jnp
from jax import lax
from jax.experimental import pallas as pl
from jax.experimental.pallas import tpu as pltpu
from jax.sharding import PartitionSpec as P

LAYERS = 2
ROUNDS = 6
STEP = 10
BETA_ONE = 0.9
BETA_TWO = 0.999
EPSILON = 1e-08
DECAY = 0.01
RATES = (0.25, 0.004, 0.09, 0.05, 0.06, 0.09, 0.2)

MESH = pl.DeviceIdType.MESH
F32 = jnp.float32
BF16 = jnp.bfloat16
GROUP = 8
WIDE = 128


def nn(left, right):
    return lax.dot_general(left, right, (((1,), (0,)), ((), ())), preferred_element_type=F32)


def nt(left, right):
    return lax.dot_general(left, right, (((1,), (1,)), ((), ())), preferred_element_type=F32)


def tn(left, right):
    return lax.dot_general(left, right, (((0,), (0,)), ((), ())), preferred_element_type=F32)


def iota(shape, dim):
    return lax.broadcasted_iota(jnp.int32, shape, dim)


def one_hot(condition):
    return jnp.where(condition, 1.0, 0.0).astype(BF16)


def wide(bias_ref, first, count):
    return jnp.concatenate([bias_ref[first + i : first + i + 1, :] for i in range(count)], axis=1)


def round_up(value, unit):
    return -(-value // unit) * unit


class Plan:
    def __init__(self, ring, peers, width, local, features):
        unit = 16 * peers
        self.edge = local * width
        self.edge_part = self.edge // peers
        self.final_at = 12 * width + 2 * width
        self.head = round_up(-(-(self.final_at + 16) // ring), unit)
        self.head_part = self.head // peers
        self.bias_at = 6 * width
        self.rest_own = round_up(-(-(self.bias_at + 16) // ring), 16)
        self.rest = round_up(self.rest_own + features + 16, unit)
        self.rest_part = self.rest // peers


def step_kernel(
    ring,
    peers,
    atom_counts,
    edge_counts,
    feats,
    source,
    target,
    states,
    targets,
    labels,
    edge_in,
    edge_out,
    gated,
    memory,
    hidden_w,
    final_w,
    bias,
    edge_sum,
    head_sum,
    rest_sum,
    totals,
    edge_low,
    pairs,
    pair_cols,
    sent,
    turned,
    slope,
    pair_grad,
    lows,
    turned_lows,
    gathered,
    gates,
    state,
    state_grad,
    gate_grad,
    pulled,
    memory_low,
    padded,
    parcels,
    reduce_send,
    reduce_recv,
    grad_gated,
    grad_bias,
    totals_all,
    edge_part,
    edge_recv,
    edge_all,
    head_part,
    head_recv,
    head_all,
    rest_full,
    rest_part,
    rest_recv,
    rest_all,
    send_sem,
    recv_sem,
    far_send,
    far_recv,
    gt,
):
    mols, features, edges = feats.shape
    rows_all, width = states.shape
    atoms = rows_all // mols
    local = width // ring
    groups = mols // GROUP
    span = GROUP * atoms
    half = GROUP * local
    block = rows_all // ring
    n_targets = targets.shape[1]
    me = lax.axis_index("row")
    place = lax.axis_index("mol")
    plan = Plan(ring, peers, width, local, features)
    started = []

    def rows16(start, count):
        return pl.ds(pl.multiple_of(start, 16), count)

    def far_copy(stage, index, peer, source_ref, target_ref):
        copy = pltpu.make_async_remote_copy(
            src_ref=source_ref,
            dst_ref=target_ref,
            send_sem=far_send.at[stage, index],
            recv_sem=far_recv.at[stage, index],
            device_id={"mol": peer},
            device_id_type=MESH,
        )
        copy.start()
        started.append(copy)
        return copy

    def row_copy(stage, k, source_ref, target_ref):
        copy = pltpu.make_async_remote_copy(
            src_ref=source_ref,
            dst_ref=target_ref,
            send_sem=send_sem.at[stage, k - 1],
            recv_sem=recv_sem.at[stage, k - 1],
            device_id={"row": lax.rem(me + k, ring)},
            device_id_type=MESH,
        )
        copy.start()
        started.append(copy)
        return copy

    barrier = pltpu.get_barrier_semaphore()
    for k in range(1, ring):
        pl.semaphore_signal(barrier, inc=1, device_id={"row": lax.rem(me + k, ring)}, device_id_type=MESH)
    for k in range(1, peers):
        pl.semaphore_signal(barrier, inc=1, device_id={"mol": lax.rem(place + k, peers)}, device_id_type=MESH)

    for r in range(local):
        edge_low[r * width : (r + 1) * width, :] = edge_out[:, r * width : (r + 1) * width].astype(BF16)
    low_in = edge_in[...].astype(BF16)
    memory_low[...] = memory[...].astype(BF16)

    lane_edge = iota((1, edges), 1)
    row_index = iota((256, edges), 0)
    for m in range(mols):
        pairs[m : m + 1, :] = jnp.where(
            lane_edge < edge_counts[m], source[m : m + 1, :] * atoms + target[m : m + 1, :], -1
        )
    pair_cols[...] = pairs[...].astype(F32).T

    def edge_network(m, carry):
        before = tn(feats[m], low_in) + bias[0:1, :]
        squash = jax.nn.sigmoid(before)
        act = before * squash
        slope[m] = squash + act * (1.0 - squash)
        act = act.astype(BF16)
        pair = pairs[pl.ds(m, 1), :]
        rows = pl.ds(pl.multiple_of(m * atoms, atoms), atoms)
        for part in range(atoms * atoms // 256):
            sums = nn(one_hot(row_index + part * 256 == pair), act).astype(BF16)
            for j in range(256 // atoms):
                a = part * (256 // atoms) + j
                sent[rows, a * width : (a + 1) * width] = sums[j * atoms : (j + 1) * atoms]
        return carry

    lax.fori_loop(0, mols, edge_network, 0)

    order = one_hot(
        (iota((span, span), 1) // atoms == iota((span, span), 0) % GROUP)
        & (iota((span, span), 1) % atoms == iota((span, span), 0) // GROUP)
    )
    order_back = one_hot(
        (iota((span, span), 0) // atoms == iota((span, span), 1) % GROUP)
        & (iota((span, span), 0) % atoms == iota((span, span), 1) // GROUP)
    )
    same_mol = iota((span, half), 0) // atoms == iota((span, half), 1) % GROUP
    same_mol_t = iota((half, span), 0) % GROUP == iota((half, span), 1) // atoms

    def message(layer):
        for g in range(groups):
            lows[layer, g * span : (g + 1) * span, :] = nn(
                order, state_low(layer, g)
            ).astype(BF16)
        low_p = lows[layer]
        turned_lows[:, layer * rows_all : (layer + 1) * rows_all] = low_p.astype(F32).T.astype(BF16)

        def rows_pair(rp, carry):
            t = nt(low_p, edge_low[pl.ds(pl.multiple_of(rp * 2 * width, 2 * width), 2 * width), :])
            for g in range(groups):
                base = (g * LAYERS + layer) * half
                where = pl.ds(pl.multiple_of(base + rp * 16, 16), 16)
                for a in range(atoms):
                    at = g * span + a * GROUP
                    tile = jnp.concatenate([t[at : at + GROUP, :width], t[at : at + GROUP, width:]], axis=0)
                    turned[where, a * width : (a + 1) * width] = tile.astype(BF16)
            return carry

        lax.fori_loop(0, local // 2, rows_pair, 0)
        packed = jnp.zeros((block, WIDE), F32)
        for g in range(groups):
            base = (g * LAYERS + layer) * half
            u = nt(sent[g * span : (g + 1) * span, :], turned[base : base + half, :])
            u = jnp.where(same_mol, u, 0.0).astype(BF16)
            for j in range(span // block):
                slot = g * (span // block) + j
                pick = one_hot(iota((half, WIDE), 1) == slot * local + iota((half, WIDE), 0) // GROUP)
                packed = packed + nn(u[j * block : (j + 1) * block], pick)
        return packed.astype(BF16)

    def state_low(layer, g):
        rows = slice(g * span, (g + 1) * span)
        if layer == 0:
            return states[rows, :]
        return state[layer - 1, rows, :].astype(BF16)

    def exchange(stage):
        return [row_copy(stage, k, parcels.at[stage, me], parcels.at[stage, me]) for k in range(1, ring)]

    gated_low = [gated[i].astype(BF16) for i in range(2)]
    bias_in = wide(bias, 1, 3)
    bias_hid = wide(bias, 4, 3)
    for layer in range(LAYERS):
        parcels[layer, me] = message(layer)
        if layer == 0:
            pl.semaphore_wait(barrier, ring + peers - 2)
        for copy in exchange(layer):
            copy.wait_recv()
        joined = jnp.concatenate([parcels[layer, q] for q in range(ring)], axis=1)
        for j in range(ring):
            line, column = iota((ring * WIDE, width), 0), iota((ring * WIDE, width), 1)
            pick = one_hot(
                (line % WIDE // local == j) & (line // WIDE == column // local) & (line % local == column % local)
            )
            rows = slice(j * block, (j + 1) * block)
            got = nn(joined, pick).astype(BF16)
            gathered[layer, rows, :] = got
            if layer == 0:
                low = states[rows, :]
                old = low.astype(F32)
            else:
                old = state[layer - 1, rows, :]
                low = old.astype(BF16)
            gate_in = nn(got, gated_low[0]) + bias_in
            gate_hid = nn(low, gated_low[1]) + bias_hid
            reset = jax.nn.sigmoid(gate_in[:, :width] + gate_hid[:, :width])
            update = jax.nn.sigmoid(gate_in[:, width : 2 * width] + gate_hid[:, width : 2 * width])
            third = gate_hid[:, 2 * width :]
            candidate = jnp.tanh(gate_in[:, 2 * width :] + reset * third)
            gates[layer, 0, rows, :] = reset
            gates[layer, 1, rows, :] = update
            gates[layer, 2, rows, :] = candidate
            gates[layer, 3, rows, :] = third
            state[layer, rows, :] = (1.0 - update) * candidate + update * old

    atom_low = state[LAYERS - 1].astype(BF16)
    counts = jnp.zeros((mols, 1), jnp.int32)
    for m in range(mols):
        counts = jnp.where(iota((mols, 1), 0) == m, atom_counts[m], counts)
    lane = iota((mols, rows_all), 1)
    own = (lane // atoms == iota((mols, rows_all), 0)) & (lane % atoms < counts)
    bias_memory = wide(bias, 7, 4)
    zero = jnp.zeros((mols, width), F32)
    cell, mem_low, read_low = zero, zero.astype(BF16), zero.astype(BF16)
    kept = []
    for turn in range(ROUNDS):
        join = jnp.concatenate([mem_low, read_low, mem_low], axis=1)
        z = jnp.broadcast_to(bias_memory, (mols, 4 * width))
        if turn > 0:
            z = nn(join, memory_low[...]) + z
        i = jax.nn.sigmoid(z[:, :width])
        f = jax.nn.sigmoid(z[:, width : 2 * width])
        c = jnp.tanh(z[:, 2 * width : 3 * width])
        o = jax.nn.sigmoid(z[:, 3 * width :])
        before_cell = cell
        cell = f * cell + i * c
        squashed = jnp.tanh(cell)
        mem_low = (o * squashed).astype(BF16)
        scores = jnp.where(own, nt(mem_low, atom_low), -1000000000.0)
        weights = jnp.exp(scores - jnp.max(scores, axis=1, keepdims=True))
        weights = weights / jnp.sum(weights, axis=1, keepdims=True)
        weights_low = weights.astype(BF16)
        read_low = nn(weights_low, atom_low).astype(BF16)
        kept.append((join, i, f, c, o, before_cell, squashed, mem_low, weights, weights_low))
    join = jnp.concatenate([mem_low, read_low], axis=1)
    hidden_low = hidden_w[...].astype(BF16)
    padded[...] = jnp.zeros_like(padded)
    padded[0:n_targets, :] = final_w[...]
    final_low = padded[0:width, :].astype(BF16)
    before = nn(join, hidden_low) + bias[11:12, :]
    squash = jax.nn.sigmoid(before)
    inner = before * squash
    inner_low = inner.astype(BF16)
    padded[width : width + mols, 0:n_targets] = targets[...]
    padded[width + mols : width + 2 * mols, 0:n_targets] = labels[...].astype(F32)
    label = padded[width + mols : width + 2 * mols, :]
    gap = nt(inner_low, final_low) + bias[12:13, :] - padded[width : width + mols, :]
    loss = jnp.sum(label * gap * gap)
    present = jnp.sum(label)
    spot = iota((8, WIDE), 1)
    totals_all[place] = jnp.where(spot == 0, loss, jnp.where(spot == 1, present, 0.0))
    total_copies = [
        far_copy(0, k - 1, lax.rem(place + k, peers), totals_all.at[place], totals_all.at[place])
        for k in range(1, peers)
    ]
    d_pred = 2.0 * label * gap
    d_pred_low = d_pred.astype(BF16)
    head_part[plan.final_at : plan.final_at + 16, :] = tn(d_pred_low, inner_low)[0:16].astype(BF16)
    d_before = nn(d_pred_low, final_low) * (squash + inner * (1.0 - squash))
    d_before_low = d_before.astype(BF16)
    head_part[12 * width : 14 * width, :] = tn(join, d_before_low).astype(BF16)
    grad_bias[...] = jnp.zeros_like(grad_bias)
    grad_bias[11:12, :] = jnp.sum(d_before, axis=0, keepdims=True)
    grad_bias[12:13, :] = jnp.sum(d_pred, axis=0, keepdims=True)
    d_join = nt(d_before_low, hidden_low)
    d_mem, d_read = d_join[:, :width], d_join[:, width:]
    d_cell = zero
    d_bias = jnp.zeros((1, 4 * width), F32)
    lefts, rights, joins, d_gates = [], [], [], []
    for turn in reversed(range(ROUNDS)):
        join, i, f, c, o, before_cell, squashed, mem_low, weights, weights_low = kept[turn]
        d_read_low = d_read.astype(BF16)
        d_weights = nt(d_read_low, atom_low)
        d_scores = weights * (d_weights - jnp.sum(weights * d_weights, axis=1, keepdims=True))
        d_scores_low = d_scores.astype(BF16)
        d_mem = d_mem + nn(d_scores_low, atom_low)
        lefts += [weights_low, d_scores_low]
        rights += [d_read_low, mem_low]
        d_out = d_mem * squashed
        d_cell = d_cell + d_mem * o * (1.0 - squashed * squashed)
        d_z = jnp.concatenate(
            [
                d_cell * c * i * (1.0 - i),
                d_cell * before_cell * f * (1.0 - f),
                d_cell * i * (1.0 - c * c),
                d_out * o * (1.0 - o),
            ],
            axis=1,
        )
        d_cell = d_cell * f
        d_bias = d_bias + jnp.sum(d_z, axis=0, keepdims=True)
        d_z_low = d_z.astype(BF16)
        if turn > 0:
            joins.append(join)
            d_gates.append(d_z_low)
            d_join = nt(d_z_low, memory_low[...])
            d_mem = d_join[:, :width] + d_join[:, 2 * width :]
            d_read = d_join[:, width : 2 * width]
    grad_memory = tn(jnp.concatenate(joins, axis=0), jnp.concatenate(d_gates, axis=0)).astype(BF16)
    for i in range(4):
        head_part[i * 3 * width : (i + 1) * 3 * width, :] = grad_memory[:, i * width : (i + 1) * width]
    used = plan.final_at + 16
    head_part[used:, :] = jnp.zeros((ring * plan.head - used, WIDE), BF16)
    head_copies = []
    for k in range(1, peers):
        peer = lax.rem(place + k, peers)
        rows = rows16(me * plan.head + peer * plan.head_part, plan.head_part)
        head_copies.append(far_copy(1, k - 1, peer, head_part.at[rows, :], head_recv.at[k - 1]))
    for i in range(4):
        grad_bias[7 + i : 8 + i, :] = d_bias[:, i * width : (i + 1) * width]
    state_grad[...] = tn(jnp.concatenate(lefts, axis=0), jnp.concatenate(rights, axis=0))

    def gated_back(layer):
        bias_parts = [jnp.zeros((1, 3 * width), F32) for _ in range(2)]
        for j in range(ring):
            rows = slice(j * block, (j + 1) * block)
            reset, update = gates[layer, 0, rows, :], gates[layer, 1, rows, :]
            candidate, third = gates[layer, 2, rows, :], gates[layer, 3, rows, :]
            old = states[rows, :].astype(F32) if layer == 0 else state[layer - 1, rows, :]
            grad = state_grad[rows, :]
            d_candidate = grad * (1.0 - update) * (1.0 - candidate * candidate)
            d_update = grad * (old - candidate) * update * (1.0 - update)
            d_reset = d_candidate * third * reset * (1.0 - reset)
            d_in = jnp.concatenate([d_reset, d_update, d_candidate], axis=1)
            d_hid = jnp.concatenate([d_reset, d_update, d_candidate * reset], axis=1)
            bias_parts[0] = bias_parts[0] + jnp.sum(d_in, axis=0, keepdims=True)
            bias_parts[1] = bias_parts[1] + jnp.sum(d_hid, axis=0, keepdims=True)
            d_in_low, d_hid_low = d_in.astype(BF16), d_hid.astype(BF16)
            gate_grad[0, rows, :] = d_in_low
            gate_grad[1, rows, :] = d_hid_low
            pulled[layer, rows, :] = nt(d_in_low, gated_low[0]).astype(BF16)
            if layer > 0:
                state_grad[rows, :] = grad * update + nt(d_hid_low, gated_low[1])
        low = states[...] if layer == 0 else state[layer - 1].astype(BF16)
        d_first = tn(gathered[layer], gate_grad[0])
        d_second = tn(low, gate_grad[1])
        if layer == LAYERS - 1:
            grad_gated[0], grad_gated[1] = d_first, d_second
        else:
            grad_gated[0] += d_first
            grad_gated[1] += d_second
        for s in range(2):
            for i in range(3):
                at = 1 + 3 * s + i
                grad_bias[at : at + 1, :] += bias_parts[s][:, i * width : (i + 1) * width]

    pick_t = one_hot(iota((half, width), 1) == me * local + iota((half, width), 0) // GROUP)
    pick_n = one_hot(iota((width, half), 0) == me * local + iota((width, half), 1) // GROUP)

    def message_back(layer):
        for g in range(groups):
            wide_grad = jnp.where(same_mol_t, nt(pick_t, pulled[layer, g * span : (g + 1) * span, :]), 0.0).astype(BF16)

            def atoms_pair(ap, carry, g=g, wide_grad=wide_grad):
                columns = pl.ds(pl.multiple_of(ap * 2 * width, 2 * width), 2 * width)
                x = nn(wide_grad, sent[g * span : (g + 1) * span, columns])
                where = pl.ds(pl.multiple_of(layer * rows_all + g * span + ap * 16, 16), 16)
                for r in range(local):
                    at = r * GROUP
                    tile = jnp.concatenate([x[at : at + GROUP, :width], x[at : at + GROUP, width:]], axis=0)
                    gt[where, r * width : (r + 1) * width] = tile.astype(BF16)
                return carry

            lax.fori_loop(0, atoms // 2, atoms_pair, 0)

    edge_copies = []
    for layer in reversed(range(LAYERS)):
        gated_back(layer)
        message_back(layer)
        if layer > 0:
            back = nn(gt[layer * rows_all : (layer + 1) * rows_all, :], edge_low[...]).astype(BF16)
            for g in range(groups):
                reduce_send[g * span : (g + 1) * span, :] = nn(order_back, back[g * span : (g + 1) * span]).astype(BF16)
            copies = []
            for k in range(1, ring):
                rows = rows16(lax.rem(me + k, ring) * block, block)
                copies.append(row_copy(LAYERS + 1, k, reduce_send.at[rows, :], reduce_recv.at[k - 1]))
            for copy in copies:
                copy.wait_recv()
            total = reduce_send[pl.ds(pl.multiple_of(me * block, block), block), :].astype(F32)
            for k in range(ring - 1):
                total = total + reduce_recv[k].astype(F32)
            parcels[LAYERS, me] = total.astype(BF16)
            for copy in exchange(LAYERS):
                copy.wait_recv()
            for j in range(ring):
                rows = slice(j * block, (j + 1) * block)
                state_grad[rows, :] += parcels[LAYERS, j].astype(F32)

    for copy in head_copies:
        copy.wait_recv()
    mine = rows16(me * plan.head + place * plan.head_part, plan.head_part)
    total = head_part[mine, :].astype(F32)
    for k in range(peers - 1):
        total = total + head_recv[k].astype(F32)
    head_all[mine, :] = total.astype(BF16)
    head_copies[:] = [
        far_copy(2, k - 1, lax.rem(place + k, peers), head_all.at[mine, :], head_all.at[mine, :])
        for k in range(1, peers)
    ]

    chunk = max(plan.edge_part, 2 * width)
    chunks, parts = plan.edge // chunk, chunk // plan.edge_part
    home, seat = lax.div(place, parts), lax.rem(place, parts)
    for j in [*range(1, chunks), 0]:
        here = lax.rem(home + j, chunks)
        for i in range(chunk // (2 * width)):
            columns = pl.ds(pl.multiple_of(here * chunk + i * 2 * width, 2 * width), 2 * width)
            edge_part[columns, :] = nn(turned_lows[...], gt[:, columns]).T.astype(BF16)
        for i in range(1 if j == 0 else 0, parts):
            peer = here * parts + lax.rem(seat + i, parts)
            k = lax.rem(peer - place + peers, peers)
            rows = rows16(peer * plan.edge_part, plan.edge_part)
            edge_copies.append(far_copy(3, k - 1, peer, edge_part.at[rows, :], edge_recv.at[k - 1]))

    for g in range(groups):
        wide_grad = jnp.concatenate(
            [
                jnp.where(same_mol, nn(pulled[layer, g * span : (g + 1) * span, :], pick_n), 0.0).astype(BF16)
                for layer in range(LAYERS)
            ],
            axis=1,
        )

        def pair_back(ap, carry, g=g, wide_grad=wide_grad):
            columns = pl.ds(pl.multiple_of(ap * 2 * width, 2 * width), 2 * width)
            x = nn(wide_grad, turned[g * LAYERS * half : (g + 1) * LAYERS * half, columns]).astype(BF16)
            for s in range(2):
                where = pl.ds(pl.multiple_of((ap * 2 + s) * atoms, atoms), atoms)
                for m in range(GROUP):
                    pair_grad[g * GROUP + m, where, :] = x[m * atoms : (m + 1) * atoms, s * width : (s + 1) * width]
            return carry

        lax.fori_loop(0, atoms // 2, pair_back, 0)

    lane_pair = iota((edges, atoms * atoms), 1).astype(F32)
    lane_mol = iota((edges, mols), 1)

    def edge_back(m, carry):
        total_in, total_bias = carry
        column = jnp.sum(jnp.where(lane_mol == m, pair_cols[...], 0.0), axis=1, keepdims=True)
        d_act = nn(one_hot(lane_pair == column), pair_grad[m])
        d_first = d_act * slope[m]
        total_in = total_in + nn(feats[m], d_first.astype(BF16))
        return (total_in, total_bias + jnp.sum(d_first, axis=0, keepdims=True))

    total_in, total_bias = lax.fori_loop(
        0, mols, edge_back, (jnp.zeros((features, width), F32), jnp.zeros((1, width), F32))
    )

    for s in range(2):
        for i in range(3):
            at = (s * 3 + i) * width
            rest_full[at : at + width, :] = grad_gated[s, :, i * width : (i + 1) * width].astype(BF16)
    rest_full[plan.bias_at : plan.bias_at + 16, :] = grad_bias[...].astype(BF16)
    used = plan.bias_at + 16
    if ring * plan.rest_own > used:
        rest_full[used:, :] = jnp.zeros((ring * plan.rest_own - used, WIDE), BF16)
    rest_part[0 : plan.rest_own, :] = rest_full[rows16(me * plan.rest_own, plan.rest_own), :]
    at = plan.rest_own
    rest_part[at : at + features, :] = total_in.astype(BF16)
    at += features
    rest_part[at : at + 16, :] = jnp.where(iota((16, WIDE), 0) == 0, total_bias, 0.0).astype(BF16)
    at += 16
    if plan.rest > at:
        rest_part[at:, :] = jnp.zeros((plan.rest - at, WIDE), BF16)
    rest_copies = []
    for k in range(1, peers):
        peer = lax.rem(place + k, peers)
        rows = rows16(peer * plan.rest_part, plan.rest_part)
        rest_copies.append(far_copy(4, k - 1, peer, rest_part.at[rows, :], rest_recv.at[k - 1]))

    for copy in edge_copies:
        copy.wait_recv()
    mine = rows16(place * plan.edge_part, plan.edge_part)
    total = edge_part[mine, :].astype(F32)
    for k in range(peers - 1):
        total = total + edge_recv[k].astype(F32)
    edge_all[mine, :] = total.astype(BF16)
    pairs_of = peers // 2
    line, side = lax.div(place, 2), lax.rem(place, 2)
    neighbour = line * 2 + 1 - side
    across = [
        far_copy(5, k, lax.rem(line + k, pairs_of) * 2 + side, edge_all.at[mine, :], edge_all.at[mine, :])
        for k in range(1, pairs_of)
    ]
    beside = [far_copy(5, 0, neighbour, edge_all.at[mine, :], edge_all.at[mine, :])]

    for copy in head_copies:
        copy.wait_recv()
    rows = rows16(me * plan.head, plan.head)
    head_rows = [row_copy(LAYERS + 2, k, head_all.at[rows, :], head_all.at[rows, :]) for k in range(1, ring)]

    for copy in rest_copies:
        copy.wait_recv()
    mine = rows16(place * plan.rest_part, plan.rest_part)
    total = rest_part[mine, :].astype(F32)
    for k in range(peers - 1):
        total = total + rest_recv[k].astype(F32)
    rest_all[me, mine, :] = total.astype(BF16)
    rest_copies = [
        far_copy(6, k - 1, lax.rem(place + k, peers), rest_all.at[me, mine, :], rest_all.at[me, mine, :])
        for k in range(1, peers)
    ]

    for k in range(1, pairs_of):
        across[k - 1].wait_recv()
        rows = rows16((lax.rem(line - k + pairs_of, pairs_of) * 2 + side) * plan.edge_part, plan.edge_part)
        beside.append(far_copy(5, pairs_of + k - 1, neighbour, edge_all.at[rows, :], edge_all.at[rows, :]))
    for copy in rest_copies:
        copy.wait_recv()
    rest_rows = [row_copy(LAYERS + 3, k, rest_all.at[me], rest_all.at[me]) for k in range(1, ring)]
    for copy in total_copies + head_rows:
        copy.wait_recv()
    total = totals_all[0]
    for k in range(1, peers):
        total = total + totals_all[k]
    totals[...] = total
    head_sum[...] = head_all[...]
    for copy in beside:
        copy.wait_recv()
    edge_sum[...] = edge_all[...]
    for copy in rest_rows:
        copy.wait_recv()
    rest_sum[...] = rest_all[...]
    for copy in started:
        copy.wait_send()


def adamw(weight, first, second, grad, rate):
    first_new = BETA_ONE * first + (1.0 - BETA_ONE) * grad
    second_new = BETA_TWO * second + (1.0 - BETA_TWO) * grad * grad
    corrected = first_new / (1.0 - BETA_ONE**STEP)
    scaled = jnp.sqrt(second_new / (1.0 - BETA_TWO**STEP))
    weight_new = weight - rate * (corrected / (scaled + EPSILON) + DECAY * weight)
    return (weight_new, first_new, second_new, weight_new.astype(BF16))


def update_kernel(ring, peers, local, counted, totals, edge_sum, head_sum, rest_sum, *refs):
    olds, news = refs[:21], refs[23:]
    loss_out, count_out = refs[21:23]
    features, width = olds[0].shape
    plan = Plan(ring, peers, width, local, features)
    inverse = (1.0 / totals[0:1, :])[0:1, 1:2]

    def update(index, view, grad):
        parts = [ref[view] for ref in olds[3 * index : 3 * index + 3]]
        for ref, value in zip(news[4 * index : 4 * index + 4], adamw(*parts, grad * inverse, RATES[index])):
            ref[view] = value

    for i in range(edge_sum.shape[0] // width):
        update(1, (slice(None), slice(i * width, (i + 1) * width)), edge_sum[i * width : (i + 1) * width, :].astype(F32))

    @pl.when(pl.program_id(0) == 0)
    def _():
        loss_out[0] = counted[0, 0]
        count_out[0] = counted[0, 1]
        rest = jnp.concatenate([rest_sum[q, 0 : plan.rest_own, :] for q in range(ring)], axis=0).astype(F32)
        own = sum(rest_sum[q, plan.rest_own : plan.rest_own + features + 16, :].astype(F32) for q in range(ring))
        update(0, (slice(None), slice(None)), own[0:features])
        for s in range(2):
            for i in range(3):
                at = (s * 3 + i) * width
                update(2, (s, slice(None), slice(i * width, (i + 1) * width)), rest[at : at + width])
        for i in range(4):
            part = head_sum[i * 3 * width : (i + 1) * 3 * width, :].astype(F32)
            update(3, (slice(None), slice(i * width, (i + 1) * width)), part)
        update(4, (slice(None), slice(None)), head_sum[12 * width : 14 * width, :].astype(F32))
        n_targets = olds[15].shape[0]
        update(5, (slice(None), slice(None)), head_sum[plan.final_at : plan.final_at + 16, :].astype(F32)[0:n_targets])
        biases = rest[plan.bias_at : plan.bias_at + 16]
        update(6, (slice(None), slice(None)), jnp.where(iota((16, WIDE), 0) == 0, own[features : features + 1], biases))


def shards(
    edge_feats,
    edge_source,
    edge_target,
    atom_counts,
    edge_counts,
    atom_states,
    targets,
    label_mask,
    edge_input,
    edge_input_first,
    edge_input_second,
    edge_output,
    edge_output_first,
    edge_output_second,
    gated_weights,
    gated_first,
    gated_second,
    memory_weights,
    memory_first,
    memory_second,
    readout_hidden,
    readout_hidden_first,
    readout_hidden_second,
    readout_final,
    readout_final_first,
    readout_final_second,
    bias_vector,
    bias_first,
    bias_second,
):
    mols, edges, features = edge_feats.shape
    atoms, width = atom_states.shape[1:]
    ring = lax.axis_size("row")
    local = width // ring
    rows_all = mols * atoms
    block = rows_all // ring
    n_bias = bias_vector.shape[0]
    n_targets = targets.shape[1]
    peers = lax.axis_size("mol")
    plan = Plan(ring, peers, width, local, features)

    def bias_rows(value):
        return jnp.pad(value, (0, 16 * WIDE - n_bias)).reshape(16, WIDE)

    bias_olds = [bias_rows(value) for value in (bias_vector, bias_first, bias_second)]
    finals = [value.T for value in (readout_final, readout_final_first, readout_final_second)]
    vmem = pl.BlockSpec(memory_space=pltpu.VMEM)
    smem = pl.BlockSpec(memory_space=pltpu.SMEM)
    shape = jax.ShapeDtypeStruct
    edge_sum, head_sum, rest_sum, totals = pl.pallas_call(
        functools.partial(step_kernel, ring, peers),
        out_shape=[
            shape((plan.edge, WIDE), BF16),
            shape((ring * plan.head, WIDE), BF16),
            shape((ring, plan.rest, WIDE), BF16),
            shape((8, WIDE), F32),
        ],
        in_specs=[smem, smem] + [vmem] * 13,
        out_specs=[vmem] * 4,
        scratch_shapes=[
            pltpu.VMEM((local * width, width), BF16),
            pltpu.VMEM((mols, edges), jnp.int32),
            pltpu.VMEM((edges, mols), F32),
            pltpu.VMEM((rows_all, atoms * width), BF16),
            pltpu.VMEM((mols // GROUP * LAYERS * GROUP * local, atoms * width), BF16),
            pltpu.VMEM((mols, edges, width), F32),
            pltpu.VMEM((mols, atoms * atoms, width), BF16),
            pltpu.VMEM((LAYERS, rows_all, width), BF16),
            pltpu.VMEM((width, LAYERS * rows_all), BF16),
            pltpu.VMEM((LAYERS, rows_all, width), BF16),
            pltpu.VMEM((LAYERS, 4, rows_all, width), F32),
            pltpu.VMEM((LAYERS, rows_all, width), F32),
            pltpu.VMEM((rows_all, width), F32),
            pltpu.VMEM((2, rows_all, 3 * width), BF16),
            pltpu.VMEM((LAYERS, rows_all, width), BF16),
            pltpu.VMEM((3 * width, 4 * width), BF16),
            pltpu.VMEM((width + 2 * mols, WIDE), F32),
            pltpu.VMEM((LAYERS + 1, ring, block, WIDE), BF16),
            pltpu.VMEM((rows_all, width), BF16),
            pltpu.VMEM((ring - 1, block, width), BF16),
            pltpu.VMEM((2, width, 3 * width), F32),
            pltpu.VMEM((16, WIDE), F32),
            pltpu.VMEM((peers, 8, WIDE), F32),
            pltpu.VMEM((plan.edge, WIDE), BF16),
            pltpu.VMEM((peers - 1, plan.edge_part, WIDE), BF16),
            pltpu.VMEM((plan.edge, WIDE), BF16),
            pltpu.VMEM((ring * plan.head, WIDE), BF16),
            pltpu.VMEM((peers - 1, plan.head_part, WIDE), BF16),
            pltpu.VMEM((ring * plan.head, WIDE), BF16),
            pltpu.VMEM((ring * plan.rest_own, WIDE), BF16),
            pltpu.VMEM((plan.rest, WIDE), BF16),
            pltpu.VMEM((peers - 1, plan.rest_part, WIDE), BF16),
            pltpu.VMEM((ring, plan.rest, WIDE), BF16),
            pltpu.SemaphoreType.DMA((LAYERS + 4, ring - 1)),
            pltpu.SemaphoreType.DMA((LAYERS + 4, ring - 1)),
            pltpu.SemaphoreType.DMA((7, peers)),
            pltpu.SemaphoreType.DMA((7, peers)),
            pltpu.VMEM((LAYERS * rows_all, local * width), BF16),
        ],
        compiler_params=pltpu.CompilerParams(
            collective_id=0, has_side_effects=True, vmem_limit_bytes=60 * 1024 * 1024
        ),
    )(
        atom_counts,
        edge_counts,
        jnp.swapaxes(edge_feats, 1, 2),
        edge_source,
        edge_target,
        atom_states.reshape(rows_all, width),
        targets,
        label_mask,
        edge_input,
        edge_output,
        gated_weights,
        memory_weights,
        readout_hidden,
        finals[0],
        bias_olds[0],
    )
    olds = [edge_input, edge_input_first, edge_input_second, edge_output, edge_output_first, edge_output_second]
    olds += [gated_weights, gated_first, gated_second, memory_weights, memory_first, memory_second]
    olds += [readout_hidden, readout_hidden_first, readout_hidden_second] + finals + bias_olds
    steps = 8
    columns = plan.edge // steps

    def whole(value):
        return pl.BlockSpec(value.shape, lambda i: (0,) * len(value.shape))

    cut = pl.BlockSpec((width, columns), lambda i: (0, i))
    out_shapes, out_specs = [shape((1,), F32)] * 2, [smem] * 2
    for index in range(7):
        old = olds[3 * index]
        for kind in (F32, F32, F32, BF16):
            out_shapes.append(shape(old.shape, kind))
            out_specs.append(cut if index == 1 else whole(old))
    outs = pl.pallas_call(
        functools.partial(update_kernel, ring, peers, local),
        grid=(steps,),
        out_shape=out_shapes,
        in_specs=[smem, whole(totals), pl.BlockSpec((columns, WIDE), lambda i: (i, 0)), whole(head_sum), whole(rest_sum)]
        + [cut if i // 3 == 1 else whole(old) for i, old in enumerate(olds)],
        out_specs=out_specs,
        compiler_params=pltpu.CompilerParams(vmem_limit_bytes=60 * 1024 * 1024),
    )(totals, totals, edge_sum, head_sum, rest_sum, *olds)
    outs = list(outs)
    outs[0], outs[1] = outs[0].reshape(()), outs[1].reshape(())
    outs[22:26] = [value.T for value in outs[22:26]]
    outs[26:30] = [value.reshape(-1)[:n_bias] for value in outs[26:30]]
    return tuple(outs)


def solution(mesh):
    cut = P(None, "row")
    per_mol = (P("mol", None, None), P("mol", None), P("mol", None), P("mol"), P("mol"), P("mol", None, None))
    per_mol += (P("mol", None), P("mol", None))
    return jax.shard_map(
        shards,
        mesh=mesh,
        in_specs=per_mol + (P(),) * 3 + (cut,) * 3 + (P(),) * 15,
        out_specs=(P(),) * 6 + (cut,) * 4 + (P(),) * 20,
        check_vma=False,
    )
```

```python
import functools

import jax
import jax.numpy as jnp
from jax import lax
from jax.experimental import pallas as pl
from jax.experimental.pallas import tpu as pltpu
from jax.sharding import PartitionSpec as P

LAYERS = 2
ROUNDS = 6
STEP = 10
BETA_ONE = 0.9
BETA_TWO = 0.999
EPSILON = 1e-08
DECAY = 0.01
RATES = (0.25, 0.004, 0.09, 0.05, 0.06, 0.09, 0.2)

MESH = pl.DeviceIdType.MESH
F32 = jnp.float32
BF16 = jnp.bfloat16
GROUP = 8
WIDE = 128


def nn(left, right):
    return lax.dot_general(left, right, (((1,), (0,)), ((), ())), preferred_element_type=F32)


def nt(left, right):
    return lax.dot_general(left, right, (((1,), (1,)), ((), ())), preferred_element_type=F32)


def tn(left, right):
    return lax.dot_general(left, right, (((0,), (0,)), ((), ())), preferred_element_type=F32)


def iota(shape, dim):
    return lax.broadcasted_iota(jnp.int32, shape, dim)


def one_hot(condition):
    return jnp.where(condition, 1.0, 0.0).astype(BF16)


def wide(bias_ref, first, count):
    return bias_ref[pl.ds(first * WIDE, count * WIDE)].reshape(1, count * WIDE)


def round_up(value, unit):
    return -(-value // unit) * unit


class Plan:
    def __init__(self, ring, peers, width, local):
        unit = 16 * peers
        self.edge = local * width
        self.edge_part = self.edge // peers
        self.final_at = 12 * width + 2 * width
        self.head = round_up(-(-(self.final_at + 16) // ring), unit)
        self.head_part = self.head // peers
        self.bias_at = 6 * width
        self.rest_own = round_up(-(-(self.bias_at + 16) // ring), 16)
        self.rest = round_up(self.rest_own, unit)
        self.rest_part = self.rest // peers


def step_kernel(
    ring,
    peers,
    atom_counts,
    edge_counts,
    feats,
    source,
    target,
    states,
    targets,
    labels,
    edge_in,
    final_w,
    bias,
    edge_far,
    gated_far,
    memory_far,
    hidden_far,
    edge_sum,
    head_sum,
    rest_sum,
    totals,
    edge_low,
    pairs,
    pair_cols,
    sent,
    turned,
    slope,
    pair_grad,
    lows,
    turned_lows,
    gathered,
    gates,
    state,
    state_grad,
    gate_grad,
    pulled,
    memory_low,
    padded,
    parcels,
    reduce_send,
    reduce_recv,
    grad_gated,
    grad_bias,
    totals_all,
    edge_part,
    edge_recv,
    edge_all,
    head_part,
    head_recv,
    head_all,
    rest_full,
    rest_part,
    rest_recv,
    rest_all,
    send_sem,
    recv_sem,
    far_send,
    far_recv,
    gt,
    edge_out,
    gated,
    memory,
    hidden_w,
    fetch_sem,
    store_sem,
    near_recv,
    near_sum,
    first_row,
    first_mol,
):
    mols, features, edges = feats.shape
    rows_all, width = states.shape
    atoms = rows_all // mols
    local = width // ring
    groups = mols // GROUP
    span = GROUP * atoms
    half = GROUP * local
    block = rows_all // ring
    n_targets = targets.shape[1]
    me = lax.axis_index("row")
    place = lax.axis_index("mol")
    plan = Plan(ring, peers, width, local)
    started = []
    fetches = [
        pltpu.make_async_copy(far, near, fetch_sem.at[i])
        for i, (far, near) in enumerate(
            ((edge_far, edge_out), (gated_far, gated), (memory_far, memory), (hidden_far, hidden_w))
        )
    ]
    for copy in fetches:
        copy.start()

    def rows16(start, count):
        return pl.ds(pl.multiple_of(start, 16), count)

    def far_copy(stage, index, peer, source_ref, target_ref):
        copy = pltpu.make_async_remote_copy(
            src_ref=source_ref,
            dst_ref=target_ref,
            send_sem=far_send.at[stage, index],
            recv_sem=far_recv.at[stage, index],
            device_id={"mol": peer},
            device_id_type=MESH,
        )
        copy.start()
        started.append(copy)
        return copy

    def row_copy(stage, k, source_ref, target_ref):
        copy = pltpu.make_async_remote_copy(
            src_ref=source_ref,
            dst_ref=target_ref,
            send_sem=send_sem.at[stage, k - 1],
            recv_sem=recv_sem.at[stage, k - 1],
            device_id={"row": lax.rem(me + k, ring)},
            device_id_type=MESH,
        )
        copy.start()
        started.append(copy)
        return copy

    barrier = pltpu.get_barrier_semaphore()
    for k in range(1, ring):
        pl.semaphore_signal(barrier, inc=1, device_id={"row": lax.rem(me + k, ring)}, device_id_type=MESH)
    for k in range(1, peers):
        pl.semaphore_signal(barrier, inc=1, device_id={"mol": lax.rem(place + k, peers)}, device_id_type=MESH)

    low_in = edge_in[...].astype(BF16)

    lane_edge = iota((1, edges), 1)
    row_index = iota((256, edges), 0)
    for m in range(mols):
        pairs[m : m + 1, :] = jnp.where(
            lane_edge < edge_counts[m], source[m : m + 1, :] * atoms + target[m : m + 1, :], -1
        )
    pair_cols[...] = pairs[...].astype(F32).T

    bias_first = wide(bias, 0, 1)

    def edge_network(m, carry):
        before = tn(feats[m], low_in) + bias_first
        squash = jax.nn.sigmoid(before)
        act = before * squash
        slope[m] = squash + act * (1.0 - squash)
        act = act.astype(BF16)
        pair = pairs[pl.ds(m, 1), :]
        rows = pl.ds(pl.multiple_of(m * atoms, atoms), atoms)
        for part in range(atoms * atoms // 256):
            sums = nn(one_hot(row_index + part * 256 == pair), act).astype(BF16)
            for j in range(256 // atoms):
                a = part * (256 // atoms) + j
                sent[rows, a * width : (a + 1) * width] = sums[j * atoms : (j + 1) * atoms]
        return carry

    lax.fori_loop(0, mols, edge_network, 0, unroll=4)

    order = one_hot(
        (iota((span, span), 1) // atoms == iota((span, span), 0) % GROUP)
        & (iota((span, span), 1) % atoms == iota((span, span), 0) // GROUP)
    )
    order_back = one_hot(
        (iota((span, span), 0) // atoms == iota((span, span), 1) % GROUP)
        & (iota((span, span), 0) % atoms == iota((span, span), 1) // GROUP)
    )
    same_mol = iota((span, half), 0) // atoms == iota((span, half), 1) % GROUP
    same_mol_t = iota((half, span), 0) % GROUP == iota((half, span), 1) // atoms

    def message(layer):
        for g in range(groups):
            lows[layer, g * span : (g + 1) * span, :] = nn(
                order, state_low(layer, g)
            ).astype(BF16)
        low_p = lows[layer]
        turned_lows[:, layer * rows_all : (layer + 1) * rows_all] = low_p.astype(F32).T.astype(BF16)

        def rows_pair(rp, carry):
            t = nt(low_p, edge_low[pl.ds(pl.multiple_of(rp * 2 * width, 2 * width), 2 * width), :])
            for g in range(groups):
                base = (g * LAYERS + layer) * half
                where = pl.ds(pl.multiple_of(base + rp * 16, 16), 16)
                for a in range(atoms):
                    at = g * span + a * GROUP
                    tile = jnp.concatenate([t[at : at + GROUP, :width], t[at : at + GROUP, width:]], axis=0)
                    turned[where, a * width : (a + 1) * width] = tile.astype(BF16)
            return carry

        lax.fori_loop(0, local // 2, rows_pair, 0, unroll=8)
        packed = jnp.zeros((block, WIDE), F32)
        for g in range(groups):
            base = (g * LAYERS + layer) * half
            u = nt(sent[g * span : (g + 1) * span, :], turned[base : base + half, :])
            u = jnp.where(same_mol, u, 0.0).astype(BF16)
            for j in range(span // block):
                slot = g * (span // block) + j
                pick = one_hot(iota((half, WIDE), 1) == slot * local + iota((half, WIDE), 0) // GROUP)
                packed = packed + nn(u[j * block : (j + 1) * block], pick)
        return packed.astype(BF16)

    def state_low(layer, g):
        rows = slice(g * span, (g + 1) * span)
        if layer == 0:
            return states[rows, :]
        return state[layer - 1, rows, :].astype(BF16)

    def exchange(stage):
        return [row_copy(stage, k, parcels.at[stage, me], parcels.at[stage, me]) for k in range(1, ring)]

    for copy in fetches:
        copy.wait()
    memory_low[...] = memory[...].astype(BF16)
    for r in range(local):
        edge_low[r * width : (r + 1) * width, :] = edge_out[:, r * width : (r + 1) * width].astype(BF16)
    gated_low = [gated[i].astype(BF16) for i in range(2)]
    bias_in = wide(bias, 1, 3)
    bias_hid = wide(bias, 4, 3)
    for layer in range(LAYERS):
        parcels[layer, me] = message(layer)
        if layer == 0:
            pl.semaphore_wait(barrier, ring + peers - 2)
        for copy in exchange(layer):
            copy.wait_recv()
        joined = jnp.concatenate([parcels[layer, q] for q in range(ring)], axis=1)
        for j in range(ring):
            line, column = iota((ring * WIDE, width), 0), iota((ring * WIDE, width), 1)
            pick = one_hot(
                (line % WIDE // local == j) & (line // WIDE == column // local) & (line % local == column % local)
            )
            rows = slice(j * block, (j + 1) * block)
            got = nn(joined, pick).astype(BF16)
            gathered[layer, rows, :] = got
            if layer == 0:
                low = states[rows, :]
                old = low.astype(F32)
            else:
                old = state[layer - 1, rows, :]
                low = old.astype(BF16)
            gate_in = nn(got, gated_low[0]) + bias_in
            gate_hid = nn(low, gated_low[1]) + bias_hid
            reset = jax.nn.sigmoid(gate_in[:, :width] + gate_hid[:, :width])
            update = jax.nn.sigmoid(gate_in[:, width : 2 * width] + gate_hid[:, width : 2 * width])
            third = gate_hid[:, 2 * width :]
            candidate = jnp.tanh(gate_in[:, 2 * width :] + reset * third)
            gates[layer, 0, rows, :] = reset
            gates[layer, 1, rows, :] = update
            gates[layer, 2, rows, :] = candidate
            gates[layer, 3, rows, :] = third
            state[layer, rows, :] = (1.0 - update) * candidate + update * old

    atom_low = state[LAYERS - 1].astype(BF16)
    counts = jnp.zeros((mols, 1), jnp.int32)
    for m in range(mols):
        counts = jnp.where(iota((mols, 1), 0) == m, atom_counts[m], counts)
    lane = iota((mols, rows_all), 1)
    own = (lane // atoms == iota((mols, rows_all), 0)) & (lane % atoms < counts)
    bias_memory = wide(bias, 7, 4)
    zero = jnp.zeros((mols, width), F32)
    cell, mem_low, read_low = zero, zero.astype(BF16), zero.astype(BF16)
    kept = []
    for turn in range(ROUNDS):
        join = jnp.concatenate([mem_low, read_low, mem_low], axis=1)
        z = jnp.broadcast_to(bias_memory, (mols, 4 * width))
        if turn > 0:
            z = nn(join, memory_low[...]) + z
        i = jax.nn.sigmoid(z[:, :width])
        f = jax.nn.sigmoid(z[:, width : 2 * width])
        c = jnp.tanh(z[:, 2 * width : 3 * width])
        o = jax.nn.sigmoid(z[:, 3 * width :])
        before_cell = cell
        cell = f * cell + i * c
        squashed = jnp.tanh(cell)
        mem_low = (o * squashed).astype(BF16)
        scores = jnp.where(own, nt(mem_low, atom_low), -1000000000.0)
        weights = jnp.exp(scores - jnp.max(scores, axis=1, keepdims=True))
        inverse = 1.0 / jnp.sum(weights, axis=1, keepdims=True)
        read_low = (nn(weights.astype(BF16), atom_low) * inverse).astype(BF16)
        weights = weights * inverse
        weights_low = weights.astype(BF16)
        kept.append((join, i, f, c, o, before_cell, squashed, mem_low, weights, weights_low))
    join = jnp.concatenate([mem_low, read_low], axis=1)
    hidden_low = hidden_w[...].astype(BF16)
    padded[...] = jnp.zeros_like(padded)
    padded[0:n_targets, :] = final_w[...]
    padded[16:17, 0:n_targets] = bias[pl.ds(12 * WIDE, n_targets)].reshape(1, n_targets)
    bias_final = padded[16:17, :]
    final_low = jnp.where(iota((width, WIDE), 0) < n_targets, padded[0:width, :], 0.0).astype(BF16)
    before = nn(join, hidden_low) + wide(bias, 11, 1)
    squash = jax.nn.sigmoid(before)
    inner = before * squash
    inner_low = inner.astype(BF16)
    padded[width : width + mols, 0:n_targets] = targets[...]
    padded[width + mols : width + 2 * mols, 0:n_targets] = labels[...].astype(F32)
    label = padded[width + mols : width + 2 * mols, :]
    gap = nt(inner_low, final_low) + bias_final - padded[width : width + mols, :]
    loss = jnp.sum(label * gap * gap)
    present = jnp.sum(label)
    spot = iota((8, WIDE), 1)
    totals_all[place] = jnp.where(spot == 0, loss, jnp.where(spot == 1, present, 0.0))
    total_copies = [
        far_copy(0, k - 1, lax.rem(place + k, peers), totals_all.at[place], totals_all.at[place])
        for k in range(1, peers)
    ]
    d_pred = 2.0 * label * gap
    d_pred_low = d_pred.astype(BF16)
    head_part[plan.final_at : plan.final_at + 16, :] = tn(d_pred_low, inner_low)[0:16].astype(BF16)
    d_before = nn(d_pred_low, final_low) * (squash + inner * (1.0 - squash))
    d_before_low = d_before.astype(BF16)
    head_part[12 * width : 14 * width, :] = tn(join, d_before_low).astype(BF16)
    grad_bias[...] = jnp.zeros_like(grad_bias)
    grad_bias[11:12, :] = jnp.sum(d_before, axis=0, keepdims=True)
    grad_bias[12:13, :] = jnp.sum(d_pred, axis=0, keepdims=True)
    d_join = nt(d_before_low, hidden_low)
    d_mem, d_read = d_join[:, :width], d_join[:, width:]
    d_cell = zero
    d_bias = jnp.zeros((1, 4 * width), F32)
    lefts, rights, joins, d_gates = [], [], [], []
    for turn in reversed(range(ROUNDS)):
        join, i, f, c, o, before_cell, squashed, mem_low, weights, weights_low = kept[turn]
        d_read_low = d_read.astype(BF16)
        d_weights = nt(d_read_low, atom_low)
        d_scores = weights * (d_weights - jnp.sum(weights * d_weights, axis=1, keepdims=True))
        d_scores_low = d_scores.astype(BF16)
        d_mem = d_mem + nn(d_scores_low, atom_low)
        lefts += [weights_low, d_scores_low]
        rights += [d_read_low, mem_low]
        d_out = d_mem * squashed
        d_cell = d_cell + d_mem * o * (1.0 - squashed * squashed)
        d_z = jnp.concatenate(
            [
                d_cell * c * i * (1.0 - i),
                d_cell * before_cell * f * (1.0 - f),
                d_cell * i * (1.0 - c * c),
                d_out * o * (1.0 - o),
            ],
            axis=1,
        )
        d_cell = d_cell * f
        d_bias = d_bias + jnp.sum(d_z, axis=0, keepdims=True)
        d_z_low = d_z.astype(BF16)
        if turn > 0:
            joins.append(join)
            d_gates.append(d_z_low)
            d_join = nt(d_z_low, memory_low[...])
            d_mem = d_join[:, :width] + d_join[:, 2 * width :]
            d_read = d_join[:, width : 2 * width]
    grad_memory = tn(jnp.concatenate(joins, axis=0), jnp.concatenate(d_gates, axis=0)).astype(BF16)
    for i in range(4):
        head_part[i * 3 * width : (i + 1) * 3 * width, :] = grad_memory[:, i * width : (i + 1) * width]
    used = plan.final_at + 16
    head_part[used:, :] = jnp.zeros((ring * plan.head - used, WIDE), BF16)
    head_copies = []
    for k in range(1, peers):
        peer = lax.rem(place + k, peers)
        rows = rows16(me * plan.head + peer * plan.head_part, plan.head_part)
        head_copies.append(far_copy(1, k - 1, peer, head_part.at[rows, :], head_recv.at[k - 1]))
    for i in range(4):
        grad_bias[7 + i : 8 + i, :] = d_bias[:, i * width : (i + 1) * width]
    state_grad[...] = tn(jnp.concatenate(lefts, axis=0), jnp.concatenate(rights, axis=0))

    def gated_back(layer):
        bias_parts = [jnp.zeros((1, 3 * width), F32) for _ in range(2)]
        for j in range(ring):
            rows = slice(j * block, (j + 1) * block)
            reset, update = gates[layer, 0, rows, :], gates[layer, 1, rows, :]
            candidate, third = gates[layer, 2, rows, :], gates[layer, 3, rows, :]
            old = states[rows, :].astype(F32) if layer == 0 else state[layer - 1, rows, :]
            grad = state_grad[rows, :]
            d_candidate = grad * (1.0 - update) * (1.0 - candidate * candidate)
            d_update = grad * (old - candidate) * update * (1.0 - update)
            d_reset = d_candidate * third * reset * (1.0 - reset)
            d_in = jnp.concatenate([d_reset, d_update, d_candidate], axis=1)
            d_hid = jnp.concatenate([d_reset, d_update, d_candidate * reset], axis=1)
            bias_parts[0] = bias_parts[0] + jnp.sum(d_in, axis=0, keepdims=True)
            bias_parts[1] = bias_parts[1] + jnp.sum(d_hid, axis=0, keepdims=True)
            d_in_low, d_hid_low = d_in.astype(BF16), d_hid.astype(BF16)
            gate_grad[layer, 0, rows, :] = d_in_low
            gate_grad[layer, 1, rows, :] = d_hid_low
            pulled[layer, rows, :] = nt(d_in_low, gated_low[0]).astype(BF16)
            if layer > 0:
                state_grad[rows, :] = grad * update + nt(d_hid_low, gated_low[1])
        for s in range(2):
            for i in range(3):
                at = 1 + 3 * s + i
                grad_bias[at : at + 1, :] += bias_parts[s][:, i * width : (i + 1) * width]

    def gated_weights_back(layer):
        low = states[...] if layer == 0 else state[layer - 1].astype(BF16)
        d_first = tn(gathered[layer], gate_grad[layer, 0])
        d_second = tn(low, gate_grad[layer, 1])
        if layer == LAYERS - 1:
            grad_gated[0], grad_gated[1] = d_first, d_second
        else:
            grad_gated[0] += d_first
            grad_gated[1] += d_second

    pick_t = one_hot(iota((half, width), 1) == me * local + iota((half, width), 0) // GROUP)
    pick_n = one_hot(iota((width, half), 0) == me * local + iota((width, half), 1) // GROUP)

    def message_back(layer):
        for g in range(groups):
            wide_grad = jnp.where(same_mol_t, nt(pick_t, pulled[layer, g * span : (g + 1) * span, :]), 0.0).astype(BF16)

            def atoms_pair(ap, carry, g=g, wide_grad=wide_grad):
                columns = pl.ds(pl.multiple_of(ap * 2 * width, 2 * width), 2 * width)
                x = nn(wide_grad, sent[g * span : (g + 1) * span, columns])
                where = pl.ds(pl.multiple_of(layer * rows_all + g * span + ap * 16, 16), 16)
                for r in range(local):
                    at = r * GROUP
                    tile = jnp.concatenate([x[at : at + GROUP, :width], x[at : at + GROUP, width:]], axis=0)
                    gt[where, r * width : (r + 1) * width] = tile.astype(BF16)
                return carry

            lax.fori_loop(0, atoms // 2, atoms_pair, 0, unroll=8)

    rest_copies = []
    for layer in reversed(range(LAYERS)):
        gated_back(layer)
        if layer == 0:
            gated_weights_back(layer)
            for s in range(2):
                for i in range(3):
                    at = (s * 3 + i) * width
                    rest_full[at : at + width, :] = grad_gated[s, :, i * width : (i + 1) * width].astype(BF16)
            rest_full[plan.bias_at : plan.bias_at + 16, :] = grad_bias[...].astype(BF16)
            used = plan.bias_at + 16
            if ring * plan.rest_own > used:
                rest_full[used:, :] = jnp.zeros((ring * plan.rest_own - used, WIDE), BF16)
            rest_part[0 : plan.rest_own, :] = rest_full[rows16(me * plan.rest_own, plan.rest_own), :]
            if plan.rest > plan.rest_own:
                rest_part[plan.rest_own :, :] = jnp.zeros((plan.rest - plan.rest_own, WIDE), BF16)
            for k in range(1, peers):
                peer = lax.rem(place + k, peers)
                rows = rows16(peer * plan.rest_part, plan.rest_part)
                rest_copies.append(far_copy(4, k - 1, peer, rest_part.at[rows, :], rest_recv.at[k - 1]))
        message_back(layer)
        if layer > 0:
            back = nn(gt[layer * rows_all : (layer + 1) * rows_all, :], edge_low[...]).astype(BF16)
            for g in range(groups):
                reduce_send[g * span : (g + 1) * span, :] = nn(order_back, back[g * span : (g + 1) * span]).astype(BF16)
            copies = []
            for k in range(1, ring):
                rows = rows16(lax.rem(me + k, ring) * block, block)
                copies.append(row_copy(LAYERS + 1, k, reduce_send.at[rows, :], reduce_recv.at[k - 1]))
            gated_weights_back(layer)
            for copy in copies:
                copy.wait_recv()
            total = reduce_send[pl.ds(pl.multiple_of(me * block, block), block), :].astype(F32)
            for k in range(ring - 1):
                total = total + reduce_recv[k].astype(F32)
            parcels[LAYERS, me] = total.astype(BF16)
            for copy in exchange(LAYERS):
                copy.wait_recv()
            for j in range(ring):
                rows = slice(j * block, (j + 1) * block)
                state_grad[rows, :] += parcels[LAYERS, j].astype(F32)

    for copy in head_copies:
        copy.wait_recv()
    mine = rows16(me * plan.head + place * plan.head_part, plan.head_part)
    total = head_part[mine, :].astype(F32)
    for k in range(peers - 1):
        total = total + head_recv[k].astype(F32)
    head_all[mine, :] = total.astype(BF16)
    head_copies[:] = [
        far_copy(2, k - 1, lax.rem(place + k, peers), head_all.at[mine, :], head_all.at[mine, :])
        for k in range(1, peers)
    ]

    lines = peers // 2
    line, side = lax.div(place, 2), lax.rem(place, 2)
    neighbour = line * 2 + 1 - side
    part = plan.edge_part
    stack = max(1, 2 * width // (2 * part))
    blocks = lines // stack
    home, seat = lax.div(line, stack), lax.rem(line, stack)

    def out_weights(start):
        columns = pl.ds(pl.multiple_of(start, 2 * width), 2 * width)
        edge_part[columns, :] = nn(turned_lows[...], gt[:, columns]).T.astype(BF16)

    def lines_of(j):
        return [lax.rem(home + j, blocks) * stack + lax.rem(seat + i, stack) for i in range(stack)]

    def scatter_near(j):
        copies = []
        if stack > 1:
            out_weights(lax.rem(home + j, blocks) * stack * 2 * part)
        for i, other in enumerate(lines_of(j)):
            if stack == 1:
                for step in range(part // (2 * width)):
                    out_weights(other * 2 * part + (1 - side) * part + step * 2 * width)
            rows = rows16(other * 2 * part + (1 - side) * part, part)
            copies.append(far_copy(7, j * stack + i, neighbour, edge_part.at[rows, :], near_recv.at[rows16(other * part, part), :]))
            if stack == 1:
                for step in range(part // (2 * width)):
                    out_weights(other * 2 * part + side * part + step * 2 * width)
        return copies

    edge_copies = []

    def scatter_far(j, copies):
        for i, other in enumerate(lines_of(j)):
            copies[i].wait_recv()
            rows = rows16(other * part, part)
            total = edge_part[rows16(other * 2 * part + side * part, part), :].astype(F32) + near_recv[rows, :].astype(F32)
            near_sum[rows, :] = total.astype(BF16)
            if j > 0 or i > 0:
                k = j if stack == 1 else lax.rem(other - line + lines, lines)
                edge_copies.append(far_copy(3, k - 1, other * 2 + side, near_sum.at[rows, :], edge_recv.at[k - 1]))

    order_of = [*range(1, blocks), 0]
    waiting = None
    for j in order_of:
        copies = scatter_near(j)
        if waiting is not None:
            scatter_far(*waiting)
        waiting = (j, copies)

    def pair_grads(g):
        wide_grad = jnp.concatenate(
            [
                jnp.where(same_mol, nn(pulled[layer, g * span : (g + 1) * span, :], pick_n), 0.0).astype(BF16)
                for layer in range(LAYERS)
            ],
            axis=1,
        )

        def pair_back(ap, carry):
            columns = pl.ds(pl.multiple_of(ap * 2 * width, 2 * width), 2 * width)
            x = nn(wide_grad, turned[g * LAYERS * half : (g + 1) * LAYERS * half, columns]).astype(BF16)
            for s in range(2):
                where = pl.ds(pl.multiple_of((ap * 2 + s) * atoms, atoms), atoms)
                for m in range(GROUP):
                    pair_grad[g * GROUP + m, where, :] = x[m * atoms : (m + 1) * atoms, s * width : (s + 1) * width]
            return carry

        lax.fori_loop(0, atoms // 2, pair_back, 0, unroll=8)

    for g in range(groups - 1):
        pair_grads(g)
    scatter_far(*waiting)
    for copy in rest_copies:
        copy.wait_recv()
    mine = rows16(place * plan.rest_part, plan.rest_part)
    total = rest_part[mine, :].astype(F32)
    for k in range(peers - 1):
        total = total + rest_recv[k].astype(F32)
    rest_all[me, mine, :] = total.astype(BF16)
    rest_copies = [
        far_copy(6, k - 1, lax.rem(place + k, peers), rest_all.at[me, mine, :], rest_all.at[me, mine, :])
        for k in range(1, peers)
    ]
    for copy in head_copies:
        copy.wait_recv()
    rows = rows16(me * plan.head, plan.head)
    head_rows = [row_copy(LAYERS + 2, k, head_all.at[rows, :], head_all.at[rows, :]) for k in range(1, ring)]
    pair_grads(groups - 1)

    for copy in edge_copies:
        copy.wait_recv()
    pieces = 2 if part >= WIDE else 1
    size = part // pieces
    across, beside = {}, {}
    for p in range(pieces):
        own = rows16(line * part + p * size, size)
        mine = rows16(place * part + p * size, size)
        total = near_sum[own, :].astype(F32)
        for k in range(lines - 1):
            total = total + edge_recv[k, p * size : (p + 1) * size, :].astype(F32)
        edge_all[mine, :] = total.astype(BF16)
        for k in range(1, lines):
            peer = lax.rem(line + k, lines) * 2 + side
            across[p, k] = far_copy(5, p * peers + k, peer, edge_all.at[mine, :], edge_all.at[mine, :])
        beside[p, 0] = far_copy(5, p * peers, neighbour, edge_all.at[mine, :], edge_all.at[mine, :])

    def onward(p):
        for k in range(1, lines):
            across[p, k].wait_recv()
            rows = rows16((lax.rem(line - k + lines, lines) * 2 + side) * part + p * size, size)
            beside[p, k] = far_copy(5, p * peers + lines + k, neighbour, edge_all.at[rows, :], edge_all.at[rows, :])

    lane_pair = iota((edges, atoms * atoms), 1).astype(F32)

    def edge_back(m):
        d_act = nn(one_hot(lane_pair == pair_cols[:, m : m + 1]), pair_grad[m])
        d_first = d_act * slope[m]
        return nn(feats[m], d_first.astype(BF16)), jnp.sum(d_first, axis=0, keepdims=True)

    total_in, total_bias = edge_back(0)
    for m in range(1, mols):
        if m == mols // 2:
            for copy in rest_copies:
                copy.wait_recv()
            rest_rows = [row_copy(LAYERS + 3, k, rest_all.at[me], rest_all.at[me]) for k in range(1, ring)]
        more_in, more_bias = edge_back(m)
        total_in, total_bias = total_in + more_in, total_bias + more_bias
    first_row[me, 0:features, :] = total_in
    first_row[me, features : features + 8, :] = jnp.broadcast_to(total_bias, (8, width))
    first_copies = [row_copy(LAYERS + 4, k, first_row.at[me], first_row.at[me]) for k in range(1, ring)]
    onward(0)
    for copy in first_copies:
        copy.wait_recv()
    total = first_row[0]
    for q in range(1, ring):
        total = total + first_row[q]
    first_mol[place] = total
    first_copies = [
        far_copy(8, k - 1, lax.rem(place + k, peers), first_mol.at[place], first_mol.at[place])
        for k in range(1, peers)
    ]
    for p in range(1, pieces):
        onward(p)

    stores = []

    def store(source_ref, target_ref):
        copy = pltpu.make_async_copy(source_ref, target_ref, store_sem.at[len(stores)])
        copy.start()
        stores.append(copy)

    for copy in head_rows:
        copy.wait_recv()
    store(head_all, head_sum)
    for copy in rest_rows:
        copy.wait_recv()
    store(rest_all, rest_sum)
    for copy in total_copies + first_copies:
        copy.wait_recv()
    total, total_first = totals_all[0], first_mol[0]
    for k in range(1, peers):
        total = total + totals_all[k]
        total_first = total_first + first_mol[k]
    totals[0:8, :] = total
    totals[8:, :] = total_first
    for copy in beside.values():
        copy.wait_recv()
    store(edge_all, edge_sum)
    for copy in started:
        copy.wait_send()
    for copy in stores:
        copy.wait()


def adamw(weight, first, second, grad, rate):
    first_new = BETA_ONE * first + (1.0 - BETA_ONE) * grad
    second_new = BETA_TWO * second + (1.0 - BETA_TWO) * grad * grad
    scaled = jnp.sqrt(second_new * (1.0 / (1.0 - BETA_TWO**STEP))) + EPSILON
    weight_new = (1.0 - rate * DECAY) * weight - (rate / (1.0 - BETA_ONE**STEP)) * first_new / scaled
    return (weight_new, first_new, second_new, weight_new.astype(BF16))


PIECES = 4


def update_kernel(ring, peers, local, counted, totals, edge_far, head_far, rest_far, *refs):
    fars, refs = refs[:21], refs[21:]
    (loss_out, count_out), refs = refs[:2], refs[2:]
    outs, refs = refs[:28], refs[28:]
    (edge_sum, head_sum, rest_sum), refs = refs[:3], refs[3:]
    olds, refs = refs[:21], refs[21:]
    news, (fetch_sem, store_sem) = refs[:28], refs[28:]
    features, width = olds[0].shape
    n_bias = olds[18].shape[0]
    plan = Plan(ring, peers, width, local)
    every = slice(None)
    columns = plan.edge // PIECES
    cuts = [(every, pl.ds(i * columns, columns)) for i in range(PIECES)]
    count = [0, 0]

    def copies_of(sides, sem, which):
        made = []
        for source_ref, target_ref in sides:
            made.append(pltpu.make_async_copy(source_ref, target_ref, sem.at[count[which]]))
            made[-1].start()
            count[which] += 1
        return made

    def fetch(index, cut=None):
        where = range(3 * index, 3 * index + 3)
        return copies_of([(fars[i], olds[i]) if cut is None else (fars[i].at[cut], olds[i].at[cut]) for i in where], fetch_sem, 0)

    def store(index, cut=None):
        where = range(4 * index, 4 * index + 4)
        return copies_of([(news[i], outs[i]) if cut is None else (news[i].at[cut], outs[i].at[cut]) for i in where], store_sem, 1)

    edge_ready = copies_of([(edge_far, edge_sum)], fetch_sem, 0)
    cut_ready = [fetch(1, cut) for cut in cuts]
    head_ready = copies_of([(head_far, head_sum)], fetch_sem, 0)
    ready = {index: fetch(index) for index in (3, 4, 5)}
    rest_ready = copies_of([(rest_far, rest_sum)], fetch_sem, 0)
    ready.update({index: fetch(index) for index in (2, 0, 6)})
    loss_out[0] = counted[0, 0]
    count_out[0] = counted[0, 1]
    inverse = (1.0 / totals[0:1, :])[0:1, 1:2]

    def update(index, view, grad):
        parts = [ref[view] for ref in olds[3 * index : 3 * index + 3]]
        for ref, value in zip(news[4 * index : 4 * index + 4], adamw(*parts, grad, RATES[index])):
            ref[view] = value

    def wait(copies):
        for copy in copies:
            copy.wait()

    stored = []
    wait(edge_ready)
    for p in range(PIECES):
        wait(cut_ready[p])
        for i in range(p * columns // width, (p + 1) * columns // width):
            grad = edge_sum[i * width : (i + 1) * width, :].astype(F32) * inverse
            update(1, (every, slice(i * width, (i + 1) * width)), grad)
        stored += store(1, cuts[p])
    wait(head_ready + ready[3])
    for i in range(4):
        grad = head_sum[i * 3 * width : (i + 1) * 3 * width, :].astype(F32) * inverse
        update(3, (every, slice(i * width, (i + 1) * width)), grad)
    stored += store(3)
    wait(rest_ready + ready[2])
    for s in range(2):
        for i in range(3):
            at, end = (s * 3 + i) * width, (s * 3 + i + 1) * width
            while at < end:
                q, low = divmod(at, plan.rest_own)
                rows = min(end - at, plan.rest_own - low)
                first = at - (s * 3 + i) * width
                grad = rest_sum[q, low : low + rows, :].astype(F32) * inverse
                update(2, (s, slice(first, first + rows), slice(i * width, (i + 1) * width)), grad)
                at += rows
    stored += store(2)
    wait(ready[4])
    update(4, (every, every), head_sum[12 * width : 14 * width, :].astype(F32) * inverse)
    stored += store(4)
    wait(ready[5])
    n_targets = olds[15].shape[0]
    update(5, (every, every), (head_sum[plan.final_at : plan.final_at + 16, :].astype(F32) * inverse)[0:n_targets])
    stored += store(5)
    own = totals[8:, :] * inverse
    wait(ready[0])
    update(0, (every, every), own[0:features])
    stored += store(0)
    q, low = divmod(plan.bias_at, plan.rest_own)
    biases = rest_sum[q, low : low + 16, :].astype(F32) * inverse
    wait(ready[6])
    for i in range(-(-n_bias // WIDE)):
        size = min(WIDE, n_bias - i * WIDE)
        grad = (own[features : features + 1] if i == 0 else biases[i : i + 1])[:, 0:size]
        update(6, pl.ds(i * WIDE, size), grad.reshape(size))
    stored += store(6)
    wait(stored)


def shards(
    edge_feats,
    edge_source,
    edge_target,
    atom_counts,
    edge_counts,
    atom_states,
    targets,
    label_mask,
    edge_input,
    edge_input_first,
    edge_input_second,
    edge_output,
    edge_output_first,
    edge_output_second,
    gated_weights,
    gated_first,
    gated_second,
    memory_weights,
    memory_first,
    memory_second,
    readout_hidden,
    readout_hidden_first,
    readout_hidden_second,
    readout_final,
    readout_final_first,
    readout_final_second,
    bias_vector,
    bias_first,
    bias_second,
):
    mols, edges, features = edge_feats.shape
    atoms, width = atom_states.shape[1:]
    ring = lax.axis_size("row")
    local = width // ring
    rows_all = mols * atoms
    block = rows_all // ring
    peers = lax.axis_size("mol")
    plan = Plan(ring, peers, width, local)

    finals = [value.T for value in (readout_final, readout_final_first, readout_final_second)]
    vmem = pl.BlockSpec(memory_space=pltpu.VMEM)
    smem = pl.BlockSpec(memory_space=pltpu.SMEM)
    far = pl.BlockSpec(memory_space=pl.ANY)
    shape = jax.ShapeDtypeStruct
    edge_sum, head_sum, rest_sum, totals = pl.pallas_call(
        functools.partial(step_kernel, ring, peers),
        out_shape=[
            shape((plan.edge, WIDE), BF16),
            shape((ring * plan.head, WIDE), BF16),
            shape((ring, plan.rest, WIDE), BF16),
            shape((8 + features + 8, WIDE), F32),
        ],
        in_specs=[smem, smem] + [vmem] * 9 + [far] * 4,
        out_specs=[far] * 3 + [vmem],
        scratch_shapes=[
            pltpu.VMEM((local * width, width), BF16),
            pltpu.VMEM((mols, edges), jnp.int32),
            pltpu.VMEM((edges, mols), F32),
            pltpu.VMEM((rows_all, atoms * width), BF16),
            pltpu.VMEM((mols // GROUP * LAYERS * GROUP * local, atoms * width), BF16),
            pltpu.VMEM((mols, edges, width), F32),
            pltpu.VMEM((mols, atoms * atoms, width), BF16),
            pltpu.VMEM((LAYERS, rows_all, width), BF16),
            pltpu.VMEM((width, LAYERS * rows_all), BF16),
            pltpu.VMEM((LAYERS, rows_all, width), BF16),
            pltpu.VMEM((LAYERS, 4, rows_all, width), F32),
            pltpu.VMEM((LAYERS, rows_all, width), F32),
            pltpu.VMEM((rows_all, width), F32),
            pltpu.VMEM((LAYERS, 2, rows_all, 3 * width), BF16),
            pltpu.VMEM((LAYERS, rows_all, width), BF16),
            pltpu.VMEM((3 * width, 4 * width), BF16),
            pltpu.VMEM((width + 2 * mols, WIDE), F32),
            pltpu.VMEM((LAYERS + 1, ring, block, WIDE), BF16),
            pltpu.VMEM((rows_all, width), BF16),
            pltpu.VMEM((ring - 1, block, width), BF16),
            pltpu.VMEM((2, width, 3 * width), F32),
            pltpu.VMEM((16, WIDE), F32),
            pltpu.VMEM((peers, 8, WIDE), F32),
            pltpu.VMEM((plan.edge, WIDE), BF16),
            pltpu.VMEM((peers // 2 - 1, plan.edge_part, WIDE), BF16),
            pltpu.VMEM((plan.edge, WIDE), BF16),
            pltpu.VMEM((ring * plan.head, WIDE), BF16),
            pltpu.VMEM((peers - 1, plan.head_part, WIDE), BF16),
            pltpu.VMEM((ring * plan.head, WIDE), BF16),
            pltpu.VMEM((ring * plan.rest_own, WIDE), BF16),
            pltpu.VMEM((plan.rest, WIDE), BF16),
            pltpu.VMEM((peers - 1, plan.rest_part, WIDE), BF16),
            pltpu.VMEM((ring, plan.rest, WIDE), BF16),
            pltpu.SemaphoreType.DMA((LAYERS + 5, ring - 1)),
            pltpu.SemaphoreType.DMA((LAYERS + 5, ring - 1)),
            pltpu.SemaphoreType.DMA((9, 2 * peers)),
            pltpu.SemaphoreType.DMA((9, 2 * peers)),
            pltpu.VMEM((LAYERS * rows_all, local * width), BF16),
            pltpu.VMEM(edge_output.shape, F32),
            pltpu.VMEM(gated_weights.shape, F32),
            pltpu.VMEM(memory_weights.shape, F32),
            pltpu.VMEM(readout_hidden.shape, F32),
            pltpu.SemaphoreType.DMA((4,)),
            pltpu.SemaphoreType.DMA((3,)),
            pltpu.VMEM((peers // 2 * plan.edge_part, WIDE), BF16),
            pltpu.VMEM((peers // 2 * plan.edge_part, WIDE), BF16),
            pltpu.VMEM((ring, features + 8, WIDE), F32),
            pltpu.VMEM((peers, features + 8, WIDE), F32),
        ],
        compiler_params=pltpu.CompilerParams(
            collective_id=0, has_side_effects=True, vmem_limit_bytes=60 * 1024 * 1024
        ),
    )(
        atom_counts,
        edge_counts,
        jnp.swapaxes(edge_feats, 1, 2),
        edge_source,
        edge_target,
        atom_states.reshape(rows_all, width),
        targets,
        label_mask,
        edge_input,
        finals[0],
        bias_vector,
        edge_output,
        gated_weights,
        memory_weights,
        readout_hidden,
    )
    olds = [edge_input, edge_input_first, edge_input_second, edge_output, edge_output_first, edge_output_second]
    olds += [gated_weights, gated_first, gated_second, memory_weights, memory_first, memory_second]
    olds += [readout_hidden, readout_hidden_first, readout_hidden_second] + finals
    olds += [bias_vector, bias_first, bias_second]
    news = [shape(olds[3 * index].shape, kind) for index in range(7) for kind in (F32, F32, F32, BF16)]
    sums = [edge_sum, head_sum, rest_sum]
    outs = pl.pallas_call(
        functools.partial(update_kernel, ring, peers, local),
        out_shape=[shape((1,), F32)] * 2 + news,
        in_specs=[smem, vmem] + [far] * 24,
        out_specs=[smem] * 2 + [far] * 28,
        scratch_shapes=[pltpu.VMEM(value.shape, value.dtype) for value in sums + olds + news]
        + [pltpu.SemaphoreType.DMA((3 + 18 + 3 * PIECES,)), pltpu.SemaphoreType.DMA((24 + 4 * PIECES,))],
        compiler_params=pltpu.CompilerParams(vmem_limit_bytes=60 * 1024 * 1024),
    )(totals, totals, *sums, *olds)
    outs = list(outs)
    outs[0], outs[1] = outs[0].reshape(()), outs[1].reshape(())
    outs[22:26] = [value.T for value in outs[22:26]]
    return tuple(outs)


def solution(mesh):
    cut = P(None, "row")
    per_mol = (P("mol", None, None), P("mol", None), P("mol", None), P("mol"), P("mol"), P("mol", None, None))
    per_mol += (P("mol", None), P("mol", None))
    return jax.shard_map(
        shards,
        mesh=mesh,
        in_specs=per_mol + (P(),) * 3 + (cut,) * 3 + (P(),) * 15,
        out_specs=(P(),) * 6 + (cut,) * 4 + (P(),) * 20,
        check_vma=False,
    )
```

```python
import functools

import jax
import jax.numpy as jnp
from jax import lax
from jax.experimental import pallas as pl
from jax.experimental.pallas import tpu as pltpu
from jax.sharding import PartitionSpec as P

LAYERS = 2
ROUNDS = 6
STEP = 10
BETA_ONE = 0.9
BETA_TWO = 0.999
EPSILON = 1e-08
DECAY = 0.01
RATES = (0.25, 0.004, 0.09, 0.05, 0.06, 0.09, 0.2)

MESH = pl.DeviceIdType.MESH
F32 = jnp.float32
BF16 = jnp.bfloat16
GROUP = 8
WIDE = 128


def nn(left, right):
    return lax.dot_general(left, right, (((1,), (0,)), ((), ())), preferred_element_type=F32)


def nt(left, right):
    return lax.dot_general(left, right, (((1,), (1,)), ((), ())), preferred_element_type=F32)


def tn(left, right):
    return lax.dot_general(left, right, (((0,), (0,)), ((), ())), preferred_element_type=F32)


def iota(shape, dim):
    return lax.broadcasted_iota(jnp.int32, shape, dim)


def one_hot(condition):
    return jnp.where(condition, 1.0, 0.0).astype(BF16)


def wide(bias_ref, first, count):
    return bias_ref[pl.ds(first * WIDE, count * WIDE)].reshape(1, count * WIDE)


def round_up(value, unit):
    return -(-value // unit) * unit


class Plan:
    def __init__(self, ring, peers, width, local):
        unit = 16 * peers
        self.edge = local * width
        self.edge_part = self.edge // peers
        self.final_at = 12 * width + 2 * width
        self.head = round_up(-(-(self.final_at + 16) // ring), unit)
        self.head_part = self.head // peers
        self.bias_at = 6 * width
        self.rest_own = round_up(-(-(self.bias_at + 16) // ring), 16)
        self.rest = round_up(self.rest_own, unit)
        self.rest_part = self.rest // peers
        self.pieces = 2 if self.edge_part >= WIDE else 1
        sizes = [peers - 1] * 9
        sizes[3], sizes[5], sizes[7] = peers // 2 - 1, self.pieces * peers, peers // 2
        self.stages = [sum(sizes[:stage]) for stage in range(10)]


def step_kernel(
    ring,
    peers,
    atom_counts,
    edge_counts,
    feats,
    source,
    target,
    states,
    targets,
    labels,
    edge_in,
    final_w,
    bias,
    edge_far,
    gated_far,
    memory_far,
    hidden_far,
    edge_sum,
    head_sum,
    rest_sum,
    totals,
    edge_low,
    pairs,
    pair_cols,
    sent,
    turned,
    slope,
    pair_grad,
    turned_lows,
    gathered,
    gates,
    state,
    state_grad,
    gate_grad,
    pulled,
    memory_low,
    padded,
    parcels,
    reduce_send,
    reduce_recv,
    grad_gated,
    grad_bias,
    totals_all,
    edge_part,
    edge_recv,
    edge_all,
    head_part,
    head_recv,
    head_all,
    rest_full,
    rest_part,
    rest_recv,
    rest_all,
    send_sem,
    recv_sem,
    far_send,
    far_recv,
    gt,
    edge_out,
    gated,
    memory,
    hidden_w,
    fetch_sem,
    store_sem,
    near_recv,
    near_sum,
    first_row,
    first_mol,
    first_grad,
):
    mols, features, edges = feats.shape
    rows_all, width = states.shape
    atoms = rows_all // mols
    local = width // ring
    groups = mols // GROUP
    span = GROUP * atoms
    half = GROUP * local
    block = span // ring
    n_targets = targets.shape[1]
    me = lax.axis_index("row")
    place = lax.axis_index("mol")
    plan = Plan(ring, peers, width, local)
    started = []
    fetches = [
        pltpu.make_async_copy(far, near, fetch_sem.at[i])
        for i, (far, near) in enumerate(
            ((edge_far, edge_out), (gated_far, gated), (memory_far, memory), (hidden_far, hidden_w))
        )
    ]
    for copy in fetches:
        copy.start()

    def rows16(start, count):
        return pl.ds(pl.multiple_of(start, 16), count)

    def far_copy(stage, index, peer, source_ref, target_ref):
        index += plan.stages[stage]
        copy = pltpu.make_async_remote_copy(
            src_ref=source_ref,
            dst_ref=target_ref,
            send_sem=far_send.at[index],
            recv_sem=far_recv.at[index],
            device_id={"mol": peer},
            device_id_type=MESH,
        )
        copy.start()
        started.append(copy)
        return copy

    def row_copy(stage, k, source_ref, target_ref):
        copy = pltpu.make_async_remote_copy(
            src_ref=source_ref,
            dst_ref=target_ref,
            send_sem=send_sem.at[stage, k - 1],
            recv_sem=recv_sem.at[stage, k - 1],
            device_id={"row": lax.rem(me + k, ring)},
            device_id_type=MESH,
        )
        copy.start()
        started.append(copy)
        return copy

    barrier = pltpu.get_barrier_semaphore()
    for k in range(1, ring):
        pl.semaphore_signal(barrier, inc=1, device_id={"row": lax.rem(me + k, ring)}, device_id_type=MESH)
    for k in range(1, peers):
        pl.semaphore_signal(barrier, inc=1, device_id={"mol": lax.rem(place + k, peers)}, device_id_type=MESH)

    low_in = edge_in[...].astype(BF16)

    lane_edge = iota((1, edges), 1)
    row_index = iota((256, edges), 0)
    for m in range(mols):
        pairs[m : m + 1, :] = jnp.where(
            lane_edge < edge_counts[m], source[m : m + 1, :] * atoms + target[m : m + 1, :], -1
        )
    pair_cols[...] = pairs[...].astype(F32).T

    bias_first = wide(bias, 0, 1)

    def edge_network(m, carry):
        before = tn(feats[m], low_in) + bias_first
        squash = jax.nn.sigmoid(before)
        act = before * squash
        slope[m] = squash + act * (1.0 - squash)
        act = act.astype(BF16)
        pair = pairs[pl.ds(m, 1), :]
        rows = pl.ds(pl.multiple_of(m * atoms, atoms), atoms)
        for part in range(atoms * atoms // 256):
            sums = nn(one_hot(row_index + part * 256 == pair), act).astype(BF16)
            for j in range(256 // atoms):
                a = part * (256 // atoms) + j
                sent[rows, a * width : (a + 1) * width] = sums[j * atoms : (j + 1) * atoms]
        return carry

    lax.fori_loop(0, mols, edge_network, 0, unroll=4)

    order = one_hot(
        (iota((span, span), 1) // atoms == iota((span, span), 0) % GROUP)
        & (iota((span, span), 1) % atoms == iota((span, span), 0) // GROUP)
    )
    order_back = one_hot(
        (iota((span, span), 0) // atoms == iota((span, span), 1) % GROUP)
        & (iota((span, span), 0) % atoms == iota((span, span), 1) // GROUP)
    )
    same_mol = iota((span, half), 0) // atoms == iota((span, half), 1) % GROUP
    same_mol_t = iota((half, span), 0) % GROUP == iota((half, span), 1) // atoms

    def state_low(layer, rows):
        if layer == 0:
            return states[rows, :]
        return state[layer - 1, rows, :].astype(BF16)

    def message(layer, g):
        rows = slice(g * span, (g + 1) * span)
        low_p = nn(order, state_low(layer, rows)).astype(BF16)
        at = layer * rows_all + g * span
        turned_lows[:, at : at + span] = low_p.astype(F32).T.astype(BF16)
        base = (g * LAYERS + layer) * half

        def rows_pair(rp, carry):
            t = nt(low_p, edge_low[pl.ds(pl.multiple_of(rp * 2 * width, 2 * width), 2 * width), :])
            where = pl.ds(pl.multiple_of(base + rp * 16, 16), 16)
            for a in range(atoms):
                at = a * GROUP
                tile = jnp.concatenate([t[at : at + GROUP, :width], t[at : at + GROUP, width:]], axis=0)
                turned[where, a * width : (a + 1) * width] = tile.astype(BF16)
            return carry

        lax.fori_loop(0, local // 2, rows_pair, 0, unroll=8)
        u = nt(sent[rows, :], turned[base : base + half, :])
        u = jnp.where(same_mol, u, 0.0).astype(BF16)
        packed = jnp.zeros((block, WIDE), F32)
        for j in range(ring):
            pick = one_hot(iota((half, WIDE), 1) == j * local + iota((half, WIDE), 0) // GROUP)
            packed = packed + nn(u[j * block : (j + 1) * block], pick)
        parcels[layer * groups + g, me] = packed.astype(BF16)

    def exchange(stage):
        return [row_copy(stage, k, parcels.at[stage, me], parcels.at[stage, me]) for k in range(1, ring)]

    def gated_step(layer, g):
        stage = layer * groups + g
        joined = jnp.concatenate([parcels[stage, q] for q in range(ring)], axis=1)
        for j in range(0, ring, 2):
            parts = []
            for i in (j, j + 1):
                row, column = iota((ring * WIDE, width), 0), iota((ring * WIDE, width), 1)
                pick = one_hot(
                    (row % WIDE // local == i) & (row // WIDE == column // local) & (row % local == column % local)
                )
                parts.append(nn(joined, pick))
            rows = slice(g * span + j * block, g * span + (j + 2) * block)
            got = jnp.concatenate(parts, axis=0).astype(BF16)
            gathered[layer, rows, :] = got
            old = states[rows, :].astype(F32) if layer == 0 else state[layer - 1, rows, :]
            gate_in = nn(got, gated_low[0]) + bias_in
            gate_hid = nn(state_low(layer, rows), gated_low[1]) + bias_hid
            reset = jax.nn.sigmoid(gate_in[:, :width] + gate_hid[:, :width])
            update = jax.nn.sigmoid(gate_in[:, width : 2 * width] + gate_hid[:, width : 2 * width])
            third = gate_hid[:, 2 * width :]
            candidate = jnp.tanh(gate_in[:, 2 * width :] + reset * third)
            gates[layer, 0, rows, :] = reset
            gates[layer, 1, rows, :] = update
            gates[layer, 2, rows, :] = candidate
            gates[layer, 3, rows, :] = third
            state[layer, rows, :] = (1.0 - update) * candidate + update * old

    for copy in fetches:
        copy.wait()
    memory_low[...] = memory[...].astype(BF16)
    for r in range(local):
        edge_low[r * width : (r + 1) * width, :] = edge_out[:, r * width : (r + 1) * width].astype(BF16)
    gated_low = [gated[i].astype(BF16) for i in range(2)]
    bias_in = wide(bias, 1, 3)
    bias_hid = wide(bias, 4, 3)
    flying = {}
    for g in range(groups):
        message(0, g)
        if g == 0:
            pl.semaphore_wait(barrier, ring + peers - 2)
        flying[0, g] = exchange(g)
    for layer in range(LAYERS):
        for g in range(groups):
            for copy in flying[layer, g]:
                copy.wait_recv()
            gated_step(layer, g)
            if layer + 1 < LAYERS:
                message(layer + 1, g)
                flying[layer + 1, g] = exchange((layer + 1) * groups + g)

    atom_low = state[LAYERS - 1].astype(BF16)
    counts = jnp.zeros((mols, 1), jnp.int32)
    for m in range(mols):
        counts = jnp.where(iota((mols, 1), 0) == m, atom_counts[m], counts)
    lane = iota((mols, rows_all), 1)
    own = (lane // atoms == iota((mols, rows_all), 0)) & (lane % atoms < counts)
    bias_memory = wide(bias, 7, 4)
    zero = jnp.zeros((mols, width), F32)
    cell, mem_low, read_low = zero, zero.astype(BF16), zero.astype(BF16)
    kept = []
    for turn in range(ROUNDS):
        join = jnp.concatenate([mem_low, read_low, mem_low], axis=1)
        z = jnp.broadcast_to(bias_memory, (mols, 4 * width))
        if turn > 0:
            z = nn(join, memory_low[...]) + z
        i = jax.nn.sigmoid(z[:, :width])
        f = jax.nn.sigmoid(z[:, width : 2 * width])
        c = jnp.tanh(z[:, 2 * width : 3 * width])
        o = jax.nn.sigmoid(z[:, 3 * width :])
        before_cell = cell
        cell = f * cell + i * c
        squashed = jnp.tanh(cell)
        mem_low = (o * squashed).astype(BF16)
        scores = jnp.where(own, nt(mem_low, atom_low), -1000000000.0)
        weights = jnp.exp(scores - jnp.max(scores, axis=1, keepdims=True))
        inverse = 1.0 / jnp.sum(weights, axis=1, keepdims=True)
        read_low = (nn(weights.astype(BF16), atom_low) * inverse).astype(BF16)
        weights = weights * inverse
        weights_low = weights.astype(BF16)
        kept.append((join, i, f, c, o, before_cell, squashed, mem_low, weights, weights_low))
    join = jnp.concatenate([mem_low, read_low], axis=1)
    hidden_low = hidden_w[...].astype(BF16)
    padded[...] = jnp.zeros_like(padded)
    padded[0:n_targets, :] = final_w[...]
    padded[16:17, 0:n_targets] = bias[pl.ds(12 * WIDE, n_targets)].reshape(1, n_targets)
    bias_final = padded[16:17, :]
    final_low = jnp.where(iota((width, WIDE), 0) < n_targets, padded[0:width, :], 0.0).astype(BF16)
    before = nn(join, hidden_low) + wide(bias, 11, 1)
    squash = jax.nn.sigmoid(before)
    inner = before * squash
    inner_low = inner.astype(BF16)
    padded[width : width + mols, 0:n_targets] = targets[...]
    padded[width + mols : width + 2 * mols, 0:n_targets] = labels[...].astype(F32)
    label = padded[width + mols : width + 2 * mols, :]
    gap = nt(inner_low, final_low) + bias_final - padded[width : width + mols, :]
    loss = jnp.sum(label * gap * gap)
    present = jnp.sum(label)
    spot = iota((8, WIDE), 1)
    totals_all[place] = jnp.where(spot == 0, loss, jnp.where(spot == 1, present, 0.0))
    total_copies = [
        far_copy(0, k - 1, lax.rem(place + k, peers), totals_all.at[place], totals_all.at[place])
        for k in range(1, peers)
    ]
    d_pred = 2.0 * label * gap
    d_pred_low = d_pred.astype(BF16)
    head_part[plan.final_at : plan.final_at + 16, :] = tn(d_pred_low, inner_low)[0:16].astype(BF16)
    d_before = nn(d_pred_low, final_low) * (squash + inner * (1.0 - squash))
    d_before_low = d_before.astype(BF16)
    head_part[12 * width : 14 * width, :] = tn(join, d_before_low).astype(BF16)
    grad_bias[...] = jnp.zeros_like(grad_bias)
    grad_bias[11:12, :] = jnp.sum(d_before, axis=0, keepdims=True)
    grad_bias[12:13, :] = jnp.sum(d_pred, axis=0, keepdims=True)
    d_join = nt(d_before_low, hidden_low)
    d_mem, d_read = d_join[:, :width], d_join[:, width:]
    d_cell = zero
    d_bias = jnp.zeros((1, 4 * width), F32)
    lefts, rights, joins, d_gates = [], [], [], []
    for turn in reversed(range(ROUNDS)):
        join, i, f, c, o, before_cell, squashed, mem_low, weights, weights_low = kept[turn]
        d_read_low = d_read.astype(BF16)
        d_weights = nt(d_read_low, atom_low)
        d_scores = weights * (d_weights - jnp.sum(weights * d_weights, axis=1, keepdims=True))
        d_scores_low = d_scores.astype(BF16)
        d_mem = d_mem + nn(d_scores_low, atom_low)
        lefts += [weights_low, d_scores_low]
        rights += [d_read_low, mem_low]
        d_out = d_mem * squashed
        d_cell = d_cell + d_mem * o * (1.0 - squashed * squashed)
        d_z = jnp.concatenate(
            [
                d_cell * c * i * (1.0 - i),
                d_cell * before_cell * f * (1.0 - f),
                d_cell * i * (1.0 - c * c),
                d_out * o * (1.0 - o),
            ],
            axis=1,
        )
        d_cell = d_cell * f
        d_bias = d_bias + jnp.sum(d_z, axis=0, keepdims=True)
        d_z_low = d_z.astype(BF16)
        if turn > 0:
            joins.append(join)
            d_gates.append(d_z_low)
            d_join = nt(d_z_low, memory_low[...])
            d_mem = d_join[:, :width] + d_join[:, 2 * width :]
            d_read = d_join[:, width : 2 * width]
    grad_memory = tn(jnp.concatenate(joins, axis=0), jnp.concatenate(d_gates, axis=0)).astype(BF16)
    for i in range(4):
        head_part[i * 3 * width : (i + 1) * 3 * width, :] = grad_memory[:, i * width : (i + 1) * width]
    used = plan.final_at + 16
    head_part[used:, :] = jnp.zeros((ring * plan.head - used, WIDE), BF16)
    head_copies = []
    for k in range(1, peers):
        peer = lax.rem(place + k, peers)
        rows = rows16(me * plan.head + peer * plan.head_part, plan.head_part)
        head_copies.append(far_copy(1, k - 1, peer, head_part.at[rows, :], head_recv.at[k - 1]))
    for i in range(4):
        grad_bias[7 + i : 8 + i, :] = d_bias[:, i * width : (i + 1) * width]
    state_grad[...] = tn(jnp.concatenate(lefts, axis=0), jnp.concatenate(rights, axis=0))

    def gated_back(layer, g):
        bias_parts = [jnp.zeros((1, 3 * width), F32) for _ in range(2)]
        for j in range(2):
            rows = slice(g * span + j * span // 2, g * span + (j + 1) * span // 2)
            reset, update = gates[layer, 0, rows, :], gates[layer, 1, rows, :]
            candidate, third = gates[layer, 2, rows, :], gates[layer, 3, rows, :]
            old = states[rows, :].astype(F32) if layer == 0 else state[layer - 1, rows, :]
            grad = state_grad[rows, :]
            d_candidate = grad * (1.0 - update) * (1.0 - candidate * candidate)
            d_update = grad * (old - candidate) * update * (1.0 - update)
            d_reset = d_candidate * third * reset * (1.0 - reset)
            d_in = jnp.concatenate([d_reset, d_update, d_candidate], axis=1)
            d_hid = jnp.concatenate([d_reset, d_update, d_candidate * reset], axis=1)
            bias_parts[0] = bias_parts[0] + jnp.sum(d_in, axis=0, keepdims=True)
            bias_parts[1] = bias_parts[1] + jnp.sum(d_hid, axis=0, keepdims=True)
            d_in_low, d_hid_low = d_in.astype(BF16), d_hid.astype(BF16)
            gate_grad[layer, 0, rows, :] = d_in_low
            gate_grad[layer, 1, rows, :] = d_hid_low
            pulled[layer, rows, :] = nt(d_in_low, gated_low[0]).astype(BF16)
            if layer > 0:
                state_grad[rows, :] = grad * update + nt(d_hid_low, gated_low[1])
        for s in range(2):
            for i in range(3):
                at = 1 + 3 * s + i
                grad_bias[at : at + 1, :] += bias_parts[s][:, i * width : (i + 1) * width]

    def gated_weights_back(layer):
        low = states[...] if layer == 0 else state[layer - 1].astype(BF16)
        d_first = tn(gathered[layer], gate_grad[layer, 0])
        d_second = tn(low, gate_grad[layer, 1])
        if layer == LAYERS - 1:
            grad_gated[0], grad_gated[1] = d_first, d_second
        else:
            grad_gated[0] += d_first
            grad_gated[1] += d_second

    pick_t = one_hot(iota((half, width), 1) == me * local + iota((half, width), 0) // GROUP)
    pick_n = one_hot(iota((width, half), 0) == me * local + iota((width, half), 1) // GROUP)

    def message_back(layer, g):
        rows = slice(g * span, (g + 1) * span)
        wide_grad = jnp.where(same_mol_t, nt(pick_t, pulled[layer, rows, :]), 0.0).astype(BF16)

        def atoms_pair(ap, carry):
            columns = pl.ds(pl.multiple_of(ap * 2 * width, 2 * width), 2 * width)
            x = nn(wide_grad, sent[rows, columns])
            where = pl.ds(pl.multiple_of(layer * rows_all + g * span + ap * 16, 16), 16)
            for r in range(local):
                at = r * GROUP
                tile = jnp.concatenate([x[at : at + GROUP, :width], x[at : at + GROUP, width:]], axis=0)
                gt[where, r * width : (r + 1) * width] = tile.astype(BF16)
            return carry

        lax.fori_loop(0, atoms // 2, atoms_pair, 0, unroll=8)

    last = LAYERS - 1
    for layer in range(last, 0, -1):
        reducing, gathering = {}, {}
        for g in range(groups):
            gated_back(layer, g)
            message_back(layer, g)
            at = layer * rows_all + g * span
            back = nn(gt[at : at + span, :], edge_low[...]).astype(BF16)
            reduce_send[g * span : (g + 1) * span, :] = nn(order_back, back).astype(BF16)
            reducing[g] = []
            for k in range(1, ring):
                rows = rows16(g * span + lax.rem(me + k, ring) * block, block)
                stage = (LAYERS + 1) * groups + g
                reducing[g].append(row_copy(stage, k, reduce_send.at[rows, :], reduce_recv.at[g, k - 1]))
        gated_weights_back(layer)
        for g in range(groups):
            for copy in reducing[g]:
                copy.wait_recv()
            total = reduce_send[rows16(g * span + me * block, block), :].astype(F32)
            for k in range(ring - 1):
                total = total + reduce_recv[g, k].astype(F32)
            parcels[LAYERS * groups + g, me] = total.astype(BF16)
            gathering[g] = exchange(LAYERS * groups + g)
    rest_copies = []
    for g in range(groups):
        for copy in gathering[g]:
            copy.wait_recv()
        for j in range(ring):
            rows = slice(g * span + j * block, g * span + (j + 1) * block)
            state_grad[rows, :] += parcels[LAYERS * groups + g, j].astype(F32)
        gated_back(0, g)
        if g == groups - 1:
            gated_weights_back(0)
            for s in range(2):
                for i in range(3):
                    at = (s * 3 + i) * width
                    rest_full[at : at + width, :] = grad_gated[s, :, i * width : (i + 1) * width].astype(BF16)
            rest_full[plan.bias_at : plan.bias_at + 16, :] = grad_bias[...].astype(BF16)
            used = plan.bias_at + 16
            if ring * plan.rest_own > used:
                rest_full[used:, :] = jnp.zeros((ring * plan.rest_own - used, WIDE), BF16)
            rest_part[0 : plan.rest_own, :] = rest_full[rows16(me * plan.rest_own, plan.rest_own), :]
            if plan.rest > plan.rest_own:
                rest_part[plan.rest_own :, :] = jnp.zeros((plan.rest - plan.rest_own, WIDE), BF16)
            for k in range(1, peers):
                peer = lax.rem(place + k, peers)
                rows = rows16(peer * plan.rest_part, plan.rest_part)
                rest_copies.append(far_copy(4, k - 1, peer, rest_part.at[rows, :], rest_recv.at[k - 1]))
        message_back(0, g)

    for copy in head_copies:
        copy.wait_recv()
    mine = rows16(me * plan.head + place * plan.head_part, plan.head_part)
    total = head_part[mine, :].astype(F32)
    for k in range(peers - 1):
        total = total + head_recv[k].astype(F32)
    head_all[mine, :] = total.astype(BF16)
    head_copies[:] = [
        far_copy(2, k - 1, lax.rem(place + k, peers), head_all.at[mine, :], head_all.at[mine, :])
        for k in range(1, peers)
    ]

    lines = peers // 2
    line, side = lax.div(place, 2), lax.rem(place, 2)
    neighbour = line * 2 + 1 - side
    part = plan.edge_part
    stack = max(1, 2 * width // (2 * part))
    blocks = lines // stack
    home, seat = lax.div(line, stack), lax.rem(line, stack)

    def out_weights(start):
        columns = pl.ds(pl.multiple_of(start, 2 * width), 2 * width)
        edge_part[columns, :] = nn(turned_lows[...], gt[:, columns]).T.astype(BF16)

    def lines_of(j):
        return [lax.rem(home + j, blocks) * stack + lax.rem(seat + i, stack) for i in range(stack)]

    def scatter_near(j):
        copies = []
        if stack > 1:
            out_weights(lax.rem(home + j, blocks) * stack * 2 * part)
        for i, other in enumerate(lines_of(j)):
            if stack == 1:
                for step in range(part // (2 * width)):
                    out_weights(other * 2 * part + (1 - side) * part + step * 2 * width)
            rows = rows16(other * 2 * part + (1 - side) * part, part)
            copies.append(far_copy(7, j * stack + i, neighbour, edge_part.at[rows, :], near_recv.at[rows16(other * part, part), :]))
            if stack == 1:
                for step in range(part // (2 * width)):
                    out_weights(other * 2 * part + side * part + step * 2 * width)
        return copies

    edge_copies = []

    def scatter_far(j, copies):
        for i, other in enumerate(lines_of(j)):
            copies[i].wait_recv()
            rows = rows16(other * part, part)
            total = edge_part[rows16(other * 2 * part + side * part, part), :].astype(F32) + near_recv[rows, :].astype(F32)
            near_sum[rows, :] = total.astype(BF16)
            if j > 0 or i > 0:
                k = j if stack == 1 else lax.rem(other - line + lines, lines)
                edge_copies.append(far_copy(3, k - 1, other * 2 + side, near_sum.at[rows, :], edge_recv.at[k - 1]))

    order_of = [*range(1, blocks), 0]
    near_copies = [(j, scatter_near(j)) for j in order_of]

    def pair_grads(g):
        wide_grad = jnp.concatenate(
            [
                jnp.where(same_mol, nn(pulled[layer, g * span : (g + 1) * span, :], pick_n), 0.0).astype(BF16)
                for layer in range(LAYERS)
            ],
            axis=1,
        )

        def pair_back(ap, carry):
            columns = pl.ds(pl.multiple_of(ap * 2 * width, 2 * width), 2 * width)
            x = nn(wide_grad, turned[g * LAYERS * half : (g + 1) * LAYERS * half, columns]).astype(BF16)
            for s in range(2):
                where = pl.ds(pl.multiple_of((ap * 2 + s) * atoms, atoms), atoms)
                for m in range(GROUP):
                    pair_grad[g * GROUP + m, where, :] = x[m * atoms : (m + 1) * atoms, s * width : (s + 1) * width]
            return carry

        lax.fori_loop(0, atoms // 2, pair_back, 0, unroll=8)

    for g in range(groups - 1):
        pair_grads(g)
    for waiting in near_copies:
        scatter_far(*waiting)
    for copy in rest_copies:
        copy.wait_recv()
    mine = rows16(place * plan.rest_part, plan.rest_part)
    total = rest_part[mine, :].astype(F32)
    for k in range(peers - 1):
        total = total + rest_recv[k].astype(F32)
    rest_all[me, mine, :] = total.astype(BF16)
    rest_copies = [
        far_copy(6, k - 1, lax.rem(place + k, peers), rest_all.at[me, mine, :], rest_all.at[me, mine, :])
        for k in range(1, peers)
    ]
    for copy in head_copies:
        copy.wait_recv()
    rows = rows16(me * plan.head, plan.head)
    head_rows = [row_copy((LAYERS + 2) * groups, k, head_all.at[rows, :], head_all.at[rows, :]) for k in range(1, ring)]
    pair_grads(groups - 1)

    for copy in edge_copies:
        copy.wait_recv()
    pieces = plan.pieces
    size = part // pieces
    across, beside = {}, {}
    for p in range(pieces):
        own = rows16(line * part + p * size, size)
        mine = rows16(place * part + p * size, size)
        total = near_sum[own, :].astype(F32)
        for k in range(lines - 1):
            total = total + edge_recv[k, p * size : (p + 1) * size, :].astype(F32)
        edge_all[mine, :] = total.astype(BF16)
        for k in range(1, lines):
            peer = lax.rem(line + k, lines) * 2 + side
            across[p, k] = far_copy(5, p * peers + k, peer, edge_all.at[mine, :], edge_all.at[mine, :])
        beside[p, 0] = far_copy(5, p * peers, neighbour, edge_all.at[mine, :], edge_all.at[mine, :])

    def onward(p):
        for k in range(1, lines):
            across[p, k].wait_recv()
            rows = rows16((lax.rem(line - k + lines, lines) * 2 + side) * part + p * size, size)
            beside[p, k] = far_copy(5, p * peers + lines + k, neighbour, edge_all.at[rows, :], edge_all.at[rows, :])

    lane_pair = iota((edges // 2, atoms * atoms), 1).astype(F32)
    total_bias = jnp.zeros((8, width), F32)
    for m in range(mols):
        if m == mols // 2:
            for copy in rest_copies:
                copy.wait_recv()
            rest_rows = [row_copy((LAYERS + 2) * groups + 1, k, rest_all.at[me], rest_all.at[me]) for k in range(1, ring)]
        for i in range(2):
            rows = slice(i * edges // 2, (i + 1) * edges // 2)
            d_first = nn(one_hot(lane_pair == pair_cols[rows, m : m + 1]), pair_grad[m]) * slope[m, rows, :]
            total_bias = total_bias + jnp.sum(d_first.reshape(edges // 16, 8, width), axis=0)
            first_grad[m * edges + i * edges // 2 : m * edges + (i + 1) * edges // 2, :] = d_first.astype(BF16)
    total_in = nn(jnp.concatenate([feats[m] for m in range(mols)], axis=1), first_grad[...])
    total_bias = jnp.sum(total_bias, axis=0, keepdims=True)
    first_row[me, 0:features, :] = total_in
    first_row[me, features : features + 8, :] = jnp.broadcast_to(total_bias, (8, width))
    first_copies = [row_copy((LAYERS + 2) * groups + 2, k, first_row.at[me], first_row.at[me]) for k in range(1, ring)]
    onward(0)
    for copy in first_copies:
        copy.wait_recv()
    total = first_row[0]
    for q in range(1, ring):
        total = total + first_row[q]
    first_mol[place] = total
    first_copies = [
        far_copy(8, k - 1, lax.rem(place + k, peers), first_mol.at[place], first_mol.at[place])
        for k in range(1, peers)
    ]
    for p in range(1, pieces):
        onward(p)

    stores = []

    def store(source_ref, target_ref):
        copy = pltpu.make_async_copy(source_ref, target_ref, store_sem.at[len(stores)])
        copy.start()
        stores.append(copy)

    for copy in head_rows:
        copy.wait_recv()
    store(head_all, head_sum)
    for copy in rest_rows:
        copy.wait_recv()
    store(rest_all, rest_sum)
    for copy in total_copies + first_copies:
        copy.wait_recv()
    total, total_first = totals_all[0], first_mol[0]
    for k in range(1, peers):
        total = total + totals_all[k]
        total_first = total_first + first_mol[k]
    totals[0:8, :] = total
    totals[8:, :] = total_first
    for copy in beside.values():
        copy.wait_recv()
    store(edge_all, edge_sum)
    for copy in started:
        copy.wait_send()
    for copy in stores:
        copy.wait()


def adamw(weight, first, second, grad, rate):
    first_new = BETA_ONE * first + (1.0 - BETA_ONE) * grad
    second_new = BETA_TWO * second + (1.0 - BETA_TWO) * grad * grad
    scaled = jnp.sqrt(second_new * (1.0 / (1.0 - BETA_TWO**STEP))) + EPSILON
    weight_new = (1.0 - rate * DECAY) * weight - (rate / (1.0 - BETA_ONE**STEP)) * first_new / scaled
    return (weight_new, first_new, second_new, weight_new.astype(BF16))


PIECES = 4


def update_kernel(ring, peers, local, counted, totals, edge_far, head_far, rest_far, *refs):
    fars, refs = refs[:21], refs[21:]
    (loss_out, count_out), refs = refs[:2], refs[2:]
    outs, refs = refs[:28], refs[28:]
    (edge_sum, head_sum, rest_sum), refs = refs[:3], refs[3:]
    olds, refs = refs[:21], refs[21:]
    news, (fetch_sem, store_sem) = refs[:28], refs[28:]
    features, width = olds[0].shape
    n_bias = olds[18].shape[0]
    plan = Plan(ring, peers, width, local)
    every = slice(None)
    columns = plan.edge // PIECES
    cuts = [(every, pl.ds(i * columns, columns)) for i in range(PIECES)]
    count = [0, 0]

    def copies_of(sides, sem, which):
        made = []
        for source_ref, target_ref in sides:
            made.append(pltpu.make_async_copy(source_ref, target_ref, sem.at[count[which]]))
            made[-1].start()
            count[which] += 1
        return made

    def fetch(index, cut=None):
        where = range(3 * index, 3 * index + 3)
        return copies_of([(fars[i], olds[i]) if cut is None else (fars[i].at[cut], olds[i].at[cut]) for i in where], fetch_sem, 0)

    def store(index, cut=None):
        where = range(4 * index, 4 * index + 4)
        return copies_of([(news[i], outs[i]) if cut is None else (news[i].at[cut], outs[i].at[cut]) for i in where], store_sem, 1)

    edge_ready = copies_of([(edge_far, edge_sum)], fetch_sem, 0)
    cut_ready = [fetch(1, cut) for cut in cuts]
    head_ready = copies_of([(head_far, head_sum)], fetch_sem, 0)
    ready = {index: fetch(index) for index in (3, 4, 5)}
    rest_ready = copies_of([(rest_far, rest_sum)], fetch_sem, 0)
    ready.update({index: fetch(index) for index in (2, 0, 6)})
    loss_out[0] = counted[0, 0]
    count_out[0] = counted[0, 1]
    inverse = (1.0 / totals[0:1, :])[0:1, 1:2]

    def update(index, view, grad):
        parts = [ref[view] for ref in olds[3 * index : 3 * index + 3]]
        for ref, value in zip(news[4 * index : 4 * index + 4], adamw(*parts, grad, RATES[index])):
            ref[view] = value

    def wait(copies):
        for copy in copies:
            copy.wait()

    stored = []
    wait(edge_ready)
    for p in range(PIECES):
        wait(cut_ready[p])
        for i in range(p * columns // width, (p + 1) * columns // width):
            grad = edge_sum[i * width : (i + 1) * width, :].astype(F32) * inverse
            update(1, (every, slice(i * width, (i + 1) * width)), grad)
        stored += store(1, cuts[p])
    wait(head_ready + ready[3])
    for i in range(4):
        grad = head_sum[i * 3 * width : (i + 1) * 3 * width, :].astype(F32) * inverse
        update(3, (every, slice(i * width, (i + 1) * width)), grad)
    stored += store(3)
    wait(rest_ready + ready[2])
    for s in range(2):
        for i in range(3):
            at, end = (s * 3 + i) * width, (s * 3 + i + 1) * width
            while at < end:
                q, low = divmod(at, plan.rest_own)
                rows = min(end - at, plan.rest_own - low)
                first = at - (s * 3 + i) * width
                grad = rest_sum[q, low : low + rows, :].astype(F32) * inverse
                update(2, (s, slice(first, first + rows), slice(i * width, (i + 1) * width)), grad)
                at += rows
    stored += store(2)
    wait(ready[4])
    update(4, (every, every), head_sum[12 * width : 14 * width, :].astype(F32) * inverse)
    stored += store(4)
    wait(ready[5])
    n_targets = olds[15].shape[0]
    update(5, (every, every), (head_sum[plan.final_at : plan.final_at + 16, :].astype(F32) * inverse)[0:n_targets])
    stored += store(5)
    own = totals[8:, :] * inverse
    wait(ready[0])
    update(0, (every, every), own[0:features])
    stored += store(0)
    q, low = divmod(plan.bias_at, plan.rest_own)
    biases = rest_sum[q, low : low + 16, :].astype(F32) * inverse
    wait(ready[6])
    for i in range(-(-n_bias // WIDE)):
        size = min(WIDE, n_bias - i * WIDE)
        grad = (own[features : features + 1] if i == 0 else biases[i : i + 1])[:, 0:size]
        update(6, pl.ds(i * WIDE, size), grad.reshape(size))
    stored += store(6)
    wait(stored)


def shards(
    edge_feats,
    edge_source,
    edge_target,
    atom_counts,
    edge_counts,
    atom_states,
    targets,
    label_mask,
    edge_input,
    edge_input_first,
    edge_input_second,
    edge_output,
    edge_output_first,
    edge_output_second,
    gated_weights,
    gated_first,
    gated_second,
    memory_weights,
    memory_first,
    memory_second,
    readout_hidden,
    readout_hidden_first,
    readout_hidden_second,
    readout_final,
    readout_final_first,
    readout_final_second,
    bias_vector,
    bias_first,
    bias_second,
):
    mols, edges, features = edge_feats.shape
    atoms, width = atom_states.shape[1:]
    ring = lax.axis_size("row")
    local = width // ring
    rows_all = mols * atoms
    block = GROUP * atoms // ring
    groups = mols // GROUP
    peers = lax.axis_size("mol")
    plan = Plan(ring, peers, width, local)

    finals = [value.T for value in (readout_final, readout_final_first, readout_final_second)]
    vmem = pl.BlockSpec(memory_space=pltpu.VMEM)
    smem = pl.BlockSpec(memory_space=pltpu.SMEM)
    far = pl.BlockSpec(memory_space=pl.ANY)
    shape = jax.ShapeDtypeStruct
    edge_sum, head_sum, rest_sum, totals = pl.pallas_call(
        functools.partial(step_kernel, ring, peers),
        out_shape=[
            shape((plan.edge, WIDE), BF16),
            shape((ring * plan.head, WIDE), BF16),
            shape((ring, plan.rest, WIDE), BF16),
            shape((8 + features + 8, WIDE), F32),
        ],
        in_specs=[smem, smem] + [vmem] * 9 + [far] * 4,
        out_specs=[far] * 3 + [vmem],
        scratch_shapes=[
            pltpu.VMEM((local * width, width), BF16),
            pltpu.VMEM((mols, edges), jnp.int32),
            pltpu.VMEM((edges, mols), F32),
            pltpu.VMEM((rows_all, atoms * width), BF16),
            pltpu.VMEM((mols // GROUP * LAYERS * GROUP * local, atoms * width), BF16),
            pltpu.VMEM((mols, edges, width), F32),
            pltpu.VMEM((mols, atoms * atoms, width), BF16),
            pltpu.VMEM((width, LAYERS * rows_all), BF16),
            pltpu.VMEM((LAYERS, rows_all, width), BF16),
            pltpu.VMEM((LAYERS, 4, rows_all, width), F32),
            pltpu.VMEM((LAYERS, rows_all, width), F32),
            pltpu.VMEM((rows_all, width), F32),
            pltpu.VMEM((LAYERS, 2, rows_all, 3 * width), BF16),
            pltpu.VMEM((LAYERS, rows_all, width), BF16),
            pltpu.VMEM((3 * width, 4 * width), BF16),
            pltpu.VMEM((width + 2 * mols, WIDE), F32),
            pltpu.VMEM(((LAYERS + 1) * groups, ring, block, WIDE), BF16),
            pltpu.VMEM((rows_all, width), BF16),
            pltpu.VMEM((groups, ring - 1, block, width), BF16),
            pltpu.VMEM((2, width, 3 * width), F32),
            pltpu.VMEM((16, WIDE), F32),
            pltpu.VMEM((peers, 8, WIDE), F32),
            pltpu.VMEM((plan.edge, WIDE), BF16),
            pltpu.VMEM((peers // 2 - 1, plan.edge_part, WIDE), BF16),
            pltpu.VMEM((plan.edge, WIDE), BF16),
            pltpu.VMEM((ring * plan.head, WIDE), BF16),
            pltpu.VMEM((peers - 1, plan.head_part, WIDE), BF16),
            pltpu.VMEM((ring * plan.head, WIDE), BF16),
            pltpu.VMEM((ring * plan.rest_own, WIDE), BF16),
            pltpu.VMEM((plan.rest, WIDE), BF16),
            pltpu.VMEM((peers - 1, plan.rest_part, WIDE), BF16),
            pltpu.VMEM((ring, plan.rest, WIDE), BF16),
            pltpu.SemaphoreType.DMA(((LAYERS + 2) * groups + 3, ring - 1)),
            pltpu.SemaphoreType.DMA(((LAYERS + 2) * groups + 3, ring - 1)),
            pltpu.SemaphoreType.DMA((plan.stages[9],)),
            pltpu.SemaphoreType.DMA((plan.stages[9],)),
            pltpu.VMEM((LAYERS * rows_all, local * width), BF16),
            pltpu.VMEM(edge_output.shape, F32),
            pltpu.VMEM(gated_weights.shape, F32),
            pltpu.VMEM(memory_weights.shape, F32),
            pltpu.VMEM(readout_hidden.shape, F32),
            pltpu.SemaphoreType.DMA((4,)),
            pltpu.SemaphoreType.DMA((3,)),
            pltpu.VMEM((peers // 2 * plan.edge_part, WIDE), BF16),
            pltpu.VMEM((peers // 2 * plan.edge_part, WIDE), BF16),
            pltpu.VMEM((ring, features + 8, WIDE), F32),
            pltpu.VMEM((peers, features + 8, WIDE), F32),
            pltpu.VMEM((mols * edges, width), BF16),
        ],
        compiler_params=pltpu.CompilerParams(
            collective_id=0, has_side_effects=True, vmem_limit_bytes=60 * 1024 * 1024
        ),
    )(
        atom_counts,
        edge_counts,
        jnp.swapaxes(edge_feats, 1, 2),
        edge_source,
        edge_target,
        atom_states.reshape(rows_all, width),
        targets,
        label_mask,
        edge_input,
        finals[0],
        bias_vector,
        edge_output,
        gated_weights,
        memory_weights,
        readout_hidden,
    )
    olds = [edge_input, edge_input_first, edge_input_second, edge_output, edge_output_first, edge_output_second]
    olds += [gated_weights, gated_first, gated_second, memory_weights, memory_first, memory_second]
    olds += [readout_hidden, readout_hidden_first, readout_hidden_second] + finals
    olds += [bias_vector, bias_first, bias_second]
    news = [shape(olds[3 * index].shape, kind) for index in range(7) for kind in (F32, F32, F32, BF16)]
    sums = [edge_sum, head_sum, rest_sum]
    outs = pl.pallas_call(
        functools.partial(update_kernel, ring, peers, local),
        out_shape=[shape((1,), F32)] * 2 + news,
        in_specs=[smem, vmem] + [far] * 24,
        out_specs=[smem] * 2 + [far] * 28,
        scratch_shapes=[pltpu.VMEM(value.shape, value.dtype) for value in sums + olds + news]
        + [pltpu.SemaphoreType.DMA((3 + 18 + 3 * PIECES,)), pltpu.SemaphoreType.DMA((24 + 4 * PIECES,))],
        compiler_params=pltpu.CompilerParams(vmem_limit_bytes=60 * 1024 * 1024),
    )(totals, totals, *sums, *olds)
    outs = list(outs)
    outs[0], outs[1] = outs[0].reshape(()), outs[1].reshape(())
    outs[22:26] = [value.T for value in outs[22:26]]
    return tuple(outs)


def solution(mesh):
    cut = P(None, "row")
    per_mol = (P("mol", None, None), P("mol", None), P("mol", None), P("mol"), P("mol"), P("mol", None, None))
    per_mol += (P("mol", None), P("mol", None))
    return jax.shard_map(
        shards,
        mesh=mesh,
        in_specs=per_mol + (P(),) * 3 + (cut,) * 3 + (P(),) * 15,
        out_specs=(P(),) * 6 + (cut,) * 4 + (P(),) * 20,
        check_vma=False,
    )
```

```python
import functools

import jax
import jax.numpy as jnp
from jax import lax
from jax.experimental import pallas as pl
from jax.experimental.pallas import tpu as pltpu
from jax.sharding import PartitionSpec as P

LAYERS = 2
ROUNDS = 6
STEP = 10
BETA_ONE = 0.9
BETA_TWO = 0.999
EPSILON = 1e-08
DECAY = 0.01
RATES = (0.25, 0.004, 0.09, 0.05, 0.06, 0.09, 0.2)

MESH = pl.DeviceIdType.MESH
F32 = jnp.float32
BF16 = jnp.bfloat16
GROUP = 8
WIDE = 128


def nn(left, right):
    return lax.dot_general(left, right, (((1,), (0,)), ((), ())), preferred_element_type=F32)


def nt(left, right):
    return lax.dot_general(left, right, (((1,), (1,)), ((), ())), preferred_element_type=F32)


def tn(left, right):
    return lax.dot_general(left, right, (((0,), (0,)), ((), ())), preferred_element_type=F32)


def iota(shape, dim):
    return lax.broadcasted_iota(jnp.int32, shape, dim)


def one_hot(condition):
    return jnp.where(condition, 1.0, 0.0).astype(BF16)


def wide(bias_ref, first, count):
    return bias_ref[pl.ds(first * WIDE, count * WIDE)].reshape(1, count * WIDE)


def round_up(value, unit):
    return -(-value // unit) * unit


class Plan:
    def __init__(self, ring, peers, width, local):
        unit = 16 * peers
        self.edge = local * width
        self.edge_part = self.edge // peers
        self.final_at = 12 * width + 2 * width
        self.head = round_up(-(-(self.final_at + 16) // ring), unit)
        self.head_part = self.head // peers
        self.bias_at = 6 * width
        self.rest_own = round_up(-(-(self.bias_at + 16) // ring), 16)
        self.rest = round_up(self.rest_own, unit)
        self.rest_part = self.rest // peers
        self.pieces = 2 if self.edge_part >= WIDE else 1
        sizes = [peers - 1] * 9
        sizes[3], sizes[5], sizes[7] = peers // 2 - 1, self.pieces * peers, peers // 2
        self.stages = [sum(sizes[:stage]) for stage in range(10)]


def step_kernel(
    ring,
    peers,
    atom_counts,
    edge_counts,
    feats,
    source,
    target,
    states,
    targets,
    labels,
    edge_in,
    final_w,
    bias,
    edge_far,
    gated_far,
    memory_far,
    hidden_far,
    edge_sum,
    head_sum,
    rest_sum,
    totals,
    edge_low,
    pairs,
    pair_cols,
    sent,
    turned,
    slope,
    pair_grad,
    turned_lows,
    gathered,
    gates,
    state,
    state_grad,
    gate_grad,
    pulled,
    memory_low,
    padded,
    parcels,
    reduce_send,
    reduce_recv,
    grad_gated,
    grad_bias,
    totals_all,
    edge_part,
    edge_recv,
    edge_all,
    head_part,
    head_recv,
    head_all,
    rest_full,
    rest_part,
    rest_recv,
    rest_all,
    send_sem,
    recv_sem,
    far_send,
    far_recv,
    gt,
    edge_out,
    gated,
    memory,
    hidden_w,
    fetch_sem,
    store_sem,
    near_recv,
    near_sum,
    first_row,
    first_mol,
    first_grad,
):
    mols, features, edges = feats.shape
    rows_all, width = states.shape
    atoms = rows_all // mols
    local = width // ring
    groups = mols // GROUP
    span = GROUP * atoms
    half = GROUP * local
    block = span // ring
    n_targets = targets.shape[1]
    me = lax.axis_index("row")
    place = lax.axis_index("mol")
    plan = Plan(ring, peers, width, local)
    started = []
    fetches = [
        pltpu.make_async_copy(far, near, fetch_sem.at[i])
        for i, (far, near) in enumerate(
            ((edge_far, edge_out), (gated_far, gated), (memory_far, memory), (hidden_far, hidden_w))
        )
    ]
    for copy in fetches:
        copy.start()

    def rows16(start, count):
        return pl.ds(pl.multiple_of(start, 16), count)

    def far_copy(stage, index, peer, source_ref, target_ref):
        index += plan.stages[stage]
        copy = pltpu.make_async_remote_copy(
            src_ref=source_ref,
            dst_ref=target_ref,
            send_sem=far_send.at[index],
            recv_sem=far_recv.at[index],
            device_id={"mol": peer},
            device_id_type=MESH,
        )
        copy.start()
        started.append(copy)
        return copy

    def row_copy(stage, k, source_ref, target_ref):
        copy = pltpu.make_async_remote_copy(
            src_ref=source_ref,
            dst_ref=target_ref,
            send_sem=send_sem.at[stage, k - 1],
            recv_sem=recv_sem.at[stage, k - 1],
            device_id={"row": lax.rem(me + k, ring)},
            device_id_type=MESH,
        )
        copy.start()
        started.append(copy)
        return copy

    barrier = pltpu.get_barrier_semaphore()
    for k in range(1, ring):
        pl.semaphore_signal(barrier, inc=1, device_id={"row": lax.rem(me + k, ring)}, device_id_type=MESH)
    for k in range(1, peers):
        pl.semaphore_signal(barrier, inc=1, device_id={"mol": lax.rem(place + k, peers)}, device_id_type=MESH)

    low_in = edge_in[...].astype(BF16)

    lane_edge = iota((1, edges), 1)
    row_index = iota((atoms * atoms, edges), 0)
    for m in range(mols):
        pairs[m : m + 1, :] = jnp.where(
            lane_edge < edge_counts[m], source[m : m + 1, :] * atoms + target[m : m + 1, :], -1
        )
    pair_cols[...] = pairs[...].astype(F32).T

    bias_first = wide(bias, 0, 1)

    def edge_network(m, carry):
        before = tn(feats[m], low_in) + bias_first
        squash = jax.nn.sigmoid(before)
        act = before * squash
        slope[m] = squash + act * (1.0 - squash)
        act = act.astype(BF16)
        pair = pairs[pl.ds(m, 1), :]
        rows = pl.ds(pl.multiple_of(m * atoms, atoms), atoms)
        sums = nn(one_hot(row_index == pair), act).astype(BF16)
        for a in range(atoms):
            sent[rows, a * width : (a + 1) * width] = sums[a * atoms : (a + 1) * atoms]
        return carry

    lax.fori_loop(0, mols, edge_network, 0, unroll=4)

    order = one_hot(
        (iota((span, span), 1) // atoms == iota((span, span), 0) % GROUP)
        & (iota((span, span), 1) % atoms == iota((span, span), 0) // GROUP)
    )
    order_back = one_hot(
        (iota((span, span), 0) // atoms == iota((span, span), 1) % GROUP)
        & (iota((span, span), 0) % atoms == iota((span, span), 1) // GROUP)
    )
    same_mol = iota((span, half), 0) // atoms == iota((span, half), 1) % GROUP
    same_mol_t = iota((half, span), 0) % GROUP == iota((half, span), 1) // atoms

    def state_low(layer, rows):
        if layer == 0:
            return states[rows, :]
        return state[layer - 1, rows, :].astype(BF16)

    def message(layer, g):
        rows = slice(g * span, (g + 1) * span)
        low_p = nn(order, state_low(layer, rows)).astype(BF16)
        at = layer * rows_all + g * span
        turned_lows[:, at : at + span] = low_p.astype(F32).T.astype(BF16)
        base = (g * LAYERS + layer) * half

        def rows_pair(rp, carry):
            t = nt(low_p, edge_low[pl.ds(pl.multiple_of(rp * 2 * width, 2 * width), 2 * width), :])
            where = pl.ds(pl.multiple_of(base + rp * 16, 16), 16)
            for a in range(atoms):
                at = a * GROUP
                tile = jnp.concatenate([t[at : at + GROUP, :width], t[at : at + GROUP, width:]], axis=0)
                turned[where, a * width : (a + 1) * width] = tile.astype(BF16)
            return carry

        lax.fori_loop(0, local // 2, rows_pair, 0, unroll=16)
        u = nt(sent[rows, :], turned[base : base + half, :])
        u = jnp.where(same_mol, u, 0.0).astype(BF16)
        packed = jnp.zeros((block, WIDE), F32)
        for j in range(ring):
            pick = one_hot(iota((half, WIDE), 1) == j * local + iota((half, WIDE), 0) // GROUP)
            packed = packed + nn(u[j * block : (j + 1) * block], pick)
        parcels[layer * groups + g, me] = packed.astype(BF16)

    def exchange(stage):
        return [row_copy(stage, k, parcels.at[stage, me], parcels.at[stage, me]) for k in range(1, ring)]

    def gated_step(layer, g):
        stage = layer * groups + g
        joined = jnp.concatenate([parcels[stage, q] for q in range(ring)], axis=1)
        for j in range(0, ring, 2):
            parts = []
            for i in (j, j + 1):
                row, column = iota((ring * WIDE, width), 0), iota((ring * WIDE, width), 1)
                pick = one_hot(
                    (row % WIDE // local == i) & (row // WIDE == column // local) & (row % local == column % local)
                )
                parts.append(nn(joined, pick))
            rows = slice(g * span + j * block, g * span + (j + 2) * block)
            got = jnp.concatenate(parts, axis=0).astype(BF16)
            gathered[layer, rows, :] = got
            old = states[rows, :].astype(F32) if layer == 0 else state[layer - 1, rows, :]
            gate_in = nn(got, gated_low[0]) + bias_in
            gate_hid = nn(state_low(layer, rows), gated_low[1]) + bias_hid
            reset = jax.nn.sigmoid(gate_in[:, :width] + gate_hid[:, :width])
            update = jax.nn.sigmoid(gate_in[:, width : 2 * width] + gate_hid[:, width : 2 * width])
            third = gate_hid[:, 2 * width :]
            candidate = jnp.tanh(gate_in[:, 2 * width :] + reset * third)
            gates[layer, 0, rows, :] = reset
            gates[layer, 1, rows, :] = update
            gates[layer, 2, rows, :] = candidate
            gates[layer, 3, rows, :] = third
            state[layer, rows, :] = (1.0 - update) * candidate + update * old

    for copy in fetches:
        copy.wait()
    memory_low[...] = memory[...].astype(BF16)
    for r in range(local):
        edge_low[r * width : (r + 1) * width, :] = edge_out[:, r * width : (r + 1) * width].astype(BF16)
    gated_low = [gated[i].astype(BF16) for i in range(2)]
    bias_in = wide(bias, 1, 3)
    bias_hid = wide(bias, 4, 3)
    flying = {}
    for g in range(groups):
        message(0, g)
        if g == 0:
            pl.semaphore_wait(barrier, ring + peers - 2)
        flying[0, g] = exchange(g)
    for layer in range(LAYERS):
        for g in range(groups):
            for copy in flying[layer, g]:
                copy.wait_recv()
            gated_step(layer, g)
            if layer + 1 < LAYERS:
                message(layer + 1, g)
                flying[layer + 1, g] = exchange((layer + 1) * groups + g)

    atom_low = state[LAYERS - 1].astype(BF16)
    counts = jnp.zeros((mols, 1), jnp.int32)
    for m in range(mols):
        counts = jnp.where(iota((mols, 1), 0) == m, atom_counts[m], counts)
    lane = iota((mols, rows_all), 1)
    own = (lane // atoms == iota((mols, rows_all), 0)) & (lane % atoms < counts)
    bias_memory = wide(bias, 7, 4)
    zero = jnp.zeros((mols, width), F32)
    cell, mem_low, read_low = zero, zero.astype(BF16), zero.astype(BF16)
    kept = []
    for turn in range(ROUNDS):
        join = jnp.concatenate([mem_low, read_low, mem_low], axis=1)
        z = jnp.broadcast_to(bias_memory, (mols, 4 * width))
        if turn > 0:
            z = nn(join, memory_low[...]) + z
        i = jax.nn.sigmoid(z[:, :width])
        f = jax.nn.sigmoid(z[:, width : 2 * width])
        c = jnp.tanh(z[:, 2 * width : 3 * width])
        o = jax.nn.sigmoid(z[:, 3 * width :])
        before_cell = cell
        cell = f * cell + i * c
        squashed = jnp.tanh(cell)
        mem_low = (o * squashed).astype(BF16)
        scores = jnp.where(own, nt(mem_low, atom_low), -1000000000.0)
        weights = jnp.exp(scores - jnp.max(scores, axis=1, keepdims=True))
        inverse = 1.0 / jnp.sum(weights, axis=1, keepdims=True)
        read_low = (nn(weights.astype(BF16), atom_low) * inverse).astype(BF16)
        weights = weights * inverse
        weights_low = weights.astype(BF16)
        kept.append((join, i, f, c, o, before_cell, squashed, mem_low, weights, weights_low))
    join = jnp.concatenate([mem_low, read_low], axis=1)
    hidden_low = hidden_w[...].astype(BF16)
    padded[...] = jnp.zeros_like(padded)
    padded[0:n_targets, :] = final_w[...]
    padded[16:17, 0:n_targets] = bias[pl.ds(12 * WIDE, n_targets)].reshape(1, n_targets)
    bias_final = padded[16:17, :]
    final_low = jnp.where(iota((width, WIDE), 0) < n_targets, padded[0:width, :], 0.0).astype(BF16)
    before = nn(join, hidden_low) + wide(bias, 11, 1)
    squash = jax.nn.sigmoid(before)
    inner = before * squash
    inner_low = inner.astype(BF16)
    padded[width : width + mols, 0:n_targets] = targets[...]
    padded[width + mols : width + 2 * mols, 0:n_targets] = labels[...].astype(F32)
    label = padded[width + mols : width + 2 * mols, :]
    gap = nt(inner_low, final_low) + bias_final - padded[width : width + mols, :]
    loss = jnp.sum(label * gap * gap)
    present = jnp.sum(label)
    spot = iota((8, WIDE), 1)
    totals_all[place] = jnp.where(spot == 0, loss, jnp.where(spot == 1, present, 0.0))
    total_copies = [
        far_copy(0, k - 1, lax.rem(place + k, peers), totals_all.at[place], totals_all.at[place])
        for k in range(1, peers)
    ]
    d_pred = 2.0 * label * gap
    d_pred_low = d_pred.astype(BF16)
    head_part[plan.final_at : plan.final_at + 16, :] = tn(d_pred_low, inner_low)[0:16].astype(BF16)
    d_before = nn(d_pred_low, final_low) * (squash + inner * (1.0 - squash))
    d_before_low = d_before.astype(BF16)
    head_part[12 * width : 14 * width, :] = tn(join, d_before_low).astype(BF16)
    grad_bias[...] = jnp.zeros_like(grad_bias)
    grad_bias[11:12, :] = jnp.sum(d_before, axis=0, keepdims=True)
    grad_bias[12:13, :] = jnp.sum(d_pred, axis=0, keepdims=True)
    d_join = nt(d_before_low, hidden_low)
    d_mem, d_read = d_join[:, :width], d_join[:, width:]
    d_cell = zero
    d_bias = jnp.zeros((1, 4 * width), F32)
    lefts, rights, joins, d_gates = [], [], [], []
    for turn in reversed(range(ROUNDS)):
        join, i, f, c, o, before_cell, squashed, mem_low, weights, weights_low = kept[turn]
        d_read_low = d_read.astype(BF16)
        d_weights = nt(d_read_low, atom_low)
        d_scores = weights * (d_weights - jnp.sum(weights * d_weights, axis=1, keepdims=True))
        d_scores_low = d_scores.astype(BF16)
        d_mem = d_mem + nn(d_scores_low, atom_low)
        lefts += [weights_low, d_scores_low]
        rights += [d_read_low, mem_low]
        d_out = d_mem * squashed
        d_cell = d_cell + d_mem * o * (1.0 - squashed * squashed)
        d_z = jnp.concatenate(
            [
                d_cell * c * i * (1.0 - i),
                d_cell * before_cell * f * (1.0 - f),
                d_cell * i * (1.0 - c * c),
                d_out * o * (1.0 - o),
            ],
            axis=1,
        )
        d_cell = d_cell * f
        d_bias = d_bias + jnp.sum(d_z, axis=0, keepdims=True)
        d_z_low = d_z.astype(BF16)
        if turn > 0:
            joins.append(join)
            d_gates.append(d_z_low)
            d_join = nt(d_z_low, memory_low[...])
            d_mem = d_join[:, :width] + d_join[:, 2 * width :]
            d_read = d_join[:, width : 2 * width]
    grad_memory = tn(jnp.concatenate(joins, axis=0), jnp.concatenate(d_gates, axis=0)).astype(BF16)
    for i in range(4):
        head_part[i * 3 * width : (i + 1) * 3 * width, :] = grad_memory[:, i * width : (i + 1) * width]
    used = plan.final_at + 16
    head_part[used:, :] = jnp.zeros((ring * plan.head - used, WIDE), BF16)
    head_copies = []
    for k in range(1, peers):
        peer = lax.rem(place + k, peers)
        rows = rows16(me * plan.head + peer * plan.head_part, plan.head_part)
        head_copies.append(far_copy(1, k - 1, peer, head_part.at[rows, :], head_recv.at[k - 1]))
    for i in range(4):
        grad_bias[7 + i : 8 + i, :] = d_bias[:, i * width : (i + 1) * width]
    state_grad[...] = tn(jnp.concatenate(lefts, axis=0), jnp.concatenate(rights, axis=0))

    def gated_back(layer, g):
        bias_parts = [jnp.zeros((1, 3 * width), F32) for _ in range(2)]
        for j in range(2):
            rows = slice(g * span + j * span // 2, g * span + (j + 1) * span // 2)
            reset, update = gates[layer, 0, rows, :], gates[layer, 1, rows, :]
            candidate, third = gates[layer, 2, rows, :], gates[layer, 3, rows, :]
            old = states[rows, :].astype(F32) if layer == 0 else state[layer - 1, rows, :]
            grad = state_grad[rows, :]
            d_candidate = grad * (1.0 - update) * (1.0 - candidate * candidate)
            d_update = grad * (old - candidate) * update * (1.0 - update)
            d_reset = d_candidate * third * reset * (1.0 - reset)
            d_in = jnp.concatenate([d_reset, d_update, d_candidate], axis=1)
            d_hid = jnp.concatenate([d_reset, d_update, d_candidate * reset], axis=1)
            bias_parts[0] = bias_parts[0] + jnp.sum(d_in, axis=0, keepdims=True)
            bias_parts[1] = bias_parts[1] + jnp.sum(d_hid, axis=0, keepdims=True)
            d_in_low, d_hid_low = d_in.astype(BF16), d_hid.astype(BF16)
            gate_grad[layer, 0, rows, :] = d_in_low
            gate_grad[layer, 1, rows, :] = d_hid_low
            pulled[layer, rows, :] = nt(d_in_low, gated_low[0]).astype(BF16)
            if layer > 0:
                state_grad[rows, :] = grad * update + nt(d_hid_low, gated_low[1])
        for s in range(2):
            for i in range(3):
                at = 1 + 3 * s + i
                grad_bias[at : at + 1, :] += bias_parts[s][:, i * width : (i + 1) * width]

    def gated_weights_back(layer):
        low = states[...] if layer == 0 else state[layer - 1].astype(BF16)
        d_first = tn(gathered[layer], gate_grad[layer, 0])
        d_second = tn(low, gate_grad[layer, 1])
        if layer == LAYERS - 1:
            grad_gated[0], grad_gated[1] = d_first, d_second
        else:
            grad_gated[0] += d_first
            grad_gated[1] += d_second

    pick_t = one_hot(iota((half, width), 1) == me * local + iota((half, width), 0) // GROUP)
    pick_n = one_hot(iota((width, half), 0) == me * local + iota((width, half), 1) // GROUP)

    def message_back(layer, g):
        rows = slice(g * span, (g + 1) * span)
        wide_grad = jnp.where(same_mol_t, nt(pick_t, pulled[layer, rows, :]), 0.0).astype(BF16)

        def atoms_pair(ap, carry):
            columns = pl.ds(pl.multiple_of(ap * 2 * width, 2 * width), 2 * width)
            x = nn(wide_grad, sent[rows, columns])
            where = pl.ds(pl.multiple_of(layer * rows_all + g * span + ap * 16, 16), 16)
            for r in range(local):
                at = r * GROUP
                tile = jnp.concatenate([x[at : at + GROUP, :width], x[at : at + GROUP, width:]], axis=0)
                gt[where, r * width : (r + 1) * width] = tile.astype(BF16)
            return carry

        lax.fori_loop(0, atoms // 2, atoms_pair, 0, unroll=16)

    last = LAYERS - 1
    for layer in range(last, 0, -1):
        reducing, gathering = {}, {}
        for g in range(groups):
            gated_back(layer, g)
            message_back(layer, g)
            at = layer * rows_all + g * span
            back = nn(gt[at : at + span, :], edge_low[...]).astype(BF16)
            reduce_send[g * span : (g + 1) * span, :] = nn(order_back, back).astype(BF16)
            reducing[g] = []
            for k in range(1, ring):
                rows = rows16(g * span + lax.rem(me + k, ring) * block, block)
                stage = (LAYERS + 1) * groups + g
                reducing[g].append(row_copy(stage, k, reduce_send.at[rows, :], reduce_recv.at[g, k - 1]))
        gated_weights_back(layer)
        for g in range(groups):
            for copy in reducing[g]:
                copy.wait_recv()
            total = reduce_send[rows16(g * span + me * block, block), :].astype(F32)
            for k in range(ring - 1):
                total = total + reduce_recv[g, k].astype(F32)
            parcels[LAYERS * groups + g, me] = total.astype(BF16)
            gathering[g] = exchange(LAYERS * groups + g)
    rest_copies = []
    for g in range(groups):
        for copy in gathering[g]:
            copy.wait_recv()
        for j in range(ring):
            rows = slice(g * span + j * block, g * span + (j + 1) * block)
            state_grad[rows, :] += parcels[LAYERS * groups + g, j].astype(F32)
        gated_back(0, g)
        if g == groups - 1:
            gated_weights_back(0)
            for s in range(2):
                for i in range(3):
                    at = (s * 3 + i) * width
                    rest_full[at : at + width, :] = grad_gated[s, :, i * width : (i + 1) * width].astype(BF16)
            rest_full[plan.bias_at : plan.bias_at + 16, :] = grad_bias[...].astype(BF16)
            used = plan.bias_at + 16
            if ring * plan.rest_own > used:
                rest_full[used:, :] = jnp.zeros((ring * plan.rest_own - used, WIDE), BF16)
            rest_part[0 : plan.rest_own, :] = rest_full[rows16(me * plan.rest_own, plan.rest_own), :]
            if plan.rest > plan.rest_own:
                rest_part[plan.rest_own :, :] = jnp.zeros((plan.rest - plan.rest_own, WIDE), BF16)
            for k in range(1, peers):
                peer = lax.rem(place + k, peers)
                rows = rows16(peer * plan.rest_part, plan.rest_part)
                rest_copies.append(far_copy(4, k - 1, peer, rest_part.at[rows, :], rest_recv.at[k - 1]))
        message_back(0, g)

    for copy in head_copies:
        copy.wait_recv()
    mine = rows16(me * plan.head + place * plan.head_part, plan.head_part)
    total = head_part[mine, :].astype(F32)
    for k in range(peers - 1):
        total = total + head_recv[k].astype(F32)
    head_all[mine, :] = total.astype(BF16)
    head_copies[:] = [
        far_copy(2, k - 1, lax.rem(place + k, peers), head_all.at[mine, :], head_all.at[mine, :])
        for k in range(1, peers)
    ]

    lines = peers // 2
    line, side = lax.div(place, 2), lax.rem(place, 2)
    neighbour = line * 2 + 1 - side
    part = plan.edge_part
    stack = max(1, 2 * width // (2 * part))
    blocks = lines // stack
    home, seat = lax.div(line, stack), lax.rem(line, stack)

    def out_weights(start):
        columns = pl.ds(pl.multiple_of(start, 2 * width), 2 * width)
        edge_part[columns, :] = nn(turned_lows[...], gt[:, columns]).T.astype(BF16)

    def lines_of(j):
        return [lax.rem(home + j, blocks) * stack + lax.rem(seat + i, stack) for i in range(stack)]

    def scatter_near(j):
        copies = []
        if stack > 1:
            out_weights(lax.rem(home + j, blocks) * stack * 2 * part)
        for i, other in enumerate(lines_of(j)):
            if stack == 1:
                for step in range(part // (2 * width)):
                    out_weights(other * 2 * part + (1 - side) * part + step * 2 * width)
            rows = rows16(other * 2 * part + (1 - side) * part, part)
            copies.append(far_copy(7, j * stack + i, neighbour, edge_part.at[rows, :], near_recv.at[rows16(other * part, part), :]))
            if stack == 1:
                for step in range(part // (2 * width)):
                    out_weights(other * 2 * part + side * part + step * 2 * width)
        return copies

    edge_copies = []

    def scatter_far(j, copies):
        for i, other in enumerate(lines_of(j)):
            copies[i].wait_recv()
            rows = rows16(other * part, part)
            total = edge_part[rows16(other * 2 * part + side * part, part), :].astype(F32) + near_recv[rows, :].astype(F32)
            near_sum[rows, :] = total.astype(BF16)
            if j > 0 or i > 0:
                k = j if stack == 1 else lax.rem(other - line + lines, lines)
                edge_copies.append(far_copy(3, k - 1, other * 2 + side, near_sum.at[rows, :], edge_recv.at[k - 1]))

    order_of = [*range(1, blocks), 0]
    near_copies = [(j, scatter_near(j)) for j in order_of]

    def pair_grads(g):
        wide_grad = jnp.concatenate(
            [
                jnp.where(same_mol, nn(pulled[layer, g * span : (g + 1) * span, :], pick_n), 0.0).astype(BF16)
                for layer in range(LAYERS)
            ],
            axis=1,
        )

        def pair_back(ap, carry):
            columns = pl.ds(pl.multiple_of(ap * 2 * width, 2 * width), 2 * width)
            x = nn(wide_grad, turned[g * LAYERS * half : (g + 1) * LAYERS * half, columns]).astype(BF16)
            for s in range(2):
                where = pl.ds(pl.multiple_of((ap * 2 + s) * atoms, atoms), atoms)
                for m in range(GROUP):
                    pair_grad[g * GROUP + m, where, :] = x[m * atoms : (m + 1) * atoms, s * width : (s + 1) * width]
            return carry

        lax.fori_loop(0, atoms // 2, pair_back, 0, unroll=8)

    for g in range(groups - 1):
        pair_grads(g)
    for waiting in near_copies:
        scatter_far(*waiting)
    for copy in rest_copies:
        copy.wait_recv()
    mine = rows16(place * plan.rest_part, plan.rest_part)
    total = rest_part[mine, :].astype(F32)
    for k in range(peers - 1):
        total = total + rest_recv[k].astype(F32)
    rest_all[me, mine, :] = total.astype(BF16)
    rest_copies = [
        far_copy(6, k - 1, lax.rem(place + k, peers), rest_all.at[me, mine, :], rest_all.at[me, mine, :])
        for k in range(1, peers)
    ]
    for copy in head_copies:
        copy.wait_recv()
    rows = rows16(me * plan.head, plan.head)
    head_rows = [row_copy((LAYERS + 2) * groups, k, head_all.at[rows, :], head_all.at[rows, :]) for k in range(1, ring)]
    pair_grads(groups - 1)

    for copy in edge_copies:
        copy.wait_recv()
    pieces = plan.pieces
    size = part // pieces
    stores = []

    def store(source_ref, target_ref):
        copy = pltpu.make_async_copy(source_ref, target_ref, store_sem.at[len(stores)])
        copy.start()
        stores.append(copy)

    across, beside = {}, {}
    for p in range(pieces):
        own = rows16(line * part + p * size, size)
        mine = rows16(place * part + p * size, size)
        total = near_sum[own, :].astype(F32)
        for k in range(lines - 1):
            total = total + edge_recv[k, p * size : (p + 1) * size, :].astype(F32)
        edge_all[mine, :] = total.astype(BF16)
        for k in range(1, lines):
            peer = lax.rem(line + k, lines) * 2 + side
            across[p, k] = far_copy(5, p * peers + k, peer, edge_all.at[mine, :], edge_all.at[mine, :])
        beside[p, 0] = far_copy(5, p * peers, neighbour, edge_all.at[mine, :], edge_all.at[mine, :])

    def onward(p):
        for k in range(1, lines):
            across[p, k].wait_recv()
            rows = rows16((lax.rem(line - k + lines, lines) * 2 + side) * part + p * size, size)
            beside[p, k] = far_copy(5, p * peers + lines + k, neighbour, edge_all.at[rows, :], edge_all.at[rows, :])
            store(edge_all.at[rows, :], edge_sum.at[rows, :])

    lane_pair = iota((edges // 2, atoms * atoms), 1).astype(F32)
    total_bias = jnp.zeros((8, width), F32)
    for m in range(mols):
        if m == mols // 2:
            for copy in rest_copies:
                copy.wait_recv()
            rest_rows = [row_copy((LAYERS + 2) * groups + 1, k, rest_all.at[me], rest_all.at[me]) for k in range(1, ring)]
        for i in range(2):
            rows = slice(i * edges // 2, (i + 1) * edges // 2)
            d_first = nn(one_hot(lane_pair == pair_cols[rows, m : m + 1]), pair_grad[m]) * slope[m, rows, :]
            total_bias = total_bias + jnp.sum(d_first.reshape(edges // 16, 8, width), axis=0)
            first_grad[m * edges + i * edges // 2 : m * edges + (i + 1) * edges // 2, :] = d_first.astype(BF16)
    total_in = nn(jnp.concatenate([feats[m] for m in range(mols)], axis=1), first_grad[...])
    total_bias = jnp.sum(total_bias, axis=0, keepdims=True)
    first_row[me, 0:features, :] = total_in
    first_row[me, features : features + 8, :] = jnp.broadcast_to(total_bias, (8, width))
    first_copies = [row_copy((LAYERS + 2) * groups + 2, k, first_row.at[me], first_row.at[me]) for k in range(1, ring)]
    onward(0)
    for copy in first_copies:
        copy.wait_recv()
    total = first_row[0]
    for q in range(1, ring):
        total = total + first_row[q]
    first_mol[place] = total
    first_copies = [
        far_copy(8, k - 1, lax.rem(place + k, peers), first_mol.at[place], first_mol.at[place])
        for k in range(1, peers)
    ]
    for p in range(1, pieces):
        onward(p)

    for copy in head_rows:
        copy.wait_recv()
    store(head_all, head_sum)
    for copy in rest_rows:
        copy.wait_recv()
    store(rest_all, rest_sum)
    for copy in total_copies + first_copies:
        copy.wait_recv()
    total, total_first = totals_all[0], first_mol[0]
    for k in range(1, peers):
        total = total + totals_all[k]
        total_first = total_first + first_mol[k]
    totals[0:8, :] = total
    totals[8:, :] = total_first
    for p in range(pieces):
        rows = rows16(place * part + p * size, size)
        store(edge_all.at[rows, :], edge_sum.at[rows, :])
        for k in range(lines):
            beside[p, k].wait_recv()
            rows = rows16((lax.rem(line - k + lines, lines) * 2 + 1 - side) * part + p * size, size)
            store(edge_all.at[rows, :], edge_sum.at[rows, :])
    for copy in started:
        copy.wait_send()
    for copy in stores:
        copy.wait()


def adamw(weight, first, second, grad, rate):
    first_new = BETA_ONE * first + (1.0 - BETA_ONE) * grad
    second_new = BETA_TWO * second + (1.0 - BETA_TWO) * grad * grad
    scaled = jnp.sqrt(second_new * (1.0 / (1.0 - BETA_TWO**STEP))) + EPSILON
    weight_new = (1.0 - rate * DECAY) * weight - (rate / (1.0 - BETA_ONE**STEP)) * first_new / scaled
    return (weight_new, first_new, second_new, weight_new.astype(BF16))


PIECES = 2


def update_kernel(ring, peers, local, counted, totals, edge_far, head_far, rest_far, *refs):
    fars, refs = refs[:21], refs[21:]
    (loss_out, count_out), refs = refs[:2], refs[2:]
    outs, refs = refs[:28], refs[28:]
    (edge_sum, head_sum, rest_sum), refs = refs[:3], refs[3:]
    olds, refs = refs[:21], refs[21:]
    news, (fetch_sem, store_sem) = refs[:28], refs[28:]
    features, width = olds[0].shape
    n_bias = olds[18].shape[0]
    plan = Plan(ring, peers, width, local)
    every = slice(None)
    columns = plan.edge // PIECES
    cuts = [(every, pl.ds(i * columns, columns)) for i in range(PIECES)]
    count = [0, 0]

    def copies_of(sides, sem, which):
        made = []
        for source_ref, target_ref in sides:
            made.append(pltpu.make_async_copy(source_ref, target_ref, sem.at[count[which]]))
            made[-1].start()
            count[which] += 1
        return made

    def fetch(index, cut=None):
        where = range(3 * index, 3 * index + 3)
        return copies_of([(fars[i], olds[i]) if cut is None else (fars[i].at[cut], olds[i].at[cut]) for i in where], fetch_sem, 0)

    def store(index, cut=None):
        where = range(4 * index, 4 * index + 4)
        return copies_of([(news[i], outs[i]) if cut is None else (news[i].at[cut], outs[i].at[cut]) for i in where], store_sem, 1)

    edge_ready = copies_of([(edge_far, edge_sum)], fetch_sem, 0)
    cut_ready = [fetch(1, cut) for cut in cuts]
    head_ready = copies_of([(head_far, head_sum)], fetch_sem, 0)
    ready = {index: fetch(index) for index in (3, 4, 5)}
    rest_ready = copies_of([(rest_far, rest_sum)], fetch_sem, 0)
    ready.update({index: fetch(index) for index in (2, 0, 6)})
    loss_out[0] = counted[0, 0]
    count_out[0] = counted[0, 1]
    inverse = (1.0 / totals[0:1, :])[0:1, 1:2]

    def update(index, view, grad):
        parts = [ref[view] for ref in olds[3 * index : 3 * index + 3]]
        for ref, value in zip(news[4 * index : 4 * index + 4], adamw(*parts, grad, RATES[index])):
            ref[view] = value

    def wait(copies):
        for copy in copies:
            copy.wait()

    stored = []
    wait(edge_ready)
    for p in range(PIECES):
        wait(cut_ready[p])
        for i in range(p * columns // width, (p + 1) * columns // width):
            grad = edge_sum[i * width : (i + 1) * width, :].astype(F32) * inverse
            update(1, (every, slice(i * width, (i + 1) * width)), grad)
        stored += store(1, cuts[p])
    wait(head_ready + ready[3])
    for i in range(4):
        grad = head_sum[i * 3 * width : (i + 1) * 3 * width, :].astype(F32) * inverse
        update(3, (every, slice(i * width, (i + 1) * width)), grad)
    stored += store(3)
    wait(rest_ready + ready[2])
    for s in range(2):
        for i in range(3):
            at, end = (s * 3 + i) * width, (s * 3 + i + 1) * width
            while at < end:
                q, low = divmod(at, plan.rest_own)
                rows = min(end - at, plan.rest_own - low)
                first = at - (s * 3 + i) * width
                grad = rest_sum[q, low : low + rows, :].astype(F32) * inverse
                update(2, (s, slice(first, first + rows), slice(i * width, (i + 1) * width)), grad)
                at += rows
    stored += store(2)
    wait(ready[4])
    update(4, (every, every), head_sum[12 * width : 14 * width, :].astype(F32) * inverse)
    stored += store(4)
    wait(ready[5])
    n_targets = olds[15].shape[0]
    update(5, (every, every), (head_sum[plan.final_at : plan.final_at + 16, :].astype(F32) * inverse)[0:n_targets])
    stored += store(5)
    own = totals[8:, :] * inverse
    wait(ready[0])
    update(0, (every, every), own[0:features])
    stored += store(0)
    q, low = divmod(plan.bias_at, plan.rest_own)
    biases = rest_sum[q, low : low + 16, :].astype(F32) * inverse
    wait(ready[6])
    for i in range(-(-n_bias // WIDE)):
        size = min(WIDE, n_bias - i * WIDE)
        grad = (own[features : features + 1] if i == 0 else biases[i : i + 1])[:, 0:size]
        update(6, pl.ds(i * WIDE, size), grad.reshape(size))
    stored += store(6)
    wait(stored)


def shards(
    edge_feats,
    edge_source,
    edge_target,
    atom_counts,
    edge_counts,
    atom_states,
    targets,
    label_mask,
    edge_input,
    edge_input_first,
    edge_input_second,
    edge_output,
    edge_output_first,
    edge_output_second,
    gated_weights,
    gated_first,
    gated_second,
    memory_weights,
    memory_first,
    memory_second,
    readout_hidden,
    readout_hidden_first,
    readout_hidden_second,
    readout_final,
    readout_final_first,
    readout_final_second,
    bias_vector,
    bias_first,
    bias_second,
):
    mols, edges, features = edge_feats.shape
    atoms, width = atom_states.shape[1:]
    ring = lax.axis_size("row")
    local = width // ring
    rows_all = mols * atoms
    block = GROUP * atoms // ring
    groups = mols // GROUP
    peers = lax.axis_size("mol")
    plan = Plan(ring, peers, width, local)

    finals = [value.T for value in (readout_final, readout_final_first, readout_final_second)]
    vmem = pl.BlockSpec(memory_space=pltpu.VMEM)
    smem = pl.BlockSpec(memory_space=pltpu.SMEM)
    far = pl.BlockSpec(memory_space=pl.ANY)
    shape = jax.ShapeDtypeStruct
    edge_sum, head_sum, rest_sum, totals = pl.pallas_call(
        functools.partial(step_kernel, ring, peers),
        out_shape=[
            shape((plan.edge, WIDE), BF16),
            shape((ring * plan.head, WIDE), BF16),
            shape((ring, plan.rest, WIDE), BF16),
            shape((8 + features + 8, WIDE), F32),
        ],
        in_specs=[smem, smem] + [vmem] * 9 + [far] * 4,
        out_specs=[far] * 3 + [vmem],
        scratch_shapes=[
            pltpu.VMEM((local * width, width), BF16),
            pltpu.VMEM((mols, edges), jnp.int32),
            pltpu.VMEM((edges, mols), F32),
            pltpu.VMEM((rows_all, atoms * width), BF16),
            pltpu.VMEM((mols // GROUP * LAYERS * GROUP * local, atoms * width), BF16),
            pltpu.VMEM((mols, edges, width), F32),
            pltpu.VMEM((mols, atoms * atoms, width), BF16),
            pltpu.VMEM((width, LAYERS * rows_all), BF16),
            pltpu.VMEM((LAYERS, rows_all, width), BF16),
            pltpu.VMEM((LAYERS, 4, rows_all, width), F32),
            pltpu.VMEM((LAYERS, rows_all, width), F32),
            pltpu.VMEM((rows_all, width), F32),
            pltpu.VMEM((LAYERS, 2, rows_all, 3 * width), BF16),
            pltpu.VMEM((LAYERS, rows_all, width), BF16),
            pltpu.VMEM((3 * width, 4 * width), BF16),
            pltpu.VMEM((width + 2 * mols, WIDE), F32),
            pltpu.VMEM(((LAYERS + 1) * groups, ring, block, WIDE), BF16),
            pltpu.VMEM((rows_all, width), BF16),
            pltpu.VMEM((groups, ring - 1, block, width), BF16),
            pltpu.VMEM((2, width, 3 * width), F32),
            pltpu.VMEM((16, WIDE), F32),
            pltpu.VMEM((peers, 8, WIDE), F32),
            pltpu.VMEM((plan.edge, WIDE), BF16),
            pltpu.VMEM((peers // 2 - 1, plan.edge_part, WIDE), BF16),
            pltpu.VMEM((plan.edge, WIDE), BF16),
            pltpu.VMEM((ring * plan.head, WIDE), BF16),
            pltpu.VMEM((peers - 1, plan.head_part, WIDE), BF16),
            pltpu.VMEM((ring * plan.head, WIDE), BF16),
            pltpu.VMEM((ring * plan.rest_own, WIDE), BF16),
            pltpu.VMEM((plan.rest, WIDE), BF16),
            pltpu.VMEM((peers - 1, plan.rest_part, WIDE), BF16),
            pltpu.VMEM((ring, plan.rest, WIDE), BF16),
            pltpu.SemaphoreType.DMA(((LAYERS + 2) * groups + 3, ring - 1)),
            pltpu.SemaphoreType.DMA(((LAYERS + 2) * groups + 3, ring - 1)),
            pltpu.SemaphoreType.DMA((plan.stages[9],)),
            pltpu.SemaphoreType.DMA((plan.stages[9],)),
            pltpu.VMEM((LAYERS * rows_all, local * width), BF16),
            pltpu.VMEM(edge_output.shape, F32),
            pltpu.VMEM(gated_weights.shape, F32),
            pltpu.VMEM(memory_weights.shape, F32),
            pltpu.VMEM(readout_hidden.shape, F32),
            pltpu.SemaphoreType.DMA((4,)),
            pltpu.SemaphoreType.DMA((2 + plan.pieces * peers,)),
            pltpu.VMEM((peers // 2 * plan.edge_part, WIDE), BF16),
            pltpu.VMEM((peers // 2 * plan.edge_part, WIDE), BF16),
            pltpu.VMEM((ring, features + 8, WIDE), F32),
            pltpu.VMEM((peers, features + 8, WIDE), F32),
            pltpu.VMEM((mols * edges, width), BF16),
        ],
        compiler_params=pltpu.CompilerParams(
            collective_id=0, has_side_effects=True, vmem_limit_bytes=60 * 1024 * 1024
        ),
    )(
        atom_counts,
        edge_counts,
        jnp.swapaxes(edge_feats, 1, 2),
        edge_source,
        edge_target,
        atom_states.reshape(rows_all, width),
        targets,
        label_mask,
        edge_input,
        finals[0],
        bias_vector,
        edge_output,
        gated_weights,
        memory_weights,
        readout_hidden,
    )
    olds = [edge_input, edge_input_first, edge_input_second, edge_output, edge_output_first, edge_output_second]
    olds += [gated_weights, gated_first, gated_second, memory_weights, memory_first, memory_second]
    olds += [readout_hidden, readout_hidden_first, readout_hidden_second] + finals
    olds += [bias_vector, bias_first, bias_second]
    news = [shape(olds[3 * index].shape, kind) for index in range(7) for kind in (F32, F32, F32, BF16)]
    sums = [edge_sum, head_sum, rest_sum]
    outs = pl.pallas_call(
        functools.partial(update_kernel, ring, peers, local),
        out_shape=[shape((1,), F32)] * 2 + news,
        in_specs=[smem, vmem] + [far] * 24,
        out_specs=[smem] * 2 + [far] * 28,
        scratch_shapes=[pltpu.VMEM(value.shape, value.dtype) for value in sums + olds + news]
        + [pltpu.SemaphoreType.DMA((3 + 18 + 3 * PIECES,)), pltpu.SemaphoreType.DMA((24 + 4 * PIECES,))],
        compiler_params=pltpu.CompilerParams(vmem_limit_bytes=60 * 1024 * 1024),
    )(totals, totals, *sums, *olds)
    outs = list(outs)
    outs[0], outs[1] = outs[0].reshape(()), outs[1].reshape(())
    outs[22:26] = [value.T for value in outs[22:26]]
    return tuple(outs)


def solution(mesh):
    cut = P(None, "row")
    per_mol = (P("mol", None, None), P("mol", None), P("mol", None), P("mol"), P("mol"), P("mol", None, None))
    per_mol += (P("mol", None), P("mol", None))
    return jax.shard_map(
        shards,
        mesh=mesh,
        in_specs=per_mol + (P(),) * 3 + (cut,) * 3 + (P(),) * 15,
        out_specs=(P(),) * 6 + (cut,) * 4 + (P(),) * 20,
        check_vma=False,
    )
```

```python
import functools

import jax
import jax.numpy as jnp
from jax import lax
from jax.experimental import pallas as pl
from jax.experimental.pallas import tpu as pltpu
from jax.sharding import PartitionSpec as P

LAYERS = 2
ROUNDS = 6
STEP = 10
BETA_ONE = 0.9
BETA_TWO = 0.999
EPSILON = 1e-08
DECAY = 0.01
RATES = (0.25, 0.004, 0.09, 0.05, 0.06, 0.09, 0.2)

MESH = pl.DeviceIdType.MESH
F32 = jnp.float32
BF16 = jnp.bfloat16
GROUP = 8
WIDE = 128


def nn(left, right):
    return lax.dot_general(left, right, (((1,), (0,)), ((), ())), preferred_element_type=F32)


def nt(left, right):
    return lax.dot_general(left, right, (((1,), (1,)), ((), ())), preferred_element_type=F32)


def tn(left, right):
    return lax.dot_general(left, right, (((0,), (0,)), ((), ())), preferred_element_type=F32)


def iota(shape, dim):
    return lax.broadcasted_iota(jnp.int32, shape, dim)


def one_hot(condition):
    return jnp.where(condition, 1.0, 0.0).astype(BF16)


def wide(bias_ref, first, count):
    return bias_ref[pl.ds(first * WIDE, count * WIDE)].reshape(1, count * WIDE)


def round_up(value, unit):
    return -(-value // unit) * unit


class Plan:
    def __init__(self, ring, peers, width, local):
        unit = 16 * peers
        self.edge = local * width
        self.edge_part = self.edge // peers
        self.final_at = 12 * width + 2 * width
        self.head = round_up(-(-(self.final_at + 16) // ring), unit)
        self.head_part = self.head // peers
        self.bias_at = 6 * width
        self.rest_own = round_up(-(-(self.bias_at + 16) // ring), 16)
        self.rest = round_up(self.rest_own, unit)
        self.rest_part = self.rest // peers
        self.pieces = 2 if self.edge_part >= WIDE else 1
        sizes = [peers - 1] * 9
        sizes[3], sizes[5], sizes[7] = peers // 2 - 1, self.pieces * peers, peers // 2
        self.stages = [sum(sizes[:stage]) for stage in range(10)]


def step_kernel(
    ring,
    peers,
    atom_counts,
    edge_counts,
    feats,
    source,
    target,
    states,
    targets,
    labels,
    edge_in,
    final_w,
    bias,
    edge_far,
    gated_far,
    memory_far,
    hidden_far,
    edge_sum,
    head_sum,
    rest_sum,
    totals,
    edge_low,
    pairs,
    pair_cols,
    sent,
    turned,
    slope,
    pair_grad,
    turned_lows,
    gathered,
    gates,
    state,
    state_grad,
    gate_grad,
    pulled,
    memory_low,
    padded,
    parcels,
    reduce_send,
    reduce_recv,
    grad_gated,
    grad_bias,
    totals_all,
    edge_part,
    edge_recv,
    edge_all,
    head_part,
    head_recv,
    head_all,
    rest_full,
    rest_part,
    rest_recv,
    rest_all,
    send_sem,
    recv_sem,
    far_send,
    far_recv,
    gt,
    edge_out,
    gated,
    memory,
    hidden_w,
    fetch_sem,
    store_sem,
    near_recv,
    near_sum,
    first_row,
    first_mol,
    first_grad,
):
    mols, features, edges = feats.shape
    rows_all, width = states.shape
    atoms = rows_all // mols
    local = width // ring
    groups = mols // GROUP
    span = GROUP * atoms
    half = GROUP * local
    block = span // ring
    n_targets = targets.shape[1]
    me = lax.axis_index("row")
    place = lax.axis_index("mol")
    plan = Plan(ring, peers, width, local)
    started = []
    fetches = [
        pltpu.make_async_copy(far, near, fetch_sem.at[i])
        for i, (far, near) in enumerate(
            ((edge_far, edge_out), (gated_far, gated), (memory_far, memory), (hidden_far, hidden_w))
        )
    ]
    for copy in fetches:
        copy.start()

    def rows16(start, count):
        return pl.ds(pl.multiple_of(start, 16), count)

    def far_copy(stage, index, peer, source_ref, target_ref):
        index += plan.stages[stage]
        copy = pltpu.make_async_remote_copy(
            src_ref=source_ref,
            dst_ref=target_ref,
            send_sem=far_send.at[index],
            recv_sem=far_recv.at[index],
            device_id={"mol": peer},
            device_id_type=MESH,
        )
        copy.start()
        started.append(copy)
        return copy

    def row_copy(stage, k, source_ref, target_ref):
        copy = pltpu.make_async_remote_copy(
            src_ref=source_ref,
            dst_ref=target_ref,
            send_sem=send_sem.at[stage, k - 1],
            recv_sem=recv_sem.at[stage, k - 1],
            device_id={"row": lax.rem(me + k, ring)},
            device_id_type=MESH,
        )
        copy.start()
        started.append(copy)
        return copy

    barrier = pltpu.get_barrier_semaphore()
    for k in range(1, ring):
        pl.semaphore_signal(barrier, inc=1, device_id={"row": lax.rem(me + k, ring)}, device_id_type=MESH)
    for k in range(1, peers):
        pl.semaphore_signal(barrier, inc=1, device_id={"mol": lax.rem(place + k, peers)}, device_id_type=MESH)

    low_in = edge_in[...].astype(BF16)

    lane_edge = iota((1, edges), 1)
    row_index = iota((atoms * atoms, edges), 0)
    for m in range(mols):
        pairs[m : m + 1, :] = jnp.where(
            lane_edge < edge_counts[m], source[m : m + 1, :] * atoms + target[m : m + 1, :], -1
        )
    pair_cols[...] = pairs[...].astype(F32).T

    bias_first = wide(bias, 0, 1)

    def edge_network(m, carry):
        before = tn(feats[m], low_in) + bias_first
        squash = jax.nn.sigmoid(before)
        act = before * squash
        slope[m] = squash + act * (1.0 - squash)
        act = act.astype(BF16)
        pair = pairs[pl.ds(m, 1), :]
        rows = pl.ds(pl.multiple_of(m * atoms, atoms), atoms)
        sums = nn(one_hot(row_index == pair), act).astype(BF16)
        for a in range(atoms):
            sent[rows, a * width : (a + 1) * width] = sums[a * atoms : (a + 1) * atoms]
        return carry

    lax.fori_loop(0, mols, edge_network, 0, unroll=4)

    order = one_hot(
        (iota((span, span), 1) // atoms == iota((span, span), 0) % GROUP)
        & (iota((span, span), 1) % atoms == iota((span, span), 0) // GROUP)
    )
    order_back = one_hot(
        (iota((span, span), 0) // atoms == iota((span, span), 1) % GROUP)
        & (iota((span, span), 0) % atoms == iota((span, span), 1) // GROUP)
    )
    same_mol = iota((span, half), 0) // atoms == iota((span, half), 1) % GROUP
    same_mol_t = iota((half, span), 0) % GROUP == iota((half, span), 1) // atoms

    def state_low(layer, rows):
        if layer == 0:
            return states[rows, :]
        return state[layer - 1, rows, :].astype(BF16)

    def message(layer, g):
        rows = slice(g * span, (g + 1) * span)
        low_p = nn(order, state_low(layer, rows)).astype(BF16)
        at = layer * rows_all + g * span
        turned_lows[:, at : at + span] = low_p.astype(F32).T.astype(BF16)
        base = (g * LAYERS + layer) * half

        def rows_pair(rp, carry):
            t = nt(low_p, edge_low[pl.ds(pl.multiple_of(rp * 2 * width, 2 * width), 2 * width), :])
            where = pl.ds(pl.multiple_of(base + rp * 16, 16), 16)
            for a in range(atoms):
                at = a * GROUP
                tile = jnp.concatenate([t[at : at + GROUP, :width], t[at : at + GROUP, width:]], axis=0)
                turned[where, a * width : (a + 1) * width] = tile.astype(BF16)
            return carry

        lax.fori_loop(0, local // 2, rows_pair, 0, unroll=16)
        u = nt(sent[rows, :], turned[base : base + half, :])
        u = jnp.where(same_mol, u, 0.0).astype(BF16)
        packed = jnp.zeros((block, WIDE), F32)
        for j in range(ring):
            pick = one_hot(iota((half, WIDE), 1) == j * local + iota((half, WIDE), 0) // GROUP)
            packed = packed + nn(u[j * block : (j + 1) * block], pick)
        parcels[layer * groups + g, me] = packed.astype(BF16)

    def exchange(stage):
        return [row_copy(stage, k, parcels.at[stage, me], parcels.at[stage, me]) for k in range(1, ring)]

    def gated_step(layer, g):
        stage = layer * groups + g
        joined = jnp.concatenate([parcels[stage, q] for q in range(ring)], axis=1)
        for j in range(0, ring, 2):
            parts = []
            for i in (j, j + 1):
                row, column = iota((ring * WIDE, width), 0), iota((ring * WIDE, width), 1)
                pick = one_hot(
                    (row % WIDE // local == i) & (row // WIDE == column // local) & (row % local == column % local)
                )
                parts.append(nn(joined, pick))
            rows = slice(g * span + j * block, g * span + (j + 2) * block)
            got = jnp.concatenate(parts, axis=0).astype(BF16)
            gathered[layer, rows, :] = got
            old = states[rows, :].astype(F32) if layer == 0 else state[layer - 1, rows, :]
            gate_in = nn(got, gated_low[0]) + bias_in
            gate_hid = nn(state_low(layer, rows), gated_low[1]) + bias_hid
            reset = jax.nn.sigmoid(gate_in[:, :width] + gate_hid[:, :width])
            update = jax.nn.sigmoid(gate_in[:, width : 2 * width] + gate_hid[:, width : 2 * width])
            third = gate_hid[:, 2 * width :]
            candidate = jnp.tanh(gate_in[:, 2 * width :] + reset * third)
            gates[layer, 0, rows, :] = reset
            gates[layer, 1, rows, :] = update
            gates[layer, 2, rows, :] = candidate
            gates[layer, 3, rows, :] = third
            state[layer, rows, :] = (1.0 - update) * candidate + update * old

    for copy in fetches:
        copy.wait()
    memory_low[...] = memory[...].astype(BF16)
    for r in range(local):
        edge_low[r * width : (r + 1) * width, :] = edge_out[:, r * width : (r + 1) * width].astype(BF16)
    gated_low = [gated[i].astype(BF16) for i in range(2)]
    bias_in = wide(bias, 1, 3)
    bias_hid = wide(bias, 4, 3)
    flying = {}
    for g in range(groups):
        message(0, g)
        if g == 0:
            pl.semaphore_wait(barrier, ring + peers - 2)
        flying[0, g] = exchange(g)
    for layer in range(LAYERS):
        for g in range(groups):
            for copy in flying[layer, g]:
                copy.wait_recv()
            gated_step(layer, g)
            if layer + 1 < LAYERS:
                message(layer + 1, g)
                flying[layer + 1, g] = exchange((layer + 1) * groups + g)

    atom_low = state[LAYERS - 1].astype(BF16)
    counts = jnp.zeros((mols, 1), jnp.int32)
    for m in range(mols):
        counts = jnp.where(iota((mols, 1), 0) == m, atom_counts[m], counts)
    lane = iota((mols, rows_all), 1)
    own = (lane // atoms == iota((mols, rows_all), 0)) & (lane % atoms < counts)
    bias_memory = wide(bias, 7, 4)
    zero = jnp.zeros((mols, width), F32)
    cell, mem_low, read_low = zero, zero.astype(BF16), zero.astype(BF16)
    kept = []
    for turn in range(ROUNDS):
        join = jnp.concatenate([mem_low, read_low, mem_low], axis=1)
        z = jnp.broadcast_to(bias_memory, (mols, 4 * width))
        if turn > 0:
            z = nn(join, memory_low[...]) + z
        i = jax.nn.sigmoid(z[:, :width])
        f = jax.nn.sigmoid(z[:, width : 2 * width])
        c = jnp.tanh(z[:, 2 * width : 3 * width])
        o = jax.nn.sigmoid(z[:, 3 * width :])
        before_cell = cell
        cell = f * cell + i * c
        squashed = jnp.tanh(cell)
        mem_low = (o * squashed).astype(BF16)
        scores = jnp.where(own, nt(mem_low, atom_low), -1000000000.0)
        weights = jnp.exp(scores - jnp.max(scores, axis=1, keepdims=True))
        inverse = 1.0 / jnp.sum(weights, axis=1, keepdims=True)
        read_low = (nn(weights.astype(BF16), atom_low) * inverse).astype(BF16)
        weights = weights * inverse
        weights_low = weights.astype(BF16)
        kept.append((join, i, f, c, o, before_cell, squashed, mem_low, weights, weights_low))
    join = jnp.concatenate([mem_low, read_low], axis=1)
    hidden_low = hidden_w[...].astype(BF16)
    padded[...] = jnp.zeros_like(padded)
    padded[0:n_targets, :] = final_w[...]
    padded[16:17, 0:n_targets] = bias[pl.ds(12 * WIDE, n_targets)].reshape(1, n_targets)
    bias_final = padded[16:17, :]
    final_low = jnp.where(iota((width, WIDE), 0) < n_targets, padded[0:width, :], 0.0).astype(BF16)
    before = nn(join, hidden_low) + wide(bias, 11, 1)
    squash = jax.nn.sigmoid(before)
    inner = before * squash
    inner_low = inner.astype(BF16)
    padded[width : width + mols, 0:n_targets] = targets[...]
    padded[width + mols : width + 2 * mols, 0:n_targets] = labels[...].astype(F32)
    label = padded[width + mols : width + 2 * mols, :]
    gap = nt(inner_low, final_low) + bias_final - padded[width : width + mols, :]
    loss = jnp.sum(label * gap * gap)
    present = jnp.sum(label)
    spot = iota((8, WIDE), 1)
    totals_all[place] = jnp.where(spot == 0, loss, jnp.where(spot == 1, present, 0.0))
    total_copies = [
        far_copy(0, k - 1, lax.rem(place + k, peers), totals_all.at[place], totals_all.at[place])
        for k in range(1, peers)
    ]
    d_pred = 2.0 * label * gap
    d_pred_low = d_pred.astype(BF16)
    head_part[plan.final_at : plan.final_at + 16, :] = tn(d_pred_low, inner_low)[0:16].astype(BF16)
    d_before = nn(d_pred_low, final_low) * (squash + inner * (1.0 - squash))
    d_before_low = d_before.astype(BF16)
    head_part[12 * width : 14 * width, :] = tn(join, d_before_low).astype(BF16)
    grad_bias[...] = jnp.zeros_like(grad_bias)
    grad_bias[11:12, :] = jnp.sum(d_before, axis=0, keepdims=True)
    grad_bias[12:13, :] = jnp.sum(d_pred, axis=0, keepdims=True)
    d_join = nt(d_before_low, hidden_low)
    d_mem, d_read = d_join[:, :width], d_join[:, width:]
    d_cell = zero
    d_bias = jnp.zeros((1, 4 * width), F32)
    lefts, rights, joins, d_gates = [], [], [], []
    for turn in reversed(range(ROUNDS)):
        join, i, f, c, o, before_cell, squashed, mem_low, weights, weights_low = kept[turn]
        d_read_low = d_read.astype(BF16)
        d_weights = nt(d_read_low, atom_low)
        d_scores = weights * (d_weights - jnp.sum(weights * d_weights, axis=1, keepdims=True))
        d_scores_low = d_scores.astype(BF16)
        d_mem = d_mem + nn(d_scores_low, atom_low)
        lefts += [weights_low, d_scores_low]
        rights += [d_read_low, mem_low]
        d_out = d_mem * squashed
        d_cell = d_cell + d_mem * o * (1.0 - squashed * squashed)
        d_z = jnp.concatenate(
            [
                d_cell * c * i * (1.0 - i),
                d_cell * before_cell * f * (1.0 - f),
                d_cell * i * (1.0 - c * c),
                d_out * o * (1.0 - o),
            ],
            axis=1,
        )
        d_cell = d_cell * f
        d_bias = d_bias + jnp.sum(d_z, axis=0, keepdims=True)
        d_z_low = d_z.astype(BF16)
        if turn > 0:
            joins.append(join)
            d_gates.append(d_z_low)
            d_join = nt(d_z_low, memory_low[...])
            d_mem = d_join[:, :width] + d_join[:, 2 * width :]
            d_read = d_join[:, width : 2 * width]
    grad_memory = tn(jnp.concatenate(joins, axis=0), jnp.concatenate(d_gates, axis=0)).astype(BF16)
    for i in range(4):
        head_part[i * 3 * width : (i + 1) * 3 * width, :] = grad_memory[:, i * width : (i + 1) * width]
    used = plan.final_at + 16
    head_part[used:, :] = jnp.zeros((ring * plan.head - used, WIDE), BF16)
    head_copies = []
    for k in range(1, peers):
        peer = lax.rem(place + k, peers)
        rows = rows16(me * plan.head + peer * plan.head_part, plan.head_part)
        head_copies.append(far_copy(1, k - 1, peer, head_part.at[rows, :], head_recv.at[k - 1]))
    for i in range(4):
        grad_bias[7 + i : 8 + i, :] = d_bias[:, i * width : (i + 1) * width]
    state_grad[...] = tn(jnp.concatenate(lefts, axis=0), jnp.concatenate(rights, axis=0))

    def gated_back(layer, g):
        bias_parts = [jnp.zeros((1, 3 * width), F32) for _ in range(2)]
        for j in range(2):
            rows = slice(g * span + j * span // 2, g * span + (j + 1) * span // 2)
            reset, update = gates[layer, 0, rows, :], gates[layer, 1, rows, :]
            candidate, third = gates[layer, 2, rows, :], gates[layer, 3, rows, :]
            old = states[rows, :].astype(F32) if layer == 0 else state[layer - 1, rows, :]
            grad = state_grad[rows, :]
            d_candidate = grad * (1.0 - update) * (1.0 - candidate * candidate)
            d_update = grad * (old - candidate) * update * (1.0 - update)
            d_reset = d_candidate * third * reset * (1.0 - reset)
            d_in = jnp.concatenate([d_reset, d_update, d_candidate], axis=1)
            d_hid = jnp.concatenate([d_reset, d_update, d_candidate * reset], axis=1)
            bias_parts[0] = bias_parts[0] + jnp.sum(d_in, axis=0, keepdims=True)
            bias_parts[1] = bias_parts[1] + jnp.sum(d_hid, axis=0, keepdims=True)
            d_in_low, d_hid_low = d_in.astype(BF16), d_hid.astype(BF16)
            gate_grad[layer, 0, rows, :] = d_in_low
            gate_grad[layer, 1, rows, :] = d_hid_low
            pulled[layer, rows, :] = nt(d_in_low, gated_low[0]).astype(BF16)
            if layer > 0:
                state_grad[rows, :] = grad * update + nt(d_hid_low, gated_low[1])
        for s in range(2):
            for i in range(3):
                at = 1 + 3 * s + i
                grad_bias[at : at + 1, :] += bias_parts[s][:, i * width : (i + 1) * width]

    def gated_weights_back(layer):
        low = states[...] if layer == 0 else state[layer - 1].astype(BF16)
        d_first = tn(gathered[layer], gate_grad[layer, 0])
        d_second = tn(low, gate_grad[layer, 1])
        if layer == LAYERS - 1:
            grad_gated[0], grad_gated[1] = d_first, d_second
        else:
            grad_gated[0] += d_first
            grad_gated[1] += d_second

    pick_t = one_hot(iota((half, width), 1) == me * local + iota((half, width), 0) // GROUP)
    pick_n = one_hot(iota((width, half), 0) == me * local + iota((width, half), 1) // GROUP)

    def message_back(layer, g):
        rows = slice(g * span, (g + 1) * span)
        wide_grad = jnp.where(same_mol_t, nt(pick_t, pulled[layer, rows, :]), 0.0).astype(BF16)

        def atoms_pair(ap, carry):
            columns = pl.ds(pl.multiple_of(ap * 2 * width, 2 * width), 2 * width)
            x = nn(wide_grad, sent[rows, columns])
            where = pl.ds(pl.multiple_of(layer * rows_all + g * span + ap * 16, 16), 16)
            for r in range(local):
                at = r * GROUP
                tile = jnp.concatenate([x[at : at + GROUP, :width], x[at : at + GROUP, width:]], axis=0)
                gt[where, r * width : (r + 1) * width] = tile.astype(BF16)
            return carry

        lax.fori_loop(0, atoms // 2, atoms_pair, 0, unroll=16)

    last = LAYERS - 1
    for layer in range(last, 0, -1):
        reducing, gathering = {}, {}
        for g in range(groups):
            gated_back(layer, g)
            message_back(layer, g)
            at = layer * rows_all + g * span
            back = nn(gt[at : at + span, :], edge_low[...]).astype(BF16)
            reduce_send[g * span : (g + 1) * span, :] = nn(order_back, back).astype(BF16)
            reducing[g] = []
            for k in range(1, ring):
                rows = rows16(g * span + lax.rem(me + k, ring) * block, block)
                stage = (LAYERS + 1) * groups + g
                reducing[g].append(row_copy(stage, k, reduce_send.at[rows, :], reduce_recv.at[g, k - 1]))
        gated_weights_back(layer)
        for g in range(groups):
            for copy in reducing[g]:
                copy.wait_recv()
            total = reduce_send[rows16(g * span + me * block, block), :].astype(F32)
            for k in range(ring - 1):
                total = total + reduce_recv[g, k].astype(F32)
            parcels[LAYERS * groups + g, me] = total.astype(BF16)
            gathering[g] = exchange(LAYERS * groups + g)
    rest_copies = []
    for g in range(groups):
        for copy in gathering[g]:
            copy.wait_recv()
        for j in range(ring):
            rows = slice(g * span + j * block, g * span + (j + 1) * block)
            state_grad[rows, :] += parcels[LAYERS * groups + g, j].astype(F32)
        gated_back(0, g)
        if g == groups - 1:
            gated_weights_back(0)
            for s in range(2):
                for i in range(3):
                    at = (s * 3 + i) * width
                    rest_full[at : at + width, :] = grad_gated[s, :, i * width : (i + 1) * width].astype(BF16)
            rest_full[plan.bias_at : plan.bias_at + 16, :] = grad_bias[...].astype(BF16)
            used = plan.bias_at + 16
            if ring * plan.rest_own > used:
                rest_full[used:, :] = jnp.zeros((ring * plan.rest_own - used, WIDE), BF16)
            rest_part[0 : plan.rest_own, :] = rest_full[rows16(me * plan.rest_own, plan.rest_own), :]
            if plan.rest > plan.rest_own:
                rest_part[plan.rest_own :, :] = jnp.zeros((plan.rest - plan.rest_own, WIDE), BF16)
            for k in range(1, peers):
                peer = lax.rem(place + k, peers)
                rows = rows16(peer * plan.rest_part, plan.rest_part)
                rest_copies.append(far_copy(4, k - 1, peer, rest_part.at[rows, :], rest_recv.at[k - 1]))
        message_back(0, g)

    for copy in head_copies:
        copy.wait_recv()
    mine = rows16(me * plan.head + place * plan.head_part, plan.head_part)
    total = head_part[mine, :].astype(F32)
    for k in range(peers - 1):
        total = total + head_recv[k].astype(F32)
    head_all[mine, :] = total.astype(BF16)
    head_copies[:] = [
        far_copy(2, k - 1, lax.rem(place + k, peers), head_all.at[mine, :], head_all.at[mine, :])
        for k in range(1, peers)
    ]

    lines = peers // 2
    line, side = lax.div(place, 2), lax.rem(place, 2)
    neighbour = line * 2 + 1 - side
    part = plan.edge_part
    stack = max(1, 2 * width // (2 * part))
    blocks = lines // stack
    home, seat = lax.div(line, stack), lax.rem(line, stack)

    def out_weights(start):
        columns = pl.ds(pl.multiple_of(start, 2 * width), 2 * width)
        edge_part[columns, :] = nn(turned_lows[...], gt[:, columns]).T.astype(BF16)

    def lines_of(j):
        return [lax.rem(home + j, blocks) * stack + lax.rem(seat + i, stack) for i in range(stack)]

    def scatter_near(j):
        copies = []
        if stack > 1:
            out_weights(lax.rem(home + j, blocks) * stack * 2 * part)
        for i, other in enumerate(lines_of(j)):
            if stack == 1:
                for step in range(part // (2 * width)):
                    out_weights(other * 2 * part + (1 - side) * part + step * 2 * width)
            rows = rows16(other * 2 * part + (1 - side) * part, part)
            copies.append(far_copy(7, j * stack + i, neighbour, edge_part.at[rows, :], near_recv.at[rows16(other * part, part), :]))
            if stack == 1:
                for step in range(part // (2 * width)):
                    out_weights(other * 2 * part + side * part + step * 2 * width)
        return copies

    edge_copies = []

    def scatter_far(j, copies):
        for i, other in enumerate(lines_of(j)):
            copies[i].wait_recv()
            rows = rows16(other * part, part)
            total = edge_part[rows16(other * 2 * part + side * part, part), :].astype(F32) + near_recv[rows, :].astype(F32)
            near_sum[rows, :] = total.astype(BF16)
            if j > 0 or i > 0:
                k = j if stack == 1 else lax.rem(other - line + lines, lines)
                edge_copies.append(far_copy(3, k - 1, other * 2 + side, near_sum.at[rows, :], edge_recv.at[k - 1]))

    order_of = [*range(1, blocks), 0]
    near_copies = [(j, scatter_near(j)) for j in order_of]

    def pair_grads(g):
        wide_grad = jnp.concatenate(
            [
                jnp.where(same_mol, nn(pulled[layer, g * span : (g + 1) * span, :], pick_n), 0.0).astype(BF16)
                for layer in range(LAYERS)
            ],
            axis=1,
        )

        def pair_back(ap, carry):
            columns = pl.ds(pl.multiple_of(ap * 2 * width, 2 * width), 2 * width)
            x = nn(wide_grad, turned[g * LAYERS * half : (g + 1) * LAYERS * half, columns]).astype(BF16)
            for s in range(2):
                where = pl.ds(pl.multiple_of((ap * 2 + s) * atoms, atoms), atoms)
                for m in range(GROUP):
                    pair_grad[g * GROUP + m, where, :] = x[m * atoms : (m + 1) * atoms, s * width : (s + 1) * width]
            return carry

        lax.fori_loop(0, atoms // 2, pair_back, 0, unroll=8)

    for g in range(groups - 1):
        pair_grads(g)
    for waiting in near_copies:
        scatter_far(*waiting)
    for copy in rest_copies:
        copy.wait_recv()
    mine = rows16(place * plan.rest_part, plan.rest_part)
    total = rest_part[mine, :].astype(F32)
    for k in range(peers - 1):
        total = total + rest_recv[k].astype(F32)
    rest_all[me, mine, :] = total.astype(BF16)
    rest_copies = [
        far_copy(6, k - 1, lax.rem(place + k, peers), rest_all.at[me, mine, :], rest_all.at[me, mine, :])
        for k in range(1, peers)
    ]
    for copy in head_copies:
        copy.wait_recv()
    rows = rows16(me * plan.head, plan.head)
    head_rows = [row_copy((LAYERS + 2) * groups, k, head_all.at[rows, :], head_all.at[rows, :]) for k in range(1, ring)]
    pair_grads(groups - 1)

    for copy in edge_copies:
        copy.wait_recv()
    pieces = plan.pieces
    size = part // pieces
    stores = []

    def store(source_ref, target_ref):
        copy = pltpu.make_async_copy(source_ref, target_ref, store_sem.at[len(stores)])
        copy.start()
        stores.append(copy)

    across, beside = {}, {}
    for p in range(pieces):
        own = rows16(line * part + p * size, size)
        mine = rows16(place * part + p * size, size)
        total = near_sum[own, :].astype(F32)
        for k in range(lines - 1):
            total = total + edge_recv[k, p * size : (p + 1) * size, :].astype(F32)
        edge_all[mine, :] = total.astype(BF16)
        for k in range(1, lines):
            peer = lax.rem(line + k, lines) * 2 + side
            across[p, k] = far_copy(5, p * peers + k, peer, edge_all.at[mine, :], edge_all.at[mine, :])
        beside[p, 0] = far_copy(5, p * peers, neighbour, edge_all.at[mine, :], edge_all.at[mine, :])

    def onward(p):
        for k in range(1, lines):
            across[p, k].wait_recv()
            rows = rows16((lax.rem(line - k + lines, lines) * 2 + side) * part + p * size, size)
            beside[p, k] = far_copy(5, p * peers + lines + k, neighbour, edge_all.at[rows, :], edge_all.at[rows, :])
            store(edge_all.at[rows, :], edge_sum.at[rows, :])

    lane_pair = iota((edges // 2, atoms * atoms), 1).astype(F32)
    total_bias = jnp.zeros((8, width), F32)
    for m in range(mols):
        if m == mols // 2:
            for copy in rest_copies:
                copy.wait_recv()
            rest_rows = [row_copy((LAYERS + 2) * groups + 1, k, rest_all.at[me], rest_all.at[me]) for k in range(1, ring)]
        for i in range(2):
            rows = slice(i * edges // 2, (i + 1) * edges // 2)
            d_first = nn(one_hot(lane_pair == pair_cols[rows, m : m + 1]), pair_grad[m]) * slope[m, rows, :]
            total_bias = total_bias + jnp.sum(d_first.reshape(edges // 16, 8, width), axis=0)
            first_grad[m * edges + i * edges // 2 : m * edges + (i + 1) * edges // 2, :] = d_first.astype(BF16)
    total_in = nn(jnp.concatenate([feats[m] for m in range(mols)], axis=1), first_grad[...])
    total_bias = jnp.sum(total_bias, axis=0, keepdims=True)
    first_row[me, 0:features, :] = total_in
    first_row[me, features : features + 8, :] = jnp.broadcast_to(total_bias, (8, width))
    first_copies = [row_copy((LAYERS + 2) * groups + 2, k, first_row.at[me], first_row.at[me]) for k in range(1, ring)]
    onward(0)
    for copy in first_copies:
        copy.wait_recv()
    total = first_row[0]
    for q in range(1, ring):
        total = total + first_row[q]
    first_mol[place] = total
    first_copies = [
        far_copy(8, k - 1, lax.rem(place + k, peers), first_mol.at[place], first_mol.at[place])
        for k in range(1, peers)
    ]
    for p in range(1, pieces):
        onward(p)

    for copy in head_rows:
        copy.wait_recv()
    store(head_all, head_sum)
    for copy in rest_rows:
        copy.wait_recv()
    store(rest_all, rest_sum)
    for copy in total_copies + first_copies:
        copy.wait_recv()
    total, total_first = totals_all[0], first_mol[0]
    for k in range(1, peers):
        total = total + totals_all[k]
        total_first = total_first + first_mol[k]
    totals[0:8, :] = total
    totals[8:, :] = total_first
    for p in range(pieces):
        rows = rows16(place * part + p * size, size)
        store(edge_all.at[rows, :], edge_sum.at[rows, :])
        for k in range(lines):
            beside[p, k].wait_recv()
            rows = rows16((lax.rem(line - k + lines, lines) * 2 + 1 - side) * part + p * size, size)
            store(edge_all.at[rows, :], edge_sum.at[rows, :])
    for copy in started:
        copy.wait_send()
    for copy in stores:
        copy.wait()


def adamw(weight, first, second, grad, rate):
    first_new = BETA_ONE * first + (1.0 - BETA_ONE) * grad
    second_new = BETA_TWO * second + (1.0 - BETA_TWO) * grad * grad
    scaled = jnp.sqrt(second_new * (1.0 / (1.0 - BETA_TWO**STEP))) + EPSILON
    weight_new = (1.0 - rate * DECAY) * weight - (rate / (1.0 - BETA_ONE**STEP)) * first_new / scaled
    return (weight_new, first_new, second_new, weight_new.astype(BF16))


PIECES = 2


def update_kernel(ring, peers, local, counted, totals, edge_far, head_far, rest_far, *refs):
    fars, refs = refs[:21], refs[21:]
    (loss_out, count_out), refs = refs[:2], refs[2:]
    outs, refs = refs[:28], refs[28:]
    (edge_sum, head_sum, rest_sum), refs = refs[:3], refs[3:]
    olds, refs = refs[:21], refs[21:]
    news, (fetch_sem, store_sem) = refs[:28], refs[28:]
    features, width = olds[0].shape
    n_bias = olds[18].shape[0]
    plan = Plan(ring, peers, width, local)
    every = slice(None)
    depth = width // PIECES
    cuts = [(pl.ds(i * depth, depth), every) for i in range(PIECES)]
    count = [0, 0]

    def copies_of(sides, sem, which):
        made = []
        for source_ref, target_ref in sides:
            made.append(pltpu.make_async_copy(source_ref, target_ref, sem.at[count[which]]))
            made[-1].start()
            count[which] += 1
        return made

    def fetch(index, cut=None):
        where = range(3 * index, 3 * index + 3)
        return copies_of([(fars[i], olds[i]) if cut is None else (fars[i].at[cut], olds[i].at[cut]) for i in where], fetch_sem, 0)

    def store(index, cut=None):
        where = range(4 * index, 4 * index + 4)
        return copies_of([(news[i], outs[i]) if cut is None else (news[i].at[cut], outs[i].at[cut]) for i in where], store_sem, 1)

    edge_ready = copies_of([(edge_far, edge_sum)], fetch_sem, 0)
    cut_ready = [fetch(1, cut) for cut in cuts]
    head_ready = copies_of([(head_far, head_sum)], fetch_sem, 0)
    ready = {index: fetch(index) for index in (3, 4, 5)}
    rest_ready = copies_of([(rest_far, rest_sum)], fetch_sem, 0)
    ready.update({index: fetch(index) for index in (2, 0, 6)})
    loss_out[0] = counted[0, 0]
    count_out[0] = counted[0, 1]
    inverse = (1.0 / totals[0:1, :])[0:1, 1:2]

    def update(index, view, grad):
        parts = [ref[view] for ref in olds[3 * index : 3 * index + 3]]
        for ref, value in zip(news[4 * index : 4 * index + 4], adamw(*parts, grad, RATES[index])):
            ref[view] = value

    def wait(copies):
        for copy in copies:
            copy.wait()

    stored = []
    wait(edge_ready)
    for p in range(PIECES):
        wait(cut_ready[p])
        for i in range(local):
            at = i * width + p * depth
            grad = edge_sum[at : at + depth, :].astype(F32) * inverse
            update(1, (slice(p * depth, (p + 1) * depth), slice(i * width, (i + 1) * width)), grad)
        stored += store(1, cuts[p])
    wait(head_ready + ready[3])
    for i in range(4):
        grad = head_sum[i * 3 * width : (i + 1) * 3 * width, :].astype(F32) * inverse
        update(3, (every, slice(i * width, (i + 1) * width)), grad)
    stored += store(3)
    wait(rest_ready + ready[2])
    for s in range(2):
        for i in range(3):
            at, end = (s * 3 + i) * width, (s * 3 + i + 1) * width
            while at < end:
                q, low = divmod(at, plan.rest_own)
                rows = min(end - at, plan.rest_own - low)
                first = at - (s * 3 + i) * width
                grad = rest_sum[q, low : low + rows, :].astype(F32) * inverse
                update(2, (s, slice(first, first + rows), slice(i * width, (i + 1) * width)), grad)
                at += rows
    stored += store(2)
    wait(ready[4])
    update(4, (every, every), head_sum[12 * width : 14 * width, :].astype(F32) * inverse)
    stored += store(4)
    wait(ready[5])
    n_targets = olds[15].shape[0]
    update(5, (every, every), (head_sum[plan.final_at : plan.final_at + 16, :].astype(F32) * inverse)[0:n_targets])
    stored += store(5)
    own = totals[8:, :] * inverse
    wait(ready[0])
    update(0, (every, every), own[0:features])
    stored += store(0)
    q, low = divmod(plan.bias_at, plan.rest_own)
    biases = rest_sum[q, low : low + 16, :].astype(F32) * inverse
    wait(ready[6])
    for i in range(-(-n_bias // WIDE)):
        size = min(WIDE, n_bias - i * WIDE)
        grad = (own[features : features + 1] if i == 0 else biases[i : i + 1])[:, 0:size]
        update(6, pl.ds(i * WIDE, size), grad.reshape(size))
    stored += store(6)
    wait(stored)


def shards(
    edge_feats,
    edge_source,
    edge_target,
    atom_counts,
    edge_counts,
    atom_states,
    targets,
    label_mask,
    edge_input,
    edge_input_first,
    edge_input_second,
    edge_output,
    edge_output_first,
    edge_output_second,
    gated_weights,
    gated_first,
    gated_second,
    memory_weights,
    memory_first,
    memory_second,
    readout_hidden,
    readout_hidden_first,
    readout_hidden_second,
    readout_final,
    readout_final_first,
    readout_final_second,
    bias_vector,
    bias_first,
    bias_second,
):
    mols, edges, features = edge_feats.shape
    atoms, width = atom_states.shape[1:]
    ring = lax.axis_size("row")
    local = width // ring
    rows_all = mols * atoms
    block = GROUP * atoms // ring
    groups = mols // GROUP
    peers = lax.axis_size("mol")
    plan = Plan(ring, peers, width, local)

    finals = [value.T for value in (readout_final, readout_final_first, readout_final_second)]
    vmem = pl.BlockSpec(memory_space=pltpu.VMEM)
    smem = pl.BlockSpec(memory_space=pltpu.SMEM)
    far = pl.BlockSpec(memory_space=pl.ANY)
    shape = jax.ShapeDtypeStruct
    edge_sum, head_sum, rest_sum, totals = pl.pallas_call(
        functools.partial(step_kernel, ring, peers),
        out_shape=[
            shape((plan.edge, WIDE), BF16),
            shape((ring * plan.head, WIDE), BF16),
            shape((ring, plan.rest, WIDE), BF16),
            shape((8 + features + 8, WIDE), F32),
        ],
        in_specs=[smem, smem] + [vmem] * 9 + [far] * 4,
        out_specs=[far] * 3 + [vmem],
        scratch_shapes=[
            pltpu.VMEM((local * width, width), BF16),
            pltpu.VMEM((mols, edges), jnp.int32),
            pltpu.VMEM((edges, mols), F32),
            pltpu.VMEM((rows_all, atoms * width), BF16),
            pltpu.VMEM((mols // GROUP * LAYERS * GROUP * local, atoms * width), BF16),
            pltpu.VMEM((mols, edges, width), F32),
            pltpu.VMEM((mols, atoms * atoms, width), BF16),
            pltpu.VMEM((width, LAYERS * rows_all), BF16),
            pltpu.VMEM((LAYERS, rows_all, width), BF16),
            pltpu.VMEM((LAYERS, 4, rows_all, width), F32),
            pltpu.VMEM((LAYERS, rows_all, width), F32),
            pltpu.VMEM((rows_all, width), F32),
            pltpu.VMEM((LAYERS, 2, rows_all, 3 * width), BF16),
            pltpu.VMEM((LAYERS, rows_all, width), BF16),
            pltpu.VMEM((3 * width, 4 * width), BF16),
            pltpu.VMEM((width + 2 * mols, WIDE), F32),
            pltpu.VMEM(((LAYERS + 1) * groups, ring, block, WIDE), BF16),
            pltpu.VMEM((rows_all, width), BF16),
            pltpu.VMEM((groups, ring - 1, block, width), BF16),
            pltpu.VMEM((2, width, 3 * width), F32),
            pltpu.VMEM((16, WIDE), F32),
            pltpu.VMEM((peers, 8, WIDE), F32),
            pltpu.VMEM((plan.edge, WIDE), BF16),
            pltpu.VMEM((peers // 2 - 1, plan.edge_part, WIDE), BF16),
            pltpu.VMEM((plan.edge, WIDE), BF16),
            pltpu.VMEM((ring * plan.head, WIDE), BF16),
            pltpu.VMEM((peers - 1, plan.head_part, WIDE), BF16),
            pltpu.VMEM((ring * plan.head, WIDE), BF16),
            pltpu.VMEM((ring * plan.rest_own, WIDE), BF16),
            pltpu.VMEM((plan.rest, WIDE), BF16),
            pltpu.VMEM((peers - 1, plan.rest_part, WIDE), BF16),
            pltpu.VMEM((ring, plan.rest, WIDE), BF16),
            pltpu.SemaphoreType.DMA(((LAYERS + 2) * groups + 3, ring - 1)),
            pltpu.SemaphoreType.DMA(((LAYERS + 2) * groups + 3, ring - 1)),
            pltpu.SemaphoreType.DMA((plan.stages[9],)),
            pltpu.SemaphoreType.DMA((plan.stages[9],)),
            pltpu.VMEM((LAYERS * rows_all, local * width), BF16),
            pltpu.VMEM(edge_output.shape, F32),
            pltpu.VMEM(gated_weights.shape, F32),
            pltpu.VMEM(memory_weights.shape, F32),
            pltpu.VMEM(readout_hidden.shape, F32),
            pltpu.SemaphoreType.DMA((4,)),
            pltpu.SemaphoreType.DMA((2 + plan.pieces * peers,)),
            pltpu.VMEM((peers // 2 * plan.edge_part, WIDE), BF16),
            pltpu.VMEM((peers // 2 * plan.edge_part, WIDE), BF16),
            pltpu.VMEM((ring, features + 8, WIDE), F32),
            pltpu.VMEM((peers, features + 8, WIDE), F32),
            pltpu.VMEM((mols * edges, width), BF16),
        ],
        compiler_params=pltpu.CompilerParams(
            collective_id=0, has_side_effects=True, vmem_limit_bytes=60 * 1024 * 1024
        ),
    )(
        atom_counts,
        edge_counts,
        jnp.swapaxes(edge_feats, 1, 2),
        edge_source,
        edge_target,
        atom_states.reshape(rows_all, width),
        targets,
        label_mask,
        edge_input,
        finals[0],
        bias_vector,
        edge_output,
        gated_weights,
        memory_weights,
        readout_hidden,
    )
    olds = [edge_input, edge_input_first, edge_input_second, edge_output, edge_output_first, edge_output_second]
    olds += [gated_weights, gated_first, gated_second, memory_weights, memory_first, memory_second]
    olds += [readout_hidden, readout_hidden_first, readout_hidden_second] + finals
    olds += [bias_vector, bias_first, bias_second]
    news = [shape(olds[3 * index].shape, kind) for index in range(7) for kind in (F32, F32, F32, BF16)]
    sums = [edge_sum, head_sum, rest_sum]
    outs = pl.pallas_call(
        functools.partial(update_kernel, ring, peers, local),
        out_shape=[shape((1,), F32)] * 2 + news,
        in_specs=[smem, vmem] + [far] * 24,
        out_specs=[smem] * 2 + [far] * 28,
        scratch_shapes=[pltpu.VMEM(value.shape, value.dtype) for value in sums + olds + news]
        + [pltpu.SemaphoreType.DMA((3 + 18 + 3 * PIECES,)), pltpu.SemaphoreType.DMA((24 + 4 * PIECES,))],
        compiler_params=pltpu.CompilerParams(vmem_limit_bytes=60 * 1024 * 1024),
    )(totals, totals, *sums, *olds)
    outs = list(outs)
    outs[0], outs[1] = outs[0].reshape(()), outs[1].reshape(())
    outs[22:26] = [value.T for value in outs[22:26]]
    return tuple(outs)


def solution(mesh):
    cut = P(None, "row")
    per_mol = (P("mol", None, None), P("mol", None), P("mol", None), P("mol"), P("mol"), P("mol", None, None))
    per_mol += (P("mol", None), P("mol", None))
    return jax.shard_map(
        shards,
        mesh=mesh,
        in_specs=per_mol + (P(),) * 3 + (cut,) * 3 + (P(),) * 15,
        out_specs=(P(),) * 6 + (cut,) * 4 + (P(),) * 20,
        check_vma=False,
    )
```
